32 devices in a mesh: dp: 8 (over z, x), rep: 4 (over y, core).
Axes of the slice: x: 2, y: 2, z: 4, core: 2. Of those that a mesh axis runs over, the one named last changes fastest.
Arguments:
- features: bfloat16 [3, 20480, 2048], P(None, ('dp', 'rep')), may hold values from -6 to 6
- cotangent: bfloat16 [3, 20480, 2048], P(None, ('dp', 'rep')), may hold values from -6 to 6
- neighbours: int32 [3, 20480, 32], P(None, ('dp', 'rep')), may hold values from 0 to 127
- segments: int32 [3, 20480], P(None, ('dp', 'rep')), may hold values from 0 to 639, never falling along the last dimension, each value on 1 to 64 neighbouring positions
- live: int32 [3, 20480], P(None, ('dp', 'rep')), may hold values 0 or 1
- weight: bfloat16 [2048, 2048], P(('dp', 'rep')), may hold values from -0.125 to 0.125
- bias: bfloat16 [2048], P(('dp', 'rep')), may hold values from -3 to 3
Outputs:
- activations: bfloat16 [3, 20480, 2048], P(None, ('dp', 'rep'))
- feature_grad: bfloat16 [3, 20480, 2048], P(None, ('dp', 'rep'))
- weight_grad: float32 [2048, 2048], P(('dp', 'rep'))
- bias_grad: float32 [2048], P(('dp', 'rep'))
The draws below stay inside these ranges and needn't reach their ends.
Inputs may be any that keep to these rules, and one draw needn't show every extreme that they name: `neighbours`: positions within the node's own slot of 128 nodes. `segments`: never falling along the nodes of a micro-batch; each cluster has 1 to 64 nodes, one exactly 64.
All inputs are finite; a program needn't handle non-finite values. No bound on the sum of `live` on one device may be relied on, other than what follows from the above.
Results may differ from the reference program's by a relative error of at most 0.0055.
Values may be sent and summed in bfloat16 or wider, within the bound.
A program may use at most 192 MiB of HBM per device.

```python
import math
import jax
import jax.numpy as jnp
import numpy as np
from jax import lax

D = 2048
SLOT = 128
NBRS = 32
MB = 3
NODES = 20480


def place_ends(drawn, rng, low, largest):
    shape = drawn.shape
    place = [jax.random.randint(jax.random.fold_in(rng, axis), (), 0, shape[axis]) for axis in range(len(shape))]
    drawn = drawn.at[tuple(place)].set(low)
    longest = shape.index(max(shape))
    place[longest] = (place[longest] + 1) % shape[longest]
    return drawn.at[tuple(place)].set(largest)


def spiked(entries, rng, source, target, parts, factor):
    owner, partner = [(jnp.arange(entries.shape[dim]) // (entries.shape[dim] // parts)).reshape([-1 if axis == dim else 1 for axis in range(entries.ndim)]) for dim in (source, target)]
    chosen = jax.random.permutation(rng, parts)[partner]
    strong = (owner == chosen) | (owner == (partner + parts // 2) % parts)
    return jnp.where(strong, factor * entries, entries)


def shard_levels(own_key, shape, split, smallest, largest):
    gain, own = 1.0, jax.random.fold_in(own_key, 6)
    for position, blocks in split:
        steps = jnp.exp(jax.random.uniform(jax.random.fold_in(own, position), (blocks,), jnp.float32, smallest / len(split), largest / len(split)))
        gain = gain * jnp.repeat(steps, shape[position] // blocks).reshape([-1 if axis == position else 1 for axis in range(len(shape))])
    return gain


def length_profile(count, total, bound, slope):
    weights = [(1 << 20) // math.isqrt(standing ** slope) + 1 for standing in range(2, count + 1)]
    rest, counts = total - bound - (count - 1), [1] * (count - 1)
    while rest > 0:
        free = [i for i in range(count - 1) if counts[i] < bound]
        whole, left = sum([weights[i] for i in free]), rest
        for i in free:
            extra = min(bound - counts[i], max(1, left * weights[i] // whole), rest)
            counts[i] = counts[i] + extra
            rest = rest - extra
    return np.array([bound] + counts)


def ragged_sizes(key, number_of, total, most, skew):
    if number_of == 2:
        one = jax.random.randint(key, (), max(1, total - most), min(most, total - 1) + 1)
        return jnp.stack([one, total - one])
    tallies = jnp.asarray(length_profile(number_of, total, most, skew), jnp.int32)
    pairs = (number_of - 1) // 2
    donor, taker = tallies[1:1 + 2 * pairs:2], tallies[2:2 + 2 * pairs:2]
    slack = jnp.minimum(donor - 1, most - taker)
    moved = jax.random.randint(jax.random.fold_in(key, 1), (pairs,), 0, 1 << 20) % (slack + 1)
    tallies = tallies.at[1:1 + 2 * pairs:2].set(donor - moved).at[2:2 + 2 * pairs:2].set(taker + moved)
    return tallies[jax.random.permutation(jax.random.fold_in(key, 2), number_of)]


def gaussian(stream_key, extent, scale, limit, split=(), kind=jnp.bfloat16):
    factor_of = shard_levels(stream_key, extent, split, -0.22, 0.18) if split else 1.0
    drawn = jax.random.normal(stream_key, extent, jnp.float32) * scale * factor_of
    return jnp.minimum(jnp.maximum(drawn, -limit), limit).astype(kind)


def bell_draw_with(stream_key, extent, deviation, bound, pieces, heavy, kind=jnp.bfloat16):
    drawn = deviation * jax.random.normal(stream_key, extent, jnp.float32)
    if pieces:
        drawn = drawn * shard_levels(stream_key, extent, pieces, -0.22, 0.18)
    return jnp.clip(spiked(drawn, jax.random.fold_in(stream_key, 3), *heavy), -bound, bound).astype(kind)


def setup_inputs(seed: int = 0) -> dict:
    splits = jax.random.split(jax.random.key(seed), 8)
    return {
        "features": bell_draw_with(splits[0], (MB, NODES, D), 1.0, 6.0, ((1, 32),), (1, 2, 32, 2.75)),
        "cotangent": gaussian(splits[1], (MB, NODES, D), 1.0, 6.0, ((1, 32),)),
        "neighbours": place_ends(jax.random.randint(splits[2], (MB, NODES, NBRS), 0, SLOT), jax.random.fold_in(splits[2], 1), 0, SLOT - 1).astype(jnp.int32),
        "segments": jax.vmap(lambda own: jnp.searchsorted(jnp.cumsum(ragged_sizes(own, NODES // 32, NODES, 64, 2)), jnp.arange(NODES), side="right"))(jax.random.split(splits[3], MB)).reshape((MB, NODES)).astype(jnp.int32),
        "live": place_ends((jax.random.randint(splits[4], (MB, NODES), 0, 8) < 7).astype(jnp.int32), jax.random.fold_in(splits[4], 1), 0, 1),
        "weight": gaussian(splits[5], (D, D), D ** -0.5, 0.125, ((0, 32),)),
        "bias": gaussian(splits[6], (D,), 0.5, 3.0, ((0, 32),)),
    }


@jax.custom_vjp
def low(v):
    return lax.optimization_barrier(v.astype(jnp.bfloat16)).astype(jnp.float32)

@jax.custom_vjp
def low_back(v):
    return v

def low_keep(v):
    return (low(v), None)

def low_pass(kept, grad):
    return (grad,)

def back_keep(v):
    return (v, None)

def back_low(kept, grad):
    return (low(grad),)
low.defvjp(low_keep, low_pass)
low_back.defvjp(back_keep, back_low)
enhance = 1.0

def normalized(neighbours, segments, live):
    slots = NODES // SLOT
    lists = neighbours.reshape(MB, slots, SLOT, NBRS)
    seg_ids = segments.reshape(MB, slots, SLOT)
    alive = live.reshape(MB, slots, SLOT).astype(jnp.float32)
    columns = jnp.arange(SLOT, dtype=jnp.int32)
    counted = jnp.zeros((MB, slots, SLOT, SLOT), jnp.float32)
    for entry in range(NBRS):
        counted = counted + (lists[..., entry][..., None] == columns).astype(jnp.float32)
    same = (seg_ids[..., :, None] == seg_ids[..., None, :]).astype(jnp.float32)
    adjacency = counted * same * alive[..., :, None] * alive[..., None, :]
    degree = lax.optimization_barrier(jnp.sum(adjacency, axis=-1))
    identity = jnp.eye(SLOT, dtype=jnp.float32)
    diagonal = lax.optimization_barrier(jnp.sum(adjacency * identity, axis=-1))
    scaled = adjacency * (1.0 - identity) + identity * ((1.0 + enhance) * (diagonal + 1.0))[..., None]
    return alive[..., None] * scaled / (degree + 1.0)[..., None]

def reference(features, cotangent, neighbours, segments, live, weight, bias):
    normed = normalized(neighbours, segments, live)
    slots = NODES // SLOT

    def forward(feats, weights, offsets):
        blocks = feats.reshape(MB, slots, SLOT, D)
        pooled = jnp.einsum('msij,msjd->msid', normed, blocks, precision=lax.Precision.HIGHEST)
        pooled = low(pooled.reshape(MB, NODES, D))
        preact = jnp.einsum('mnd,de->mne', pooled, weights, precision=lax.Precision.HIGHEST) + offsets
        preact = low_back(preact)
        return jax.nn.silu(preact)
    outputs, pullback = jax.vjp(forward, features.astype(jnp.float32), weight.astype(jnp.float32), bias.astype(jnp.float32))
    feat_grad, weight_grad, bias_grad = pullback(cotangent.astype(jnp.float32))
    return (outputs.astype(jnp.bfloat16), feat_grad.astype(jnp.bfloat16), weight_grad, bias_grad)
```

```python
import functools

import jax
import jax.numpy as jnp
from jax import lax
from jax.experimental import pallas as pl
from jax.experimental.pallas import tpu as pltpu
from jax.sharding import PartitionSpec as P

SLOT = 128
LANES = 128
CHUNK = 256
RING = 4
MESH = pl.DeviceIdType.MESH
F32, BF16 = jnp.float32, jnp.bfloat16
ENHANCE = 1.0


def split_axes(dp, rep):
    b = 2 ** ((dp.bit_length() - 1) // 2)
    return dp // b, b, rep // 2, 2


def kernel(
    dims, feat, cot, nbr, seg, live, weight, bias, act_out, fgrad_out, wgrad_out, bgrad_out,
    wg, pool, pool_t, gp, ct, act, acc, csend, crecv, s1a, s1b, s2a, s2b, sz, r1a, r1b, r2a, r2b, rz,
    nbuf, sbuf, lbuf, adj_t, scale, fout, wout, bb, brow, bacc, bt, bsum, brc, br1, br2, brz,
    in_sem, ct_sem, act_sem, fout_sem, wout_sem,
    gz_s, gz_r, g1a_s, g1a_r, g1b_s, g1b_r, g2a_s, g2a_r, g2b_s, g2b_r, gc_s, gc_r,
    rc_s, rc_r, p1a_s, p1a_r, p1b_s, p1b_r, p2a_s, p2a_r, p2b_s, p2b_r, pz_s, pz_r,
    bz_s, bz_r, b1_s, b1_r, b2_s, b2_r, bc_s, bc_r, dc_s, dc_r, d1_s, d1_r, d2_s, d2_r, dz_s, dz_r,
):
    A, B, Y, C = dims
    batches, local, D = feat.shape
    rows = weight.shape[0]
    slots = local // SLOT
    N = batches * local
    chunks = D // CHUNK
    groups = A * B * Y
    plane = groups * rows
    wide = D // A
    half = N // 2

    dp, rep = lax.axis_index("dp"), lax.axis_index("rep")
    a, b, y, c = lax.div(dp, B), lax.rem(dp, B), lax.div(rep, C), lax.rem(rep, C)
    oc = 1 - c

    def device(a_, b_, y_, c_):
        return (a_ * B + b_, y_ * C + c_)

    def up(v, d, n):
        return lax.rem(v + d, n)

    def down(v, d, n):
        return lax.rem(v + n - d, n)

    to_a = [(d, device(up(a, d, A), b, y, c)) for d in range(1, A)]
    to_b = [(d, device(a, up(b, d, B), y, c)) for d in range(1, B)]
    to_y = [(d, device(a, b, up(y, d, Y), c)) for d in range(1, Y)]
    to_c = device(a, b, y, oc)

    def remote(src, dst, ssem, rsem, dev):
        return pltpu.make_async_remote_copy(
            src_ref=src, dst_ref=dst, send_sem=ssem, recv_sem=rsem, device_id=dev, device_id_type=MESH
        )

    weight_loads = [
        pltpu.make_async_copy(
            weight.at[:, pl.ds((2 * k + h) * LANES, LANES)], wg.at[k, h, a, b, y, c], in_sem.at[0, k * 2 + h]
        )
        for k in range(chunks)
        for h in range(2)
    ]
    side_loads = [
        pltpu.make_async_copy(nbr, nbuf, in_sem.at[1, 0]),
        pltpu.make_async_copy(seg, sbuf, in_sem.at[1, 1]),
        pltpu.make_async_copy(live, lbuf, in_sem.at[1, 2]),
    ]
    bias_load = pltpu.make_async_copy(bias, bb.at[a, b, y, c], in_sem.at[1, 3])
    feat_loads = [
        pltpu.make_async_copy(feat.at[m], gp.at[pl.ds(m * local, local)], in_sem.at[1, 4 + m]) for m in range(batches)
    ]
    for copy in weight_loads:
        copy.start()
    bias_load.start()
    for copy in side_loads:
        copy.start()
    for copy in feat_loads:
        copy.start()

    barrier = pltpu.get_barrier_semaphore()
    partners = [dev for _, dev in to_a + to_b + to_y] + [to_c]
    for dev in partners:
        pl.semaphore_signal(barrier, inc=1, device_id=dev, device_id_type=MESH)

    def cot_load(k, m):
        return pltpu.make_async_copy(
            cot.at[m, :, pl.ds(pl.multiple_of(k * CHUNK, CHUNK), CHUNK)],
            ct.at[lax.rem(k, 2), pl.ds(m * local, local)],
            ct_sem.at[lax.rem(k, 2), m],
        )

    def act_store(k, m):
        return pltpu.make_async_copy(
            act.at[lax.rem(k, 2), pl.ds(m * local, local)],
            act_out.at[m, :, pl.ds(pl.multiple_of(k * CHUNK, CHUNK), CHUNK)],
            act_sem.at[lax.rem(k, 2), m],
        )

    pl.semaphore_wait(barrier, len(partners))

    def gather_z(k, d, dev, mine):
        at = a if mine else down(a, d, A)
        ref = wg.at[k, :, at, b, y, c]
        return remote(ref, ref, gz_s.at[k, d - 1], gz_r.at[k, d - 1], dev)

    def gather_1(k, mine):
        out = []
        for d, dev in to_b:
            ref = wg.at[k, 0, :, b if mine else down(b, d, B), y, c]
            out.append(remote(ref, ref, g1a_s.at[k, d - 1], g1a_r.at[k, d - 1], dev))
        for d, dev in to_y:
            ref = wg.at[k, 1, :, b, y if mine else down(y, d, Y), c]
            out.append(remote(ref, ref, g1b_s.at[k, d - 1], g1b_r.at[k, d - 1], dev))
        return out

    def gather_2(k, mine):
        out = []
        for d, dev in to_y:
            ref = wg.at[k, 0, :, :, y if mine else down(y, d, Y), c]
            out.append(remote(ref, ref, g2a_s.at[k, d - 1], g2a_r.at[k, d - 1], dev))
        for d, dev in to_b:
            ref = wg.at[k, 1, :, b if mine else down(b, d, B), :, c]
            out.append(remote(ref, ref, g2b_s.at[k, d - 1], g2b_r.at[k, d - 1], dev))
        return out

    def gather_c(k, mine):
        ref = wg.at[k, :, :, :, :, c if mine else oc]
        return remote(ref, ref, gc_s.at[k], gc_r.at[k], to_c)

    def guarded(fn):
        def at(k):
            if isinstance(k, int):
                if 0 <= k < chunks:
                    fn(k)
            else:
                pl.when(jnp.logical_and(k >= 0, k < chunks))(lambda: fn(k))

        return at

    def bias_z(d, dev, mine):
        ref = bb.at[a if mine else down(a, d, A), b, y, c]
        return remote(ref, ref, bz_s.at[d - 1], bz_r.at[d - 1], dev)

    def bias_1(d, dev, mine):
        ref = bb.at[:, b if mine else down(b, d, B), y, c]
        return remote(ref, ref, b1_s.at[d - 1], b1_r.at[d - 1], dev)

    def bias_2(d, dev, mine):
        ref = bb.at[:, :, y if mine else down(y, d, Y), c]
        return remote(ref, ref, b2_s.at[d - 1], b2_r.at[d - 1], dev)

    def bias_c(mine):
        ref = bb.at[:, :, :, c if mine else oc]
        return remote(ref, ref, bc_s.at[0], bc_r.at[0], to_c)

    @guarded
    def ag1(k):
        for d, dev in to_a:
            gather_z(k, d, dev, False).wait_recv()
        for copy in gather_1(k, True):
            copy.start()

    @guarded
    def ag2(k):
        for copy in gather_1(k, False):
            copy.wait_recv()
        for copy in gather_2(k, True):
            copy.start()

    @guarded
    def ag3(k):
        for copy in gather_2(k, False):
            copy.wait_recv()
        gather_c(k, True).start()

    def bias_ag1():
        for d, dev in to_a:
            bias_z(d, dev, False).wait_recv()
        for d, dev in to_b:
            bias_1(d, dev, True).start()

    def bias_ag2():
        for d, dev in to_b:
            bias_1(d, dev, False).wait_recv()
        for d, dev in to_y:
            bias_2(d, dev, True).start()

    def bias_ag3():
        for d, dev in to_y:
            bias_2(d, dev, False).wait_recv()
        bias_c(True).start()

    for copy in weight_loads[:2]:
        copy.wait()
    bias_load.wait()
    for d, dev in to_a:
        gather_z(0, d, dev, True).start()
        bias_z(d, dev, True).start()
    for copy in weight_loads[2:]:
        copy.wait()
    for k in range(1, chunks):
        for d, dev in to_a:
            gather_z(k, d, dev, True).start()

    for copy in side_loads:
        copy.wait()
    for m in range(batches):
        cot_load(0, m).start()
    bacc[...] = jnp.zeros_like(bacc)

    def pooling(m, q):
        s = m * slots + q
        here = pl.multiple_of(q * SLOT, SLOT)
        flat = pl.multiple_of(s * SLOT, SLOT)
        lists = nbuf[m, pl.ds(here, SLOT), :]
        lane = lax.broadcasted_iota(jnp.int32, (SLOT, SLOT), 1)
        sub = lax.broadcasted_iota(jnp.int32, (SLOT, SLOT), 0)
        reps = SLOT // lists.shape[1]
        listed = jnp.concatenate([lists] * reps, axis=1).astype(F32).T.astype(BF16)
        position = sub.astype(F32).astype(BF16)
        counted = jnp.zeros((SLOT, SLOT), BF16)
        for j in range(lists.shape[1]):
            counted = counted + jnp.where(listed[j : j + 1, :] == position, jnp.bfloat16(1), jnp.bfloat16(0))
        counted = counted.astype(F32).T
        ids, alive = sbuf[m : m + 1, pl.ds(here, SLOT)], lbuf[m : m + 1, pl.ds(here, SLOT)]
        along = jnp.where(alive > 0, ids, -1)
        down_ = jnp.broadcast_to(jnp.where(alive > 0, ids, -2), (SLOT, SLOT)).T
        adjacency = jnp.where(down_ == along, counted, 0.0)
        degree = jnp.sum(adjacency, axis=1, keepdims=True)
        factor = jnp.where(down_ >= 0, 1.0 / (degree + 1.0), 0.0)
        adjacency = jnp.where(lane == sub, (1.0 + ENHANCE) * (adjacency + 1.0), adjacency)
        adj_t[s] = adjacency.T.astype(BF16)
        scale[pl.ds(flat, SLOT), :] = factor
        pooled = jnp.dot(adjacency.astype(BF16), gp[pl.ds(flat, SLOT), :], preferred_element_type=F32)
        pooled = (pooled * jnp.concatenate([factor] * (D // SLOT), axis=1)).astype(BF16)
        pool[pl.ds(flat, SLOT), :] = pooled
        pool_t[:, :, :, pl.ds(flat, SLOT)] = pooled.T.reshape(groups, C, rows, SLOT)

    early = {
        4: [lambda: ag1(0), bias_ag1],
        7: [lambda: ag1(1)],
        8: [lambda: ag2(0), bias_ag2],
        10: [lambda: ag1(2)],
        11: [lambda: ag2(1)],
        13: [lambda: ag3(0), bias_ag3, lambda: ag1(3)],
    }
    for m in range(batches):
        feat_loads[m].wait()

        def step(q, carry, m=m):
            pooling(m, q)
            for at, events in early.items():
                if m * slots <= at < (m + 1) * slots:

                    @pl.when(q == at - m * slots)
                    def _(events=events):
                        for event in events:
                            event()

            return carry

        lax.fori_loop(0, slots, step, 0)

    bias_c(False).wait_recv()
    tiles = bb[...].reshape(groups * C, 8, LANES)
    per = LANES // rows
    owner = lax.div(lax.broadcasted_iota(jnp.int32, (1, LANES), 1), rows)
    for j in range(D // LANES):
        row = jnp.zeros((1, LANES), F32)
        for p in range(per):
            row = jnp.where(owner == p, tiles[j * per + p, 0:1, :], row)
        brow[j] = jnp.broadcast_to(row, (8, LANES))

    def reduce_c(k):
        return remote(csend.at[lax.rem(k, 2)], crecv.at[k], rc_s.at[k], rc_r.at[k], to_c)

    def reduce_1(k):
        e = lax.rem(k, 2)
        out_a = [
            remote(s1a.at[e, d - 1], r1a.at[k, d - 1], p1a_s.at[k, d - 1], p1a_r.at[k, d - 1], dev) for d, dev in to_y
        ]
        out_b = [
            remote(s1b.at[e, d - 1], r1b.at[k, d - 1], p1b_s.at[k, d - 1], p1b_r.at[k, d - 1], dev) for d, dev in to_b
        ]
        return out_a + out_b

    def reduce_2(k):
        e = lax.rem(k, 2)
        out_a = [
            remote(s2a.at[e, d - 1], r2a.at[k, d - 1], p2a_s.at[k, d - 1], p2a_r.at[k, d - 1], dev) for d, dev in to_b
        ]
        out_b = [
            remote(s2b.at[e, d - 1], r2b.at[k, d - 1], p2b_s.at[k, d - 1], p2b_r.at[k, d - 1], dev) for d, dev in to_y
        ]
        return out_a + out_b

    def reduce_z(k):
        e = lax.rem(k, 2)
        return [remote(sz.at[e, d - 1], rz.at[k, d - 1], pz_s.at[k, d - 1], pz_r.at[k, d - 1], dev) for d, dev in to_a]

    def ago(k, n, copies):
        def wait():
            for copy in copies(k - n):
                copy.wait_send()

        if isinstance(k, int):
            if k >= n:
                wait()
        else:
            pl.when(k >= n)(wait)

    lo, hi = slice(0, LANES), slice(LANES, CHUNK)

    @guarded
    def rs1(k):
        t, e = lax.rem(k, RING), lax.rem(k, 2)
        reduce_c(k).wait_recv()
        ago(k, 2, reduce_1)
        for d, _ in to_y:
            v = up(y, d, Y)
            s1a[e, d - 1] = (acc[t, :, :, v, :, lo] + crecv[k, :, :, v, :, lo].astype(F32)).astype(BF16)
        for d, _ in to_b:
            v = up(b, d, B)
            s1b[e, d - 1] = (acc[t, :, v, :, :, hi] + crecv[k, :, v, :, :, hi].astype(F32)).astype(BF16)
        for copy in reduce_1(k):
            copy.start()
        acc[t, :, :, y, :, lo] = acc[t, :, :, y, :, lo] + crecv[k, :, :, y, :, lo].astype(F32)
        acc[t, :, b, :, :, hi] = acc[t, :, b, :, :, hi] + crecv[k, :, b, :, :, hi].astype(F32)

    @guarded
    def rs2(k):
        t, e = lax.rem(k, RING), lax.rem(k, 2)
        for copy in reduce_1(k):
            copy.wait_recv()
        ago(k, 2, reduce_2)

        def total_a(v):
            out = acc[t, :, v, y, :, lo]
            for d, _ in to_y:
                out = out + r1a[k, d - 1, :, v].astype(F32)
            return out

        def total_b(v):
            out = acc[t, :, b, v, :, hi]
            for d, _ in to_b:
                out = out + r1b[k, d - 1, :, v].astype(F32)
            return out

        for d, _ in to_b:
            s2a[e, d - 1] = total_a(up(b, d, B)).astype(BF16)
        for d, _ in to_y:
            s2b[e, d - 1] = total_b(up(y, d, Y)).astype(BF16)
        for copy in reduce_2(k):
            copy.start()
        acc[t, :, b, y, :, lo] = total_a(b)
        acc[t, :, b, y, :, hi] = total_b(y)

    @guarded
    def rs3(k):
        t, e = lax.rem(k, RING), lax.rem(k, 2)
        for copy in reduce_2(k):
            copy.wait_recv()
        ago(k, 2, reduce_z)

        def total(v):
            left, right = acc[t, v, b, y, :, lo], acc[t, v, b, y, :, hi]
            for d, _ in to_b:
                left = left + r2a[k, d - 1, v].astype(F32)
            for d, _ in to_y:
                right = right + r2b[k, d - 1, v].astype(F32)
            return jnp.concatenate([left, right], axis=1)

        for d, _ in to_a:
            sz[e, d - 1] = total(up(a, d, A)).astype(BF16)
        for copy in reduce_z(k):
            copy.start()
        acc[t, a, b, y] = total(a)

    def wout_store(k):
        cols = pl.ds(pl.multiple_of(k * CHUNK, CHUNK), CHUNK)
        return pltpu.make_async_copy(wout.at[k], wgrad_out.at[:, cols], wout_sem.at[k])

    @guarded
    def rs4(k):
        t = lax.rem(k, RING)
        for copy in reduce_z(k):
            copy.wait_recv()
        out = acc[t, a, b, y]
        for d, _ in to_a:
            out = out + rz[k, d - 1].astype(F32)
        wout[k] = out
        wout_store(k).start()

    def columns(k):
        return pl.ds(pl.multiple_of(k * CHUNK, CHUNK), CHUNK)

    def forward(k, i):
        e = lax.rem(k, 2)
        part = pl.ds(i * half, half)
        w = jnp.concatenate([wg[k, h].reshape(D, LANES) for h in range(2)], axis=1)
        offset = jnp.concatenate([brow[2 * k + h][0:1] for h in range(2)], axis=1)
        preact = jnp.dot(pool[part, :], w, preferred_element_type=F32) + offset
        squash = jax.nn.sigmoid(preact)
        active = preact * squash
        act[e, part, :] = active.astype(BF16)
        grad = (ct[e, part, :].astype(F32) * (squash + active * (1.0 - squash))).astype(BF16)
        gp[part, columns(k)] = grad
        bacc[:, columns(k)] += jnp.sum(grad.astype(F32).reshape(half // 8, 8, CHUNK), axis=0)

    def weight_term(k, which):
        left = pool_t[:, which].reshape(plane, N)
        return jnp.dot(left, gp[:, columns(k)], preferred_element_type=F32).reshape(A, B, Y, rows, CHUNK)

    def chunk(k, carry):
        e, t = lax.rem(k, 2), lax.rem(k, RING)
        gather_c(k, False).wait_recv()
        for m in range(batches):
            cot_load(k, m).wait()

        @pl.when(k + 1 < chunks)
        def _():
            for m in range(batches):
                cot_load(k + 1, m).start()

        @pl.when(k >= 2)
        def _():
            for m in range(batches):
                act_store(k - 2, m).wait()

        pl.when(k >= 0)(lambda: forward(k, 0))
        ag2(k + 2)
        ag3(k + 1)
        rs1(k - 1)
        rs4(k - 4)
        pl.when(k >= 0)(lambda: forward(k, 1))
        for m in range(batches):
            act_store(k, m).start()
        rs2(k - 2)
        ago(k, 2, lambda j: [reduce_c(j)])

        @pl.when(k >= 0)
        def _():
            csend[e] = weight_term(k, oc).astype(BF16)

        reduce_c(k).start()
        ag1(k + 4)
        rs3(k - 3)

        @pl.when(k >= 0)
        def _():
            acc[t] = weight_term(k, c)

        return carry

    lax.fori_loop(0, chunks, chunk, 0)

    def bred_c():
        return remote(bt.at[:, :, :, oc], brc, dc_s.at[0], dc_r.at[0], to_c)

    def bred_1():
        return [remote(bsum.at[:, :, up(y, d, Y)], br1.at[d - 1], d1_s.at[d - 1], d1_r.at[d - 1], dev) for d, dev in to_y]

    def bred_2():
        return [remote(bsum.at[:, up(b, d, B), y], br2.at[d - 1], d2_s.at[d - 1], d2_r.at[d - 1], dev) for d, dev in to_b]

    def bred_z():
        return [remote(bsum.at[up(a, d, A), b, y], brz.at[d - 1], dz_s.at[d - 1], dz_r.at[d - 1], dev) for d, dev in to_a]

    for a_ in range(A):
        for b_ in range(B):
            for y_ in range(Y):
                for c_ in range(C):
                    block = (((a_ * B + b_) * Y + y_) * C + c_) * rows // LANES
                    bt[a_, b_, y_, c_] = bacc[:, block * LANES : (block + 1) * LANES]
    bred_c().start()

    def bias_rs1():
        bred_c().wait_recv()
        bsum[...] = bt[:, :, :, c] + brc[...]
        for copy in bred_1():
            copy.start()

    def bias_rs2():
        for copy in bred_1():
            copy.wait_recv()
        for d, _ in to_y:
            bsum[:, :, y] = bsum[:, :, y] + br1[d - 1]
        for copy in bred_2():
            copy.start()

    def bias_rs3():
        for copy in bred_2():
            copy.wait_recv()
        for d, _ in to_b:
            bsum[:, b, y] = bsum[:, b, y] + br2[d - 1]
        for copy in bred_z():
            copy.start()

    def bias_rs4():
        for copy in bred_z():
            copy.wait_recv()
        out = bsum[a, b, y]
        for d, _ in to_a:
            out = out + brz[d - 1]
        out = jnp.sum(out, axis=0, keepdims=True)
        place = lax.rem((dp * (Y * C) + rep) * rows, LANES)
        mine = jnp.zeros((1, rows), F32)
        for p in range(per):
            mine = jnp.where(place == p * rows, out[:, p * rows : (p + 1) * rows], mine)
        bgrad_out[...] = mine

    def fout_store(i):
        return pltpu.make_async_copy(
            fout.at[lax.rem(i, 2)],
            fgrad_out.at[lax.rem(i, batches), :, pl.ds(pl.multiple_of(lax.div(i, batches) * wide, wide), wide)],
            fout_sem.at[lax.rem(i, 2)],
        )

    def feature_grad(i):
        e, n, m = lax.rem(i, 2), lax.div(i, batches), lax.rem(i, batches)
        base = pl.multiple_of(m * local, local)
        w = jnp.concatenate([wg[k, h, n].reshape(wide, LANES) for k in range(chunks) for h in range(2)], axis=1)
        grad = lax.dot_general(gp[pl.ds(base, local), :], w, (((1,), (1,)), ((), ())), preferred_element_type=F32)
        grad = grad * jnp.concatenate([scale[pl.ds(base, local), :]] * (wide // LANES), axis=1)
        high = grad.astype(BF16)
        low = (grad - high.astype(F32)).astype(BF16)
        for q in range(slots):
            left = adj_t[m * slots + q]
            part = slice(q * SLOT, (q + 1) * SLOT)
            right = jnp.concatenate([high[part], low[part]], axis=0)
            out = jnp.dot(jnp.concatenate([left, left], axis=1), right, preferred_element_type=F32)
            fout[e, part, :] = out.astype(BF16)

    late = {
        0: [lambda: rs1(chunks - 1), bias_rs1, lambda: rs2(chunks - 2), lambda: rs3(chunks - 3), lambda: rs4(chunks - 4)],
        2: [lambda: rs2(chunks - 1), bias_rs2, lambda: rs3(chunks - 2), lambda: rs4(chunks - 3)],
        5: [lambda: rs3(chunks - 1), bias_rs3, lambda: rs4(chunks - 2)],
        8: [lambda: rs4(chunks - 1), bias_rs4],
    }
    steps = A * batches

    def last(i, carry):
        @pl.when(i >= 2)
        def _():
            fout_store(i - 2).wait()

        pl.when(i >= 0)(lambda: feature_grad(i))
        fout_store(i).start()
        for at, events in late.items():

            @pl.when(i == at)
            def _(events=events):
                for event in events:
                    event()

        return carry

    lax.fori_loop(0, steps, last, 0)

    for i in (steps - 2, steps - 1):
        fout_store(i).wait()
    for k in (chunks - 2, chunks - 1):
        for m in range(batches):
            act_store(k, m).wait()
        for copy in [reduce_c(k)] + reduce_1(k) + reduce_2(k) + reduce_z(k):
            copy.wait_send()

    def drained(k, carry):
        wout_store(k).wait()
        for d, dev in to_a:
            gather_z(k, d, dev, True).wait_send()
        for copy in gather_1(k, True) + gather_2(k, True) + [gather_c(k, True)]:
            copy.wait_send()
        return carry

    lax.fori_loop(0, chunks, drained, 0)
    for d, dev in to_a:
        bias_z(d, dev, True).wait_send()
    for d, dev in to_b:
        bias_1(d, dev, True).wait_send()
    for d, dev in to_y:
        bias_2(d, dev, True).wait_send()
    bias_c(True).wait_send()
    for copy in [bred_c()] + bred_1() + bred_2() + bred_z():
        copy.wait_send()


def per_device(dims, features, cotangent, neighbours, segments, live, weight, bias):
    A, B, Y, C = dims
    batches, local, D = features.shape
    rows = weight.shape[0]
    N = batches * local
    chunks = D // CHUNK
    groups = A * B * Y
    wide = D // A
    tile = jnp.broadcast_to(jnp.tile(bias.astype(F32), LANES // rows)[None], (8, LANES))
    any_spec = pl.BlockSpec(memory_space=pl.ANY)
    vmem, dma = pltpu.VMEM, pltpu.SemaphoreType.DMA
    scratch = [
        vmem((chunks, 2, A, B, Y, C, rows, LANES), BF16),
        vmem((N, D), BF16),
        vmem((groups, C, rows, N), BF16),
        vmem((N, D), BF16),
        vmem((2, N, CHUNK), BF16),
        vmem((2, N, CHUNK), BF16),
        vmem((RING, A, B, Y, rows, CHUNK), F32),
        vmem((2, A, B, Y, rows, CHUNK), BF16),
        vmem((chunks, A, B, Y, rows, CHUNK), BF16),
        vmem((2, Y - 1, A, B, rows, LANES), BF16),
        vmem((2, B - 1, A, Y, rows, LANES), BF16),
        vmem((2, B - 1, A, rows, LANES), BF16),
        vmem((2, Y - 1, A, rows, LANES), BF16),
        vmem((2, A - 1, rows, CHUNK), BF16),
        vmem((chunks, Y - 1, A, B, rows, LANES), BF16),
        vmem((chunks, B - 1, A, Y, rows, LANES), BF16),
        vmem((chunks, B - 1, A, rows, LANES), BF16),
        vmem((chunks, Y - 1, A, rows, LANES), BF16),
        vmem((chunks, A - 1, rows, CHUNK), BF16),
        vmem(neighbours.shape, jnp.int32),
        vmem(segments.shape, jnp.int32),
        vmem(live.shape, jnp.int32),
        vmem((N // SLOT, SLOT, SLOT), BF16),
        vmem((N, SLOT), F32),
        vmem((2, local, wide), BF16),
        vmem((chunks, rows, CHUNK), F32),
        vmem((A, B, Y, C, 8, LANES), F32),
        vmem((D // LANES, 8, LANES), F32),
        vmem((8, D), F32),
        vmem((A, B, Y, C, 8, LANES), F32),
        vmem((A, B, Y, 8, LANES), F32),
        vmem((A, B, Y, 8, LANES), F32),
        vmem((Y - 1, A, B, 8, LANES), F32),
        vmem((B - 1, A, 8, LANES), F32),
        vmem((A - 1, 8, LANES), F32),
        dma((2, 2 * chunks)),
        dma((2, batches)),
        dma((2, batches)),
        dma((2,)),
        dma((chunks,)),
    ]
    for shape in (
        [(chunks, A - 1), (chunks, B - 1), (chunks, Y - 1), (chunks, Y - 1), (chunks, B - 1), (chunks,)]
        + [(chunks,), (chunks, Y - 1), (chunks, B - 1), (chunks, B - 1), (chunks, Y - 1), (chunks, A - 1)]
        + [(A - 1,), (B - 1,), (Y - 1,), (1,)]
        + [(1,), (Y - 1,), (B - 1,), (A - 1,)]
    ):
        scratch += [dma(shape), dma(shape)]
    act, fgrad, wgrad, bgrad = pl.pallas_call(
        functools.partial(kernel, dims),
        out_shape=[
            jax.ShapeDtypeStruct(features.shape, BF16),
            jax.ShapeDtypeStruct(features.shape, BF16),
            jax.ShapeDtypeStruct(weight.shape, F32),
            jax.ShapeDtypeStruct((1, rows), F32),
        ],
        in_specs=[any_spec] * 7,
        out_specs=[any_spec] * 3 + [pl.BlockSpec(memory_space=pltpu.VMEM)],
        scratch_shapes=scratch,
        compiler_params=pltpu.CompilerParams(
            collective_id=0, has_side_effects=True, vmem_limit_bytes=62 * 2**20
        ),
        cost_estimate=pl.CostEstimate(
            flops=6 * N * D * D, bytes_accessed=8 * N * D, transcendentals=N * D
        ),
    )(features, cotangent, neighbours, segments, live, weight, tile)
    return act, fgrad, wgrad, bgrad.reshape(rows)


def solution(mesh):
    both = ("dp", "rep")
    dims = split_axes(mesh.shape["dp"], mesh.shape["rep"])
    return jax.shard_map(
        functools.partial(per_device, dims),
        mesh=mesh,
        in_specs=(
            P(None, both, None), P(None, both, None), P(None, both, None),
            P(None, both), P(None, both), P(both, None), P(both),
        ),
        out_specs=(P(None, both, None), P(None, both, None), P(both, None), P(both)),
        check_vma=False,
    )
```

```python
import functools

import jax
import jax.numpy as jnp
from jax import lax
from jax.experimental import pallas as pl
from jax.experimental.pallas import tpu as pltpu
from jax.sharding import PartitionSpec as P

SLOT = 128
LANES = 128
CHUNK = 256
MESH = pl.DeviceIdType.MESH
F32, BF16 = jnp.float32, jnp.bfloat16
ENHANCE = 1.0


def split_axes(dp, rep):
    b = 2 ** ((dp.bit_length() - 1) // 2)
    return dp // b, b, rep // 2, 2


def kernel(
    dims, feat, cot, nbr, seg, live, weight, bias, act_out, fgrad_out, wgrad_out, bgrad_out,
    wg, pool, pool_t, gp, ct, act, acc, csend, crecv, s1a, s1b, s2a, s2b, sz, r1a, r1b, r2a, r2b, rz,
    nbuf, sbuf, lbuf, adj_t, scale, fout, wout, bb, brow, bacc, bt, bsum, brc, br1, br2, brz,
    in_sem, ct_sem, act_sem, fout_sem, wout_sem,
    gz_s, gz_r, g1a_s, g1a_r, g1b_s, g1b_r, g2a_s, g2a_r, g2b_s, g2b_r, gc_s, gc_r,
    rc_s, rc_r, p1a_s, p1a_r, p1b_s, p1b_r, p2a_s, p2a_r, p2b_s, p2b_r, pz_s, pz_r,
    bz_s, bz_r, b1_s, b1_r, b2_s, b2_r, bc_s, bc_r, dc_s, dc_r, d1_s, d1_r, d2_s, d2_r, dz_s, dz_r,
):
    A, B, Y, C = dims
    batches, local, D = feat.shape
    rows = weight.shape[0]
    slots = local // SLOT
    N = batches * local
    chunks = D // CHUNK
    groups = A * B * Y
    plane = groups * rows
    wide = D // A

    dp, rep = lax.axis_index("dp"), lax.axis_index("rep")
    a, b, y, c = lax.div(dp, B), lax.rem(dp, B), lax.div(rep, C), lax.rem(rep, C)
    oc = 1 - c

    def device(a_, b_, y_, c_):
        return (a_ * B + b_, y_ * C + c_)

    def columns(k):
        return pl.ds(k * CHUNK, CHUNK)

    def up(v, d, n):
        return lax.rem(v + d, n)

    def down(v, d, n):
        return lax.rem(v + n - d, n)

    to_a = [(d, device(up(a, d, A), b, y, c)) for d in range(1, A)]
    to_b = [(d, device(a, up(b, d, B), y, c)) for d in range(1, B)]
    to_y = [(d, device(a, b, up(y, d, Y), c)) for d in range(1, Y)]
    to_c = device(a, b, y, oc)

    def remote(src, dst, ssem, rsem, dev):
        return pltpu.make_async_remote_copy(
            src_ref=src, dst_ref=dst, send_sem=ssem, recv_sem=rsem, device_id=dev, device_id_type=MESH
        )

    weight_loads = [
        pltpu.make_async_copy(
            weight.at[:, pl.ds((2 * k + h) * LANES, LANES)], wg.at[k, h, a, b, y, c], in_sem.at[0, k * 2 + h]
        )
        for k in range(chunks)
        for h in range(2)
    ]
    side_loads = [
        pltpu.make_async_copy(nbr, nbuf, in_sem.at[1, 0]),
        pltpu.make_async_copy(seg, sbuf, in_sem.at[1, 1]),
        pltpu.make_async_copy(live, lbuf, in_sem.at[1, 2]),
    ]
    feat_loads = [
        pltpu.make_async_copy(feat.at[m], gp.at[pl.ds(m * local, local)], in_sem.at[1, 4 + m]) for m in range(batches)
    ]
    for copy in weight_loads:
        copy.start()
    for copy in side_loads:
        copy.start()
    for copy in feat_loads:
        copy.start()

    barrier = pltpu.get_barrier_semaphore()
    partners = [dev for _, dev in to_a + to_b + to_y] + [to_c]
    for dev in partners:
        pl.semaphore_signal(barrier, inc=1, device_id=dev, device_id_type=MESH)

    def cot_load(k):
        return pltpu.make_async_copy(cot.at[:, :, columns(k)], ct.at[k % 2], ct_sem.at[k % 2])

    def act_store(k):
        return pltpu.make_async_copy(act.at[k % 2], act_out.at[:, :, columns(k)], act_sem.at[k % 2])

    pl.semaphore_wait(barrier, len(partners))

    def gather_z(k, d, dev, mine):
        at = a if mine else down(a, d, A)
        ref = wg.at[k, :, at, b, y, c]
        return remote(ref, ref, gz_s.at[d - 1], gz_r.at[k, d - 1], dev)

    def gather_1(k, mine):
        out = []
        for d, dev in to_b:
            ref = wg.at[k, 0, :, b if mine else down(b, d, B), y, c]
            out.append(remote(ref, ref, g1a_s.at[d - 1], g1a_r.at[k, d - 1], dev))
        for d, dev in to_y:
            ref = wg.at[k, 1, :, b, y if mine else down(y, d, Y), c]
            out.append(remote(ref, ref, g1b_s.at[d - 1], g1b_r.at[k, d - 1], dev))
        return out

    def gather_2(k, mine):
        out = []
        for d, dev in to_y:
            ref = wg.at[k, 0, :, :, y if mine else down(y, d, Y), c]
            out.append(remote(ref, ref, g2a_s.at[d - 1], g2a_r.at[k, d - 1], dev))
        for d, dev in to_b:
            ref = wg.at[k, 1, :, b if mine else down(b, d, B), :, c]
            out.append(remote(ref, ref, g2b_s.at[d - 1], g2b_r.at[k, d - 1], dev))
        return out

    def gather_c(k, mine):
        ref = wg.at[k, :, :, :, :, c if mine else oc]
        return remote(ref, ref, gc_s.at[0], gc_r.at[k], to_c)

    def region(fn):
        pl.when(dp >= 0)(fn)

    def bias_z(d, dev, mine):
        ref = bb.at[a if mine else down(a, d, A), b, y, c]
        return remote(ref, ref, bz_s.at[d - 1], bz_r.at[d - 1], dev)

    def bias_1(d, dev, mine):
        ref = bb.at[:, b if mine else down(b, d, B), y, c]
        return remote(ref, ref, b1_s.at[d - 1], b1_r.at[d - 1], dev)

    def bias_2(d, dev, mine):
        ref = bb.at[:, :, y if mine else down(y, d, Y), c]
        return remote(ref, ref, b2_s.at[d - 1], b2_r.at[d - 1], dev)

    def bias_c(mine):
        ref = bb.at[:, :, :, c if mine else oc]
        return remote(ref, ref, bc_s.at[0], bc_r.at[0], to_c)

    def ag1(k):
        for d, dev in to_a:
            gather_z(k, d, dev, False).wait_recv()
        for copy in gather_1(k, True):
            copy.start()

    def ag2(k):
        for copy in gather_1(k, False):
            copy.wait_recv()
        for copy in gather_2(k, True):
            copy.start()

    def ag3(k):
        for copy in gather_2(k, False):
            copy.wait_recv()
        gather_c(k, True).start()

    def bias_ag1():
        for d, dev in to_a:
            bias_z(d, dev, False).wait_recv()
        for d, dev in to_b:
            bias_1(d, dev, True).start()

    def bias_ag2():
        for d, dev in to_b:
            bias_1(d, dev, False).wait_recv()
        for d, dev in to_y:
            bias_2(d, dev, True).start()

    def bias_ag3():
        for d, dev in to_y:
            bias_2(d, dev, False).wait_recv()
        bias_c(True).start()

    def agz(k):
        for copy in weight_loads[2 * k : 2 * k + 2]:
            copy.wait()
        for d, dev in to_a:
            gather_z(k, d, dev, True).start()

    def bias_agz():
        spread = lax.rem(lax.broadcasted_iota(jnp.int32, (rows, LANES), 1), rows)
        spread = (spread == lax.broadcasted_iota(jnp.int32, (rows, LANES), 0)).astype(F32).astype(BF16)
        own_bias = jnp.broadcast_to(bias[...], (8, rows))
        bb[a, b, y, c] = jnp.dot(own_bias, spread, preferred_element_type=F32)
        for d, dev in to_a:
            bias_z(d, dev, True).start()

    bias_agz()
    agz(0)

    for copy in side_loads:
        copy.wait()
    cot_load(0).start()
    bacc[...] = jnp.zeros_like(bacc)

    def pooling(m, q):
        s = m * slots + q
        here = pl.multiple_of(q * SLOT, SLOT)
        flat = pl.multiple_of(s * SLOT, SLOT)
        listed = nbuf[m, :, pl.ds(here, SLOT)].astype(F32).astype(BF16)
        lane = lax.broadcasted_iota(jnp.int32, (SLOT, SLOT), 1)
        sub = lax.broadcasted_iota(jnp.int32, (SLOT, SLOT), 0)
        position = sub.astype(F32).astype(BF16)
        counted = jnp.zeros((SLOT, SLOT), BF16)
        for j in range(listed.shape[0]):
            counted = counted + jnp.where(listed[j : j + 1, :] == position, jnp.bfloat16(1), jnp.bfloat16(0))
        counted = counted.astype(F32).T
        ids, alive = sbuf[m : m + 1, pl.ds(here, SLOT)], lbuf[m : m + 1, pl.ds(here, SLOT)]
        along = jnp.where(alive > 0, ids, -1)
        down_ = jnp.broadcast_to(jnp.where(alive > 0, ids, -2), (SLOT, SLOT)).T
        adjacency = jnp.where(down_ == along, counted, 0.0)
        degree = jnp.sum(adjacency, axis=1, keepdims=True)
        factor = jnp.where(down_ >= 0, 1.0 / (degree + 1.0), 0.0)
        adjacency = jnp.where(lane == sub, (1.0 + ENHANCE) * (adjacency + 1.0), adjacency)
        adj_t[s] = adjacency.T.astype(BF16)
        scale[pl.ds(flat, SLOT), :] = factor
        pooled = jnp.dot(adjacency.astype(BF16), gp[pl.ds(flat, SLOT), :], preferred_element_type=F32)
        pooled = (pooled * jnp.concatenate([factor] * (D // SLOT), axis=1)).astype(BF16)
        pool[pl.ds(flat, SLOT), :] = pooled
        pool_t[:, :, :, pl.ds(flat, SLOT)] = pooled.T.reshape(groups, C, rows, SLOT)

    early = {
        1: [bias_ag1, lambda: ag1(0), lambda: agz(1)],
        6: [bias_ag2, lambda: ag2(0), lambda: agz(2)],
        8: [lambda: ag1(1)],
        10: [lambda: agz(3)],
        12: [lambda: agz(4)],
        13: [bias_ag3, lambda: ag3(0), lambda: ag1(2), lambda: ag2(1)],
    }
    for m in range(batches):
        feat_loads[m].wait()

        def step(q, carry, m=m):
            pooling(m, q)
            for at, events in early.items():
                if m * slots <= at < (m + 1) * slots:

                    @pl.when(q == at - m * slots)
                    def _(events=events):
                        for event in events:
                            event()

            return carry

        lax.fori_loop(0, slots, step, 0)

    bias_c(False).wait_recv()
    tiles = bb[...].reshape(groups * C, 8, LANES)
    per = LANES // rows
    owner = lax.div(lax.broadcasted_iota(jnp.int32, (1, LANES), 1), rows)
    for j in range(D // LANES):
        row = jnp.zeros((1, LANES), F32)
        for p in range(per):
            row = jnp.where(owner == p, tiles[j * per + p, 0:1, :], row)
        brow[j] = jnp.broadcast_to(row, (8, LANES))

    def reduce_c(k):
        return remote(csend.at[k % 2], crecv.at[k], rc_s.at[k], rc_r.at[k], to_c)

    def reduce_1(k):
        e = k % 2
        out_a = [
            remote(s1a.at[e, d - 1], r1a.at[k, d - 1], p1a_s.at[k, d - 1], p1a_r.at[k, d - 1], dev) for d, dev in to_y
        ]
        out_b = [
            remote(s1b.at[e, d - 1], r1b.at[k, d - 1], p1b_s.at[k, d - 1], p1b_r.at[k, d - 1], dev) for d, dev in to_b
        ]
        return out_a + out_b

    def reduce_2(k):
        e = k % 2
        out_a = [
            remote(s2a.at[e, d - 1], r2a.at[k, d - 1], p2a_s.at[k, d - 1], p2a_r.at[k, d - 1], dev) for d, dev in to_b
        ]
        out_b = [
            remote(s2b.at[e, d - 1], r2b.at[k, d - 1], p2b_s.at[k, d - 1], p2b_r.at[k, d - 1], dev) for d, dev in to_y
        ]
        return out_a + out_b

    def reduce_z(k):
        e = k % 2
        return [remote(sz.at[e, d - 1], rz.at[k, d - 1], pz_s.at[k, d - 1], pz_r.at[k, d - 1], dev) for d, dev in to_a]

    def ago(k, n, copies):
        if k >= n:
            for copy in copies(k - n):
                copy.wait_send()

    lo, hi = slice(0, LANES), slice(LANES, CHUNK)

    def rs1(k):
        t, e = k, k % 2
        reduce_c(k).wait_recv()
        ago(k, 2, reduce_1)
        for d, _ in to_y:
            v = up(y, d, Y)
            s1a[e, d - 1] = (acc[t, :, :, v, :, lo] + crecv[k, :, :, v, :, lo].astype(F32)).astype(BF16)
        for d, _ in to_b:
            v = up(b, d, B)
            s1b[e, d - 1] = (acc[t, :, v, :, :, hi] + crecv[k, :, v, :, :, hi].astype(F32)).astype(BF16)
        for copy in reduce_1(k):
            copy.start()
        acc[t, :, :, y, :, lo] = acc[t, :, :, y, :, lo] + crecv[k, :, :, y, :, lo].astype(F32)
        acc[t, :, b, :, :, hi] = acc[t, :, b, :, :, hi] + crecv[k, :, b, :, :, hi].astype(F32)

    def rs2(k):
        t, e = k, k % 2
        for copy in reduce_1(k):
            copy.wait_recv()
        ago(k, 2, reduce_2)

        def total_a(v):
            out = acc[t, :, v, y, :, lo]
            for d, _ in to_y:
                out = out + r1a[k, d - 1, :, v].astype(F32)
            return out

        def total_b(v):
            out = acc[t, :, b, v, :, hi]
            for d, _ in to_b:
                out = out + r1b[k, d - 1, :, v].astype(F32)
            return out

        for d, _ in to_b:
            s2a[e, d - 1] = total_a(up(b, d, B)).astype(BF16)
        for d, _ in to_y:
            s2b[e, d - 1] = total_b(up(y, d, Y)).astype(BF16)
        for copy in reduce_2(k):
            copy.start()
        acc[t, :, b, y, :, lo] = total_a(b)
        acc[t, :, b, y, :, hi] = total_b(y)

    def rs3(k):
        t, e = k, k % 2
        for copy in reduce_2(k):
            copy.wait_recv()
        ago(k, 2, reduce_z)

        def total(v):
            left, right = acc[t, v, b, y, :, lo], acc[t, v, b, y, :, hi]
            for d, _ in to_b:
                left = left + r2a[k, d - 1, v].astype(F32)
            for d, _ in to_y:
                right = right + r2b[k, d - 1, v].astype(F32)
            return jnp.concatenate([left, right], axis=1)

        for d, _ in to_a:
            sz[e, d - 1] = total(up(a, d, A)).astype(BF16)
        for copy in reduce_z(k):
            copy.start()
        acc[t, a, b, y] = total(a)

    def wout_store(k):
        cols = columns(k)
        return pltpu.make_async_copy(wout.at[k], wgrad_out.at[:, cols], wout_sem.at[0])

    def rs4(k):
        t = k
        for copy in reduce_z(k):
            copy.wait_recv()
        out = acc[t, a, b, y]
        for d, _ in to_a:
            out = out + rz[k, d - 1].astype(F32)
        wout[k] = out
        wout_store(k).start()

    def forward(k):
        e = k % 2
        w = jnp.concatenate([wg[k, h].reshape(D, LANES) for h in range(2)], axis=1)
        offset = jnp.concatenate([brow[2 * k + h][0:1] for h in range(2)], axis=1)
        sums = jnp.zeros((8, CHUNK), F32)
        for m in range(batches):
            part = slice(m * local, (m + 1) * local)
            preact = jnp.dot(pool[part, :], w, preferred_element_type=F32) + offset
            squash = jax.nn.sigmoid(preact)
            active = preact * squash
            act[e, m] = active.astype(BF16)
            grad = (ct[e, m].astype(F32) * (squash + active * (1.0 - squash))).astype(BF16)
            gp[part, columns(k)] = grad
            sums = sums + jnp.sum(grad.astype(F32).reshape(local // 8, 8, CHUNK), axis=0)
        bacc[:, columns(k)] = sums

    def weight_term(k, which):
        left = pool_t[:, which].reshape(plane, N)
        return jnp.dot(left, gp[:, columns(k)], preferred_element_type=F32).reshape(A, B, Y, rows, CHUNK)

    def forward_region(k):
        gather_c(k, False).wait_recv()
        cot_load(k).wait()
        if k + 1 < chunks:
            cot_load(k + 1).start()
        if k >= 2:
            act_store(k - 2).wait()

    def weight_region(k):
        ago(k, 2, lambda j: [reduce_c(j)])

    def weight_terms(k):
        csend[k % 2] = weight_term(k, oc).astype(BF16)
        acc[k] = weight_term(k, c)

    regions = [(0, None), (None, 0), (1, None)] + [(k, k - 1) for k in range(2, chunks)] + [(None, chunks - 1)]
    plan = [
        (ag1, {3: 0, 4: 1, 5: 3, 6: 4, 7: 5}),
        (agz, {5: 0, 6: 1, 7: 2}),
        (ag3, {1: 1, 2: 2, 3: 3, 4: 4, 5: 5, 6: 6, 7: 7}),
        (ag2, {2: 0, 3: 2, 4: 3, 5: 4, 6: 5, 7: 6}),
        (rs4, {}),
        (rs3, {0: 8, 1: 9}),
        (rs2, {0: 6, 1: 7, 2: 8, 3: 9}),
        (rs1, {0: 4, 1: 5, 2: 6, 3: 7, 4: 8, 5: 9}),
    ]
    for at, (f, w) in enumerate(regions):
        for stage, when in plan:
            for k, ahead in when.items():
                if ahead == at:
                    stage(k)
        if f is not None:
            forward_region(f)
        if w is not None:
            weight_region(w)

        @region
        def _(f=f, w=w):
            if f is not None:
                forward(f)
            if w is not None:
                weight_terms(w)

        if f is not None:
            act_store(f).start()
        if w is not None:
            reduce_c(w).start()

    def bred_c():
        return remote(bt.at[:, :, :, oc], brc, dc_s.at[0], dc_r.at[0], to_c)

    def bred_1():
        return [remote(bsum.at[:, :, up(y, d, Y)], br1.at[d - 1], d1_s.at[d - 1], d1_r.at[d - 1], dev) for d, dev in to_y]

    def bred_2():
        return [remote(bsum.at[:, up(b, d, B), y], br2.at[d - 1], d2_s.at[d - 1], d2_r.at[d - 1], dev) for d, dev in to_b]

    def bred_z():
        return [remote(bsum.at[up(a, d, A), b, y], brz.at[d - 1], dz_s.at[d - 1], dz_r.at[d - 1], dev) for d, dev in to_a]

    for a_ in range(A):
        for b_ in range(B):
            for y_ in range(Y):
                for c_ in range(C):
                    block = (((a_ * B + b_) * Y + y_) * C + c_) * rows // LANES
                    bt[a_, b_, y_, c_] = bacc[:, block * LANES : (block + 1) * LANES]
    bred_c().start()

    def bias_rs1():
        bred_c().wait_recv()
        bsum[...] = bt[:, :, :, c] + brc[...]
        for copy in bred_1():
            copy.start()

    def bias_rs2():
        for copy in bred_1():
            copy.wait_recv()
        for d, _ in to_y:
            bsum[:, :, y] = bsum[:, :, y] + br1[d - 1]
        for copy in bred_2():
            copy.start()

    def bias_rs3():
        for copy in bred_2():
            copy.wait_recv()
        for d, _ in to_b:
            bsum[:, b, y] = bsum[:, b, y] + br2[d - 1]
        for copy in bred_z():
            copy.start()

    def bias_rs4():
        for copy in bred_z():
            copy.wait_recv()
        out = bsum[a, b, y]
        for d, _ in to_a:
            out = out + brz[d - 1]
        out = jnp.sum(out, axis=0, keepdims=True)
        place = lax.rem((dp * (Y * C) + rep) * rows, LANES)
        mine = jnp.zeros((1, rows), F32)
        for p in range(per):
            mine = jnp.where(place == p * rows, out[:, p * rows : (p + 1) * rows], mine)
        bgrad_out[...] = mine

    def fout_store(i):
        return pltpu.make_async_copy(
            fout.at[lax.rem(i, 2)],
            fgrad_out.at[lax.rem(i, batches), :, pl.ds(pl.multiple_of(lax.div(i, batches) * wide, wide), wide)],
            fout_sem.at[lax.rem(i, 2)],
        )

    def feature_grad(i):
        e, n, m = lax.rem(i, 2), lax.div(i, batches), lax.rem(i, batches)
        base = pl.multiple_of(m * local, local)
        w = jnp.concatenate([wg[k, h, n].reshape(wide, LANES) for k in range(chunks) for h in range(2)], axis=1)
        grad = lax.dot_general(gp[pl.ds(base, local), :], w, (((1,), (1,)), ((), ())), preferred_element_type=F32)
        grad = grad * jnp.concatenate([scale[pl.ds(base, local), :]] * (wide // LANES), axis=1)
        high = grad.astype(BF16)
        low = (grad - high.astype(F32)).astype(BF16)
        for q in range(slots):
            left = adj_t[m * slots + q]
            part = slice(q * SLOT, (q + 1) * SLOT)
            right = jnp.concatenate([high[part], low[part]], axis=0)
            out = jnp.dot(jnp.concatenate([left, left], axis=1), right, preferred_element_type=F32)
            fout[e, part, :] = out.astype(BF16)

    late = [
        (rs1, {6: 0, 7: 2}),
        (rs2, {4: 0, 5: 1, 6: 4, 7: 6}),
        (rs3, {2: 0, 3: 1, 4: 3, 5: 5, 6: 7, 7: 9}),
        (rs4, {0: 0, 1: 1, 2: 3, 3: 4, 4: 6, 5: 8, 6: 10, 7: 11}),
        (lambda _: bias_rs1(), {0: 1}),
        (lambda _: bias_rs2(), {0: 4}),
        (lambda _: bias_rs3(), {0: 7}),
        (lambda _: bias_rs4(), {0: 10}),
    ]
    steps = A * batches

    def last(i, carry):
        @pl.when(i >= 2)
        def _():
            fout_store(i - 2).wait()

        pl.when(i >= 0)(lambda: feature_grad(i))
        fout_store(i).start()
        for stage, when in late:
            for k, at in when.items():
                pl.when(i == at)(functools.partial(stage, k))
        return carry

    lax.fori_loop(0, steps, last, 0)

    for i in (steps - 2, steps - 1):
        fout_store(i).wait()
    for k in (chunks - 2, chunks - 1):
        act_store(k).wait()
        for copy in [reduce_c(k)] + reduce_1(k) + reduce_2(k) + reduce_z(k):
            copy.wait_send()

    def drained(ref, sem, dev):
        remote(ref, ref, sem, sem, dev).wait_send()

    pltpu.make_async_copy(wgrad_out, wgrad_out, wout_sem.at[0]).wait()
    for d, dev in to_a:
        drained(wg.at[:, :, a, b, y, c], gz_s.at[d - 1], dev)
    for d, dev in to_b:
        drained(wg.at[:, 0, :, b, y, c], g1a_s.at[d - 1], dev)
        drained(wg.at[:, 1, :, b, :, c], g2b_s.at[d - 1], dev)
    for d, dev in to_y:
        drained(wg.at[:, 1, :, b, y, c], g1b_s.at[d - 1], dev)
        drained(wg.at[:, 0, :, :, y, c], g2a_s.at[d - 1], dev)
    drained(wg.at[:, :, :, :, :, c], gc_s.at[0], to_c)
    for d, dev in to_a:
        bias_z(d, dev, True).wait_send()
    for d, dev in to_b:
        bias_1(d, dev, True).wait_send()
    for d, dev in to_y:
        bias_2(d, dev, True).wait_send()
    bias_c(True).wait_send()
    for copy in [bred_c()] + bred_1() + bred_2() + bred_z():
        copy.wait_send()


def per_device(dims, features, cotangent, neighbours, segments, live, weight, bias):
    A, B, Y, C = dims
    batches, local, D = features.shape
    rows = weight.shape[0]
    N = batches * local
    chunks = D // CHUNK
    groups = A * B * Y
    wide = D // A
    neighbours = jnp.swapaxes(neighbours, 1, 2)
    any_spec = pl.BlockSpec(memory_space=pl.ANY)
    vmem, dma = pltpu.VMEM, pltpu.SemaphoreType.DMA
    scratch = [
        vmem((chunks, 2, A, B, Y, C, rows, LANES), BF16),
        vmem((N, D), BF16),
        vmem((groups, C, rows, N), BF16),
        vmem((N, D), BF16),
        vmem((2, batches, local, CHUNK), BF16),
        vmem((2, batches, local, CHUNK), BF16),
        vmem((chunks, A, B, Y, rows, CHUNK), F32),
        vmem((2, A, B, Y, rows, CHUNK), BF16),
        vmem((chunks, A, B, Y, rows, CHUNK), BF16),
        vmem((2, Y - 1, A, B, rows, LANES), BF16),
        vmem((2, B - 1, A, Y, rows, LANES), BF16),
        vmem((2, B - 1, A, rows, LANES), BF16),
        vmem((2, Y - 1, A, rows, LANES), BF16),
        vmem((2, A - 1, rows, CHUNK), BF16),
        vmem((chunks, Y - 1, A, B, rows, LANES), BF16),
        vmem((chunks, B - 1, A, Y, rows, LANES), BF16),
        vmem((chunks, B - 1, A, rows, LANES), BF16),
        vmem((chunks, Y - 1, A, rows, LANES), BF16),
        vmem((chunks, A - 1, rows, CHUNK), BF16),
        vmem(neighbours.shape, jnp.int32),
        vmem(segments.shape, jnp.int32),
        vmem(live.shape, jnp.int32),
        vmem((N // SLOT, SLOT, SLOT), BF16),
        vmem((N, SLOT), F32),
        vmem((2, local, wide), BF16),
        vmem((chunks, rows, CHUNK), F32),
        vmem((A, B, Y, C, 8, LANES), F32),
        vmem((D // LANES, 8, LANES), F32),
        vmem((8, D), F32),
        vmem((A, B, Y, C, 8, LANES), F32),
        vmem((A, B, Y, 8, LANES), F32),
        vmem((A, B, Y, 8, LANES), F32),
        vmem((Y - 1, A, B, 8, LANES), F32),
        vmem((B - 1, A, 8, LANES), F32),
        vmem((A - 1, 8, LANES), F32),
        dma((2, 2 * chunks)),
        dma((2,)),
        dma((2,)),
        dma((2,)),
        dma((1,)),
    ]
    for sent, received in (
        ((A - 1,), (chunks, A - 1)),
        ((B - 1,), (chunks, B - 1)),
        ((Y - 1,), (chunks, Y - 1)),
        ((Y - 1,), (chunks, Y - 1)),
        ((B - 1,), (chunks, B - 1)),
        ((1,), (chunks,)),
        ((chunks,), (chunks,)),
        ((chunks, Y - 1), (chunks, Y - 1)),
        ((chunks, B - 1), (chunks, B - 1)),
        ((chunks, B - 1), (chunks, B - 1)),
        ((chunks, Y - 1), (chunks, Y - 1)),
        ((chunks, A - 1), (chunks, A - 1)),
        ((A - 1,), (A - 1,)),
        ((B - 1,), (B - 1,)),
        ((Y - 1,), (Y - 1,)),
        ((1,), (1,)),
        ((1,), (1,)),
        ((Y - 1,), (Y - 1,)),
        ((B - 1,), (B - 1,)),
        ((A - 1,), (A - 1,)),
    ):
        scratch += [dma(sent), dma(received)]
    act, fgrad, wgrad, bgrad = pl.pallas_call(
        functools.partial(kernel, dims),
        out_shape=[
            jax.ShapeDtypeStruct(features.shape, BF16),
            jax.ShapeDtypeStruct(features.shape, BF16),
            jax.ShapeDtypeStruct(weight.shape, F32),
            jax.ShapeDtypeStruct((1, rows), F32),
        ],
        in_specs=[any_spec] * 6 + [pl.BlockSpec(memory_space=pltpu.VMEM)],
        out_specs=[any_spec] * 3 + [pl.BlockSpec(memory_space=pltpu.VMEM)],
        scratch_shapes=scratch,
        compiler_params=pltpu.CompilerParams(
            collective_id=0, has_side_effects=True, vmem_limit_bytes=62 * 2**20
        ),
        cost_estimate=pl.CostEstimate(
            flops=6 * N * D * D, bytes_accessed=8 * N * D, transcendentals=N * D
        ),
    )(features, cotangent, neighbours, segments, live, weight, bias.reshape(1, rows))
    return act, fgrad, wgrad, bgrad.reshape(rows)


def solution(mesh):
    both = ("dp", "rep")
    dims = split_axes(mesh.shape["dp"], mesh.shape["rep"])
    return jax.shard_map(
        functools.partial(per_device, dims),
        mesh=mesh,
        in_specs=(
            P(None, both, None), P(None, both, None), P(None, both, None),
            P(None, both), P(None, both), P(both, None), P(both),
        ),
        out_specs=(P(None, both, None), P(None, both, None), P(both, None), P(both)),
        check_vma=False,
    )
```

```python
import functools

import jax
import jax.numpy as jnp
from jax import lax
from jax.experimental import pallas as pl
from jax.experimental.pallas import tpu as pltpu
from jax.sharding import PartitionSpec as P

SLOT = 128
LANES = 128
CHUNK = 256
MESH = pl.DeviceIdType.MESH
F32, BF16 = jnp.float32, jnp.bfloat16
ENHANCE = 1.0
LATE = 1
SLOTS = 6
LAST_GATHERED = (6, 7)


def split_axes(dp, rep):
    b = 2 ** ((dp.bit_length() - 1) // 2)
    return dp // b, b, rep // 2, 2


def feature_tile(dims, wg, gp, adj_t, scale, local, n, m):
    A, B, Y, C = dims
    chunks, rows = wg.shape[0], wg.shape[-2]
    wide = B * Y * C * rows
    slots = local // SLOT
    base = m * local if isinstance(m, int) else pl.multiple_of(m * local, local)
    w = jnp.concatenate([wg[k, h, n].reshape(wide, LANES) for k in range(chunks) for h in range(2)], axis=1)
    grad = lax.dot_general(gp[pl.ds(base, local), :], w, (((1,), (1,)), ((), ())), preferred_element_type=F32)
    grad = grad * jnp.concatenate([scale[pl.ds(base, local), :]] * (wide // LANES), axis=1)
    high = grad.astype(BF16)
    low = (grad - high.astype(F32)).astype(BF16)
    tiles = []
    for q in range(slots):
        left = adj_t[m * slots + q]
        part = slice(q * SLOT, (q + 1) * SLOT)
        right = jnp.concatenate([high[part], low[part]], axis=0)
        out = jnp.dot(jnp.concatenate([left, left], axis=1), right, preferred_element_type=F32)
        tiles.append(out.astype(BF16))
    return jnp.concatenate(tiles, axis=0)


def finish(
    dims, act, wg, gp, done, adj_t, scale, wout, bgrad_in, act_out, fgrad_out, wgrad_out, bgrad_out,
    fout, act_sem, done_sem, fout_sem, wout_sem,
):
    batches, local, D = fgrad_out.shape
    blocks, wide, early = dims[0], D // dims[0], batches - LATE

    def store(i):
        n, m = i // LATE, early + i % LATE
        return pltpu.make_async_copy(fout.at[i], fgrad_out.at[m, :, pl.ds(n * wide, wide)], fout_sem.at[i])

    kept = [pltpu.make_async_copy(wout, wgrad_out, wout_sem.at[0])]
    for m in range(early):
        kept.append(pltpu.make_async_copy(done.at[pl.ds(m * local, local)], fgrad_out.at[m], done_sem.at[m]))
    for copy in kept:
        copy.start()
    for k in range(act.shape[0]):
        pltpu.make_async_copy(act.at[k], act_out.at[:, :, pl.ds(k * CHUNK, CHUNK)], act_sem.at[0]).start()
    bgrad_out[...] = bgrad_in[...]
    for i in range(blocks * LATE):
        @pl.when(lax.axis_index("dp") >= 0)
        def _(i=i):
            fout[i] = feature_tile(dims, wg, gp, adj_t, scale, local, i // LATE, i % LATE)

        store(i).start()
    for i in range(blocks * LATE):
        store(i).wait()
    pltpu.make_async_copy(act, act, act_sem.at[0]).wait()
    for copy in kept:
        copy.wait()


def kernel(
    dims, feat, cot, nbr, seg, live, weight, bias, act, wg, gp_l, pool_e, adj_l, scale_l, wout, bgrad_out,
    gp_e, pool_l, adj_e, scale_e, pool_t, ct, acc, csend, crecv, s1a, s1b, s2a, s2b, sz, r1a, r1b, r2a, r2b, rz,
    nbuf, sbuf, lbuf, bb, brow, bacc, bt, bsum, brc, br1, br2, brz,
    in_sem, ct_sem,
    gz_s, gz_r, g1a_s, g1a_r, g1b_s, g1b_r, g2a_s, g2a_r, g2b_s, g2b_r, gc_s, gc_r,
    rc_s, rc_r, p1a_s, p1a_r, p1b_s, p1b_r, p2a_s, p2a_r, p2b_s, p2b_r, pz_s, pz_r,
    bz_s, bz_r, b1_s, b1_r, b2_s, b2_r, bc_s, bc_r, dc_s, dc_r, d1_s, d1_r, d2_s, d2_r, dz_s, dz_r,
):
    A, B, Y, C = dims
    batches, local, D = feat.shape
    rows = weight.shape[0]
    slots = local // SLOT
    N = batches * local
    chunks = D // CHUNK
    groups = A * B * Y
    plane = groups * rows
    first = batches - LATE
    wide = D // A

    dp, rep = lax.axis_index("dp"), lax.axis_index("rep")
    a, b, y, c = lax.div(dp, B), lax.rem(dp, B), lax.div(rep, C), lax.rem(rep, C)
    oc = 1 - c

    def device(a_, b_, y_, c_):
        return (a_ * B + b_, y_ * C + c_)

    def columns(k):
        return pl.ds(k * CHUNK, CHUNK)

    def of(m, ref_e, ref_l):
        return (ref_e, m) if m < first else (ref_l, m - first)

    def rows_of(m, ref_e, ref_l):
        ref, at = of(m, ref_e, ref_l)
        return ref.at[pl.ds(at * local, local)]

    def up(v, d, n):
        return lax.rem(v + d, n)

    def down(v, d, n):
        return lax.rem(v + n - d, n)

    to_a = [(d, device(up(a, d, A), b, y, c)) for d in range(1, A)]
    to_b = [(d, device(a, up(b, d, B), y, c)) for d in range(1, B)]
    to_y = [(d, device(a, b, up(y, d, Y), c)) for d in range(1, Y)]
    to_c = device(a, b, y, oc)

    def remote(src, dst, ssem, rsem, dev):
        return pltpu.make_async_remote_copy(
            src_ref=src, dst_ref=dst, send_sem=ssem, recv_sem=rsem, device_id=dev, device_id_type=MESH
        )

    weight_loads = [
        pltpu.make_async_copy(
            weight.at[:, pl.ds((2 * k + h) * LANES, LANES)], wg.at[k, h, a, b, y, c], in_sem.at[0]
        )
        for k in range(chunks)
        for h in range(2)
    ]
    side_loads = [
        pltpu.make_async_copy(nbr, nbuf, in_sem.at[1]),
        pltpu.make_async_copy(seg, sbuf, in_sem.at[2]),
        pltpu.make_async_copy(live, lbuf, in_sem.at[3]),
    ]
    feat_loads = [
        pltpu.make_async_copy(feat.at[m], rows_of(m, gp_e, gp_l), in_sem.at[4 + m]) for m in range(batches)
    ]
    for copy in weight_loads:
        copy.start()
    for copy in side_loads:
        copy.start()
    for copy in feat_loads:
        copy.start()

    barrier = pltpu.get_barrier_semaphore()
    partners = [dev for _, dev in to_a + to_b + to_y] + [to_c]
    for dev in partners:
        pl.semaphore_signal(barrier, inc=1, device_id=dev, device_id_type=MESH)

    def cot_load(k):
        return pltpu.make_async_copy(cot.at[:, :, columns(k)], ct.at[k % 2], ct_sem.at[k % 2])

    pl.semaphore_wait(barrier, len(partners))

    def gather_z(k, d, dev):
        ref = wg.at[k, :, a, b, y, c]
        return remote(ref, ref, gz_s.at[0], gz_r.at[k], dev)

    def gather_1(k, mine):
        out = []
        for d, dev in to_b:
            ref = wg.at[k, 0, :, b if mine else down(b, d, B), y, c]
            out.append(remote(ref, ref, g1a_s.at[0, d - 1], g1a_r.at[k, d - 1], dev))
        for d, dev in to_y:
            ref = wg.at[k, 1, :, b, y if mine else down(y, d, Y), c]
            out.append(remote(ref, ref, g1b_s.at[0, d - 1], g1b_r.at[k, d - 1], dev))
        return out

    def gather_2(k, mine):
        out = []
        for d, dev in to_y:
            ref = wg.at[k, 0, :, :, y if mine else down(y, d, Y), c]
            out.append(remote(ref, ref, g2a_s.at[0, d - 1], g2a_r.at[k, d - 1], dev))
        for d, dev in to_b:
            ref = wg.at[k, 1, :, b if mine else down(b, d, B), :, c]
            out.append(remote(ref, ref, g2b_s.at[0, d - 1], g2b_r.at[k, d - 1], dev))
        return out

    def turned_1(k, mine):
        out = []
        for d, dev in to_b:
            ref = wg.at[k, 0, a, b if mine else down(b, d, B), y, c]
            out.append(remote(ref, ref, g1a_s.at[1, d - 1], g1a_r.at[k, d - 1], dev))
        for d, dev in to_y:
            ref = wg.at[k, 1, a, b, y if mine else down(y, d, Y), c]
            out.append(remote(ref, ref, g1b_s.at[1, d - 1], g1b_r.at[k, d - 1], dev))
        return out

    def turned_2(k, mine):
        out = []
        for d, dev in to_y:
            ref = wg.at[k, 0, a, :, y if mine else down(y, d, Y), c]
            out.append(remote(ref, ref, g2a_s.at[1, d - 1], g2a_r.at[k, d - 1], dev))
        for d, dev in to_b:
            ref = wg.at[k, 1, a, b if mine else down(b, d, B), :, c]
            out.append(remote(ref, ref, g2b_s.at[1, d - 1], g2b_r.at[k, d - 1], dev))
        return out

    def turned_z(k):
        out = []
        ref = wg.at[k, :, a, :, :, c]
        for d, dev in to_a:
            out.append(remote(ref, ref, gz_s.at[1], gz_r.at[k], dev))
        return out

    def gather_c(k, mine):
        ref = wg.at[k, :, :, :, :, c if mine else oc]
        return remote(ref, ref, gc_s.at[0], gc_r.at[k], to_c)

    def region(fn):
        pl.when(dp >= 0)(fn)

    def bias_z(d, dev):
        ref = bb.at[a, b, y, c]
        return remote(ref, ref, bz_s.at[0], bz_r.at[0], dev)

    def bias_1(d, dev, mine):
        ref = bb.at[:, b if mine else down(b, d, B), y, c]
        return remote(ref, ref, b1_s.at[d - 1], b1_r.at[d - 1], dev)

    def bias_2(d, dev, mine):
        ref = bb.at[:, :, y if mine else down(y, d, Y), c]
        return remote(ref, ref, b2_s.at[d - 1], b2_r.at[d - 1], dev)

    def bias_c(mine):
        ref = bb.at[:, :, :, c if mine else oc]
        return remote(ref, ref, bc_s.at[0], bc_r.at[0], to_c)

    def ag1(k):
        every = wg.at[k, :, : A - 1, b, y, c]
        remote(every, every, gz_s.at[0], gz_r.at[k], to_c).wait_recv()
        for copy in gather_1(k, True):
            copy.start()

    def ag2(k):
        for copy in gather_1(k, False):
            copy.wait_recv()
        for copy in gather_2(k, True):
            copy.start()

    def ag3(k):
        for copy in gather_2(k, False):
            copy.wait_recv()
        gather_c(k, True).start()

    def at1(k):
        for copy in turned_1(k, True):
            copy.start()

    def at2(k):
        for copy in turned_1(k, False):
            copy.wait_recv()
        for copy in turned_2(k, True):
            copy.start()

    def atz(k):
        for copy in turned_2(k, False):
            copy.wait_recv()
        for copy in turned_z(k):
            copy.start()

    def at3(k):
        every = wg.at[k, :, : A - 1, :, :, c]
        remote(every, every, gz_s.at[1], gz_r.at[k], to_c).wait_recv()
        gather_c(k, True).start()

    def bias_ag1():
        every = bb.at[: A - 1, b, y, c]
        remote(every, every, bz_s.at[0], bz_r.at[0], to_c).wait_recv()
        for d, dev in to_b:
            bias_1(d, dev, True).start()

    def bias_ag2():
        for d, dev in to_b:
            bias_1(d, dev, False).wait_recv()
        for d, dev in to_y:
            bias_2(d, dev, True).start()

    def bias_ag3():
        for d, dev in to_y:
            bias_2(d, dev, False).wait_recv()
        bias_c(True).start()

    def agz(k):
        for d, dev in to_a:
            gather_z(k, d, dev).start()

    def bias_agz():
        spread = lax.rem(lax.broadcasted_iota(jnp.int32, (rows, LANES), 1), rows)
        spread = (spread == lax.broadcasted_iota(jnp.int32, (rows, LANES), 0)).astype(F32).astype(BF16)
        own_bias = jnp.broadcast_to(bias[...], (8, rows))
        bb[a, b, y, c] = jnp.dot(own_bias, spread, preferred_element_type=F32)
        for d, dev in to_a:
            bias_z(d, dev).start()

    pltpu.make_async_copy(weight, weight, in_sem.at[0]).wait()
    bias_agz()
    agz(0)
    for k in LAST_GATHERED:
        at1(k)

    for copy in side_loads:
        copy.wait()
    cot_load(0).start()
    bacc[...] = jnp.zeros_like(bacc)

    def pooling(m, q):
        here = pl.multiple_of(q * SLOT, SLOT)
        flat = pl.multiple_of((m * slots + q) * SLOT, SLOT)
        listed = nbuf[m, :, pl.ds(here, SLOT)].astype(F32).astype(BF16)
        lane = lax.broadcasted_iota(jnp.int32, (SLOT, SLOT), 1)
        sub = lax.broadcasted_iota(jnp.int32, (SLOT, SLOT), 0)
        position = sub.astype(F32).astype(BF16)
        counted = jnp.zeros((SLOT, SLOT), BF16)
        for j in range(listed.shape[0]):
            counted = counted + jnp.where(listed[j : j + 1, :] == position, jnp.bfloat16(1), jnp.bfloat16(0))
        counted = counted.astype(F32).T
        ids, alive = sbuf[m : m + 1, pl.ds(here, SLOT)], lbuf[m : m + 1, pl.ds(here, SLOT)]
        along = jnp.where(alive > 0, ids, -1)
        down_ = jnp.broadcast_to(jnp.where(alive > 0, ids, -2), (SLOT, SLOT)).T
        adjacency = jnp.where(down_ == along, counted, 0.0)
        degree = jnp.sum(adjacency, axis=1, keepdims=True)
        factor = jnp.where(down_ >= 0, 1.0 / (degree + 1.0), 0.0)
        adjacency = jnp.where(lane == sub, (1.0 + ENHANCE) * (adjacency + 1.0), adjacency)
        adj, at = of(m, adj_e, adj_l)
        adj[at * slots + q] = adjacency.T.astype(BF16)
        rows_of(m, scale_e, scale_l)[pl.ds(here, SLOT), :] = factor
        block = rows_of(m, gp_e, gp_l)[pl.ds(here, SLOT), :]
        pooled = jnp.dot(adjacency.astype(BF16), block, preferred_element_type=F32)
        pooled = (pooled * jnp.concatenate([factor] * (D // SLOT), axis=1)).astype(BF16)
        rows_of(m, pool_e, pool_l)[pl.ds(here, SLOT), :] = pooled
        pool_t[:, :, :, pl.ds(flat, SLOT)] = pooled.T.reshape(groups, C, rows, SLOT)

    early = {
        2: [lambda: agz(1)],
        4: [bias_ag1, lambda: ag1(0)],
        6: [lambda: at2(6), lambda: at2(7), lambda: agz(2)],
        10: [bias_ag2, lambda: ag2(0), lambda: ag1(1), lambda: agz(3)],
    }
    for m in range(batches):
        feat_loads[m].wait()

        def step(q, carry, m=m):
            pooling(m, q)
            for at, events in early.items():
                if m * slots <= at < (m + 1) * slots:

                    @pl.when(q == at - m * slots)
                    def _(events=events):
                        for event in events:
                            event()

            return carry

        lax.fori_loop(0, slots, step, 0)

    agz(4)
    ag1(2)
    bias_ag3()
    ag3(0)
    agz(5)

    bias_c(False).wait_recv()
    tiles = bb[...].reshape(groups * C, 8, LANES)
    per = LANES // rows
    owner = lax.div(lax.broadcasted_iota(jnp.int32, (1, LANES), 1), rows)
    for j in range(D // LANES):
        row = jnp.zeros((1, LANES), F32)
        for p in range(per):
            row = jnp.where(owner == p, tiles[j * per + p, 0:1, :], row)
        brow[j] = jnp.broadcast_to(row, (8, LANES))

    def reduce_c(k):
        return remote(csend.at[k % 2], crecv.at[k], rc_s.at[k % 2], rc_r.at[k], to_c)

    def reduce_1(k):
        e = k % 2
        out_a = [
            remote(s1a.at[e, d - 1], r1a.at[k, d - 1], p1a_s.at[e, d - 1], p1a_r.at[k, d - 1], dev) for d, dev in to_y
        ]
        out_b = [
            remote(s1b.at[e, d - 1], r1b.at[k, d - 1], p1b_s.at[e, d - 1], p1b_r.at[k, d - 1], dev) for d, dev in to_b
        ]
        return out_a + out_b

    def reduce_2(k):
        e = k % 2
        out_a = [
            remote(s2a.at[e, d - 1], r2a.at[k, d - 1], p2a_s.at[e, d - 1], p2a_r.at[k, d - 1], dev) for d, dev in to_b
        ]
        out_b = [
            remote(s2b.at[e, d - 1], r2b.at[k, d - 1], p2b_s.at[e, d - 1], p2b_r.at[k, d - 1], dev) for d, dev in to_y
        ]
        return out_a + out_b

    def reduce_z(k):
        e = k % 2
        return [remote(sz.at[e, d - 1], rz.at[k, d - 1], pz_s.at[e], pz_r.at[k], dev) for d, dev in to_a]

    def reduce_z_sent(k):
        remote(sz.at[k % 2], rz.at[k], pz_s.at[k % 2], pz_r.at[k], to_c).wait_send()

    def ago(k, n, copies):
        if k >= n:
            for copy in copies(k - n):
                copy.wait_send()

    lo, hi = slice(0, LANES), slice(LANES, CHUNK)

    def rs1(k):
        t, e = k % SLOTS, k % 2
        reduce_c(k).wait_recv()
        ago(k, 2, reduce_1)
        for d, _ in to_y:
            v = up(y, d, Y)
            s1a[e, d - 1] = (acc[t, :, :, v, :, lo] + crecv[k, :, :, v, :, lo].astype(F32)).astype(BF16)
        for d, _ in to_b:
            v = up(b, d, B)
            s1b[e, d - 1] = (acc[t, :, v, :, :, hi] + crecv[k, :, v, :, :, hi].astype(F32)).astype(BF16)
        for copy in reduce_1(k):
            copy.start()
        acc[t, :, :, y, :, lo] = acc[t, :, :, y, :, lo] + crecv[k, :, :, y, :, lo].astype(F32)
        acc[t, :, b, :, :, hi] = acc[t, :, b, :, :, hi] + crecv[k, :, b, :, :, hi].astype(F32)

    def rs2(k):
        t, e = k % SLOTS, k % 2
        for copy in reduce_1(k):
            copy.wait_recv()
        ago(k, 2, reduce_2)

        def total_a(v):
            out = acc[t, :, v, y, :, lo]
            for d, _ in to_y:
                out = out + r1a[k, d - 1, :, v].astype(F32)
            return out

        def total_b(v):
            out = acc[t, :, b, v, :, hi]
            for d, _ in to_b:
                out = out + r1b[k, d - 1, :, v].astype(F32)
            return out

        for d, _ in to_b:
            s2a[e, d - 1] = total_a(up(b, d, B)).astype(BF16)
        for d, _ in to_y:
            s2b[e, d - 1] = total_b(up(y, d, Y)).astype(BF16)
        for copy in reduce_2(k):
            copy.start()
        acc[t, :, b, y, :, lo] = total_a(b)
        acc[t, :, b, y, :, hi] = total_b(y)

    def rs3(k):
        t, e = k % SLOTS, k % 2
        for copy in reduce_2(k):
            copy.wait_recv()
        if k >= 2:
            reduce_z_sent(k - 2)

        def total(v):
            left, right = acc[t, v, b, y, :, lo], acc[t, v, b, y, :, hi]
            for d, _ in to_b:
                left = left + r2a[k, d - 1, v].astype(F32)
            for d, _ in to_y:
                right = right + r2b[k, d - 1, v].astype(F32)
            return jnp.concatenate([left, right], axis=1)

        for d, _ in to_a:
            sz[e, d - 1] = total(up(a, d, A)).astype(BF16)
        for copy in reduce_z(k):
            copy.start()
        acc[t, a, b, y] = total(a)

    def rs4(k):
        t = k % SLOTS
        remote(sz.at[k % 2], rz.at[k], pz_s.at[k % 2], pz_r.at[k], to_c).wait_recv()
        out = acc[t, a, b, y]
        for d, _ in to_a:
            out = out + rz[k, d - 1].astype(F32)
        wout[:, columns(k)] = out

    def bred_c():
        return remote(bt.at[:, :, :, oc], brc, dc_s.at[0], dc_r.at[0], to_c)

    def bred_1():
        return [remote(bsum.at[:, :, up(y, d, Y)], br1.at[d - 1], d1_s.at[d - 1], d1_r.at[d - 1], dev) for d, dev in to_y]

    def bred_2():
        return [remote(bsum.at[:, up(b, d, B), y], br2.at[d - 1], d2_s.at[d - 1], d2_r.at[d - 1], dev) for d, dev in to_b]

    def bred_z():
        return [remote(bsum.at[up(a, d, A), b, y], brz.at[d - 1], dz_s.at[0], dz_r.at[0], dev) for d, dev in to_a]

    def bias_rs0():
        for a_ in range(A):
            for b_ in range(B):
                for y_ in range(Y):
                    for c_ in range(C):
                        block = (((a_ * B + b_) * Y + y_) * C + c_) * rows // LANES
                        bt[a_, b_, y_, c_] = bacc[:, block * LANES : (block + 1) * LANES]
        bred_c().start()

    def bias_rs1():
        bred_c().wait_recv()
        bsum[...] = bt[:, :, :, c] + brc[...]
        for copy in bred_1():
            copy.start()

    def bias_rs2():
        for copy in bred_1():
            copy.wait_recv()
        for d, _ in to_y:
            bsum[:, :, y] = bsum[:, :, y] + br1[d - 1]
        for copy in bred_2():
            copy.start()

    def bias_rs3():
        for copy in bred_2():
            copy.wait_recv()
        for d, _ in to_b:
            bsum[:, b, y] = bsum[:, b, y] + br2[d - 1]
        for copy in bred_z():
            copy.start()

    def bias_rs4():
        remote(brz, brz, dz_s.at[0], dz_r.at[0], to_c).wait_recv()
        out = bsum[a, b, y]
        for d, _ in to_a:
            out = out + brz[d - 1]
        out = jnp.sum(out, axis=0, keepdims=True)
        place = lax.rem((dp * (Y * C) + rep) * rows, LANES)
        mine = jnp.zeros((1, rows), F32)
        for p in range(per):
            mine = jnp.where(place == p * rows, out[:, p * rows : (p + 1) * rows], mine)
        bgrad_out[...] = mine

    def forward(k):
        e = k % 2
        w = jnp.concatenate([wg[k, h].reshape(D, LANES) for h in range(2)], axis=1)
        offset = jnp.concatenate([brow[2 * k + h][0:1] for h in range(2)], axis=1)
        sums = jnp.zeros((8, CHUNK), F32)
        for m in range(batches):
            preact = jnp.dot(rows_of(m, pool_e, pool_l)[...], w, preferred_element_type=F32) + offset
            squash = jax.nn.sigmoid(preact)
            active = preact * squash
            act[k, m] = active.astype(BF16)
            grad = (ct[e, m].astype(F32) * (squash + active * (1.0 - squash))).astype(BF16)
            rows_of(m, gp_e, gp_l)[:, columns(k)] = grad
            sums = sums + jnp.sum(grad.astype(F32).reshape(local // 8, 8, CHUNK), axis=0)
        bacc[:, columns(k)] = sums

    def weight_term(k, which):
        left = pool_t[:, which].reshape(plane, N)
        right = jnp.concatenate([gp_e[:, columns(k)], gp_l[:, columns(k)]], axis=0)
        return jnp.dot(left, right, preferred_element_type=F32).reshape(A, B, Y, rows, CHUNK)

    def forward_region(k):
        gather_c(k, False).wait_recv()
        cot_load(k).wait()
        if k + 1 < chunks:
            cot_load(k + 1).start()

    def weight_region(k):
        if k >= 2:
            reduce_c(k - 2).wait_send()

    def weight_terms(k):
        csend[k % 2] = weight_term(k, oc).astype(BF16)
        acc[k % SLOTS] = weight_term(k, c)

    regions = [(0, None), (None, 0), (1, None), (None, 1), (2, None)]
    regions += [(k, k - 1) for k in range(3, chunks)] + [(None, chunks - 1)]
    plan = [
        (lambda _: bias_rs0(), {0: 10}),
        (lambda _: bias_rs1(), {0: 11}),
        (ag2, {1: 0, 2: 1, 3: 2, 4: 3, 5: 5}),
        (ag1, {3: 0, 4: 1, 5: 3}),
        (ag3, {1: 1, 2: 3, 3: 4, 4: 5, 5: 6}),
        (at3, {6: 7, 7: 8}),
        (atz, {6: 0, 7: 4}),
        (rs4, {0: 9, 1: 10}),
        (rs3, {0: 8, 1: 9, 2: 10}),
        (rs2, {0: 7, 1: 8, 2: 9, 3: 10, 4: 11}),
        (rs1, {0: 5, 1: 6, 2: 7, 3: 8, 4: 9, 5: 10, 6: 11}),
    ]
    regions.append((None, None))
    for at, (f, w) in enumerate(regions):
        for stage, when in plan:
            for k, ahead in when.items():
                if ahead == at:
                    stage(k)
        if f is not None:
            forward_region(f)
        if w is not None:
            weight_region(w)
        if f is None and w is None:
            continue

        @region
        def _(f=f, w=w):
            if f is not None:
                forward(f)
            if w is not None:
                weight_terms(w)

        if w is not None:
            reduce_c(w).start()

    def feature_grad(i):
        n, m = lax.div(i, first), lax.rem(i, first)
        part, cols = pl.ds(pl.multiple_of(m * local, local), local), pl.ds(pl.multiple_of(n * wide, wide), wide)
        pool_e[part, cols] = feature_tile(dims, wg, gp_e, adj_e, scale_e, local, n, m)

    late = [
        (rs1, {7: 0}),
        (lambda _: bias_rs2(), {0: 1}),
        (rs2, {5: 1, 6: 2, 7: 4}),
        (rs3, {3: 0, 4: 2, 5: 4, 6: 5, 7: 6}),
        (lambda _: bias_rs3(), {0: 5}),
        (rs4, {2: 1, 3: 3, 4: 5, 5: 7, 6: 7, 7: 7}),
        (lambda _: bias_rs4(), {0: 7}),
    ]

    def last(i, carry):
        pl.when(i >= 0)(lambda: feature_grad(i))
        for stage, when in late:
            for k, at in when.items():
                pl.when(i == at)(functools.partial(stage, k))
        return carry

    lax.fori_loop(0, A * first, last, 0)

    for k in (chunks - 2, chunks - 1):
        for copy in [reduce_c(k)] + reduce_1(k) + reduce_2(k):
            copy.wait_send()
        reduce_z_sent(k)

    def drained(ref, sem, dev):
        remote(ref, ref, sem, sem, dev).wait_send()

    plain, turned = slice(0, LAST_GATHERED[0]), slice(LAST_GATHERED[0], chunks)
    drained(wg.at[plain, :, : A - 1, b, y, c], gz_s.at[0], to_c)
    drained(wg.at[turned, :, : A - 1, :, :, c], gz_s.at[1], to_c)
    for d, dev in to_b:
        drained(wg.at[plain, 0, :, b, y, c], g1a_s.at[0, d - 1], dev)
        drained(wg.at[plain, 1, :, b, :, c], g2b_s.at[0, d - 1], dev)
        drained(wg.at[turned, 0, a, b, y, c], g1a_s.at[1, d - 1], dev)
        drained(wg.at[turned, 1, a, b, :, c], g2b_s.at[1, d - 1], dev)
    for d, dev in to_y:
        drained(wg.at[plain, 1, :, b, y, c], g1b_s.at[0, d - 1], dev)
        drained(wg.at[plain, 0, :, :, y, c], g2a_s.at[0, d - 1], dev)
        drained(wg.at[turned, 1, a, b, y, c], g1b_s.at[1, d - 1], dev)
        drained(wg.at[turned, 0, a, :, y, c], g2a_s.at[1, d - 1], dev)
    drained(wg.at[:, :, :, :, :, c], gc_s.at[0], to_c)
    drained(bb.at[: A - 1, b, y, c], bz_s.at[0], to_c)
    for d, dev in to_b:
        bias_1(d, dev, True).wait_send()
    for d, dev in to_y:
        bias_2(d, dev, True).wait_send()
    bias_c(True).wait_send()
    for copy in [bred_c()] + bred_1() + bred_2():
        copy.wait_send()
    drained(brz, dz_s.at[0], to_c)


def per_device(dims, features, cotangent, neighbours, segments, live, weight, bias):
    A, B, Y, C = dims
    batches, local, D = features.shape
    rows = weight.shape[0]
    N = batches * local
    N_l = LATE * local
    N_e = N - N_l
    chunks = D // CHUNK
    groups = A * B * Y
    wide = D // A
    neighbours = jnp.swapaxes(neighbours, 1, 2)
    any_spec = pl.BlockSpec(memory_space=pl.ANY)
    vmem, dma = pltpu.VMEM, pltpu.SemaphoreType.DMA
    scratch = [
        vmem((N_e, D), BF16),
        vmem((N_l, D), BF16),
        vmem((N_e // SLOT, SLOT, SLOT), BF16),
        vmem((N_e, SLOT), F32),
        vmem((groups, C, rows, N), BF16),
        vmem((2, batches, local, CHUNK), BF16),
        vmem((SLOTS, A, B, Y, rows, CHUNK), F32),
        vmem((2, A, B, Y, rows, CHUNK), BF16),
        vmem((chunks, A, B, Y, rows, CHUNK), BF16),
        vmem((2, Y - 1, A, B, rows, LANES), BF16),
        vmem((2, B - 1, A, Y, rows, LANES), BF16),
        vmem((2, B - 1, A, rows, LANES), BF16),
        vmem((2, Y - 1, A, rows, LANES), BF16),
        vmem((2, A - 1, rows, CHUNK), BF16),
        vmem((chunks, Y - 1, A, B, rows, LANES), BF16),
        vmem((chunks, B - 1, A, Y, rows, LANES), BF16),
        vmem((chunks, B - 1, A, rows, LANES), BF16),
        vmem((chunks, Y - 1, A, rows, LANES), BF16),
        vmem((chunks, A - 1, rows, CHUNK), BF16),
        vmem(neighbours.shape, jnp.int32),
        vmem(segments.shape, jnp.int32),
        vmem(live.shape, jnp.int32),
        vmem((A, B, Y, C, 8, LANES), F32),
        vmem((D // LANES, 8, LANES), F32),
        vmem((8, D), F32),
        vmem((A, B, Y, C, 8, LANES), F32),
        vmem((A, B, Y, 8, LANES), F32),
        vmem((A, B, Y, 8, LANES), F32),
        vmem((Y - 1, A, B, 8, LANES), F32),
        vmem((B - 1, A, 8, LANES), F32),
        vmem((A - 1, 8, LANES), F32),
        dma((4 + batches,)),
        dma((2,)),
    ]
    for sent, received in (
        ((2,), (chunks,)),
        ((2, B - 1), (chunks, B - 1)),
        ((2, Y - 1), (chunks, Y - 1)),
        ((2, Y - 1), (chunks, Y - 1)),
        ((2, B - 1), (chunks, B - 1)),
        ((1,), (chunks,)),
        ((2,), (chunks,)),
        ((2, Y - 1), (chunks, Y - 1)),
        ((2, B - 1), (chunks, B - 1)),
        ((2, B - 1), (chunks, B - 1)),
        ((2, Y - 1), (chunks, Y - 1)),
        ((2,), (chunks,)),
        ((1,), (1,)),
        ((B - 1,), (B - 1,)),
        ((Y - 1,), (Y - 1,)),
        ((1,), (1,)),
        ((1,), (1,)),
        ((Y - 1,), (Y - 1,)),
        ((B - 1,), (B - 1,)),
        ((1,), (1,)),
    ):
        scratch += [dma(sent), dma(received)]
    vmem_spec = pl.BlockSpec(memory_space=pltpu.VMEM)
    kept = [
        vmem((chunks, batches, local, CHUNK), BF16),
        vmem((chunks, 2, A, B, Y, C, rows, LANES), BF16),
        vmem((N_l, D), BF16),
        vmem((N_e, D), BF16),
        vmem((N_l // SLOT, SLOT, SLOT), BF16),
        vmem((N_l, SLOT), F32),
        vmem((rows, D), F32),
        vmem((1, rows), F32),
    ]
    kept_arrays = pl.pallas_call(
        functools.partial(kernel, dims),
        out_shape=kept,
        in_specs=[any_spec] * 6 + [vmem_spec],
        out_specs=[vmem_spec] * len(kept),
        scratch_shapes=scratch,
        compiler_params=pltpu.CompilerParams(
            collective_id=0, has_side_effects=True, vmem_limit_bytes=39 * 2**20
        ),
        cost_estimate=pl.CostEstimate(
            flops=6 * N * D * D, bytes_accessed=8 * N * D, transcendentals=N * D
        ),
    )(features, cotangent, neighbours, segments, live, weight, bias.reshape(1, rows))
    act, fgrad, wgrad, bgrad = pl.pallas_call(
        functools.partial(finish, dims),
        out_shape=[
            jax.ShapeDtypeStruct(features.shape, BF16),
            jax.ShapeDtypeStruct(features.shape, BF16),
            jax.ShapeDtypeStruct(weight.shape, F32),
            jax.ShapeDtypeStruct((1, rows), F32),
        ],
        in_specs=[vmem_spec] * len(kept),
        out_specs=[any_spec] * 3 + [vmem_spec],
        scratch_shapes=[
            vmem((A * LATE, local, wide), BF16),
            dma((1,)), dma((batches - LATE,)), dma((A * LATE,)), dma((1,)),
        ],
        compiler_params=pltpu.CompilerParams(vmem_limit_bytes=8 * 2**20),
    )(
        *[pltpu.with_memory_space_constraint(x, pltpu.VMEM) for x in kept_arrays],
    )
    return act, fgrad, wgrad, bgrad.reshape(rows)


def solution(mesh):
    both = ("dp", "rep")
    dims = split_axes(mesh.shape["dp"], mesh.shape["rep"])
    return jax.shard_map(
        functools.partial(per_device, dims),
        mesh=mesh,
        in_specs=(
            P(None, both, None), P(None, both, None), P(None, both, None),
            P(None, both), P(None, both), P(both, None), P(both),
        ),
        out_specs=(P(None, both, None), P(None, both, None), P(both, None), P(both)),
        check_vma=False,
    )
```

```python
import functools

import jax
import jax.numpy as jnp
from jax import lax
from jax.experimental import pallas as pl
from jax.experimental.pallas import tpu as pltpu
from jax.sharding import PartitionSpec as P

SLOT = 128
LANES = 128
CHUNK = 256
MESH = pl.DeviceIdType.MESH
F32, BF16 = jnp.float32, jnp.bfloat16
ENHANCE = 1.0
LATE = 1
SLOTS = 6
LAST_GATHERED = (6, 7)


def split_axes(dp, rep):
    b = 2 ** ((dp.bit_length() - 1) // 2)
    return dp // b, b, rep // 2, 2


def feature_tile(dims, wg, gp, adj_t, scale, local, n, m):
    A, B, Y, C = dims
    chunks, rows = wg.shape[0], wg.shape[-2]
    wide = B * Y * C * rows
    slots = local // SLOT
    base = m * local if isinstance(m, int) else pl.multiple_of(m * local, local)
    w = jnp.concatenate([wg[k, h, n].reshape(wide, LANES) for k in range(chunks) for h in range(2)], axis=1)
    grad = lax.dot_general(gp[pl.ds(base, local), :], w, (((1,), (1,)), ((), ())), preferred_element_type=F32)
    grad = grad * jnp.concatenate([scale[pl.ds(base, local), :]] * (wide // LANES), axis=1)
    high = grad.astype(BF16)
    low = (grad - high.astype(F32)).astype(BF16)
    tiles = []
    for q in range(slots):
        left = adj_t[m * slots + q]
        part = slice(q * SLOT, (q + 1) * SLOT)
        right = jnp.concatenate([high[part], low[part]], axis=0)
        out = jnp.dot(jnp.concatenate([left, left], axis=1), right, preferred_element_type=F32)
        tiles.append(out.astype(BF16))
    return jnp.concatenate(tiles, axis=0)


def finish(
    dims, act, wg, gp, done, adj_t, scale, wout, bgrad_in, act_out, fgrad_out, wgrad_out, bgrad_out,
    fout, act_sem, done_sem, fout_sem, wout_sem,
):
    batches, local, D = fgrad_out.shape
    blocks, wide, early = dims[0], D // dims[0], batches - LATE

    def store(i):
        n, m = lax.div(i, LATE), early + lax.rem(i, LATE)
        cols = pl.ds(pl.multiple_of(n * wide, wide), wide)
        return pltpu.make_async_copy(fout.at[i], fgrad_out.at[m, :, cols], fout_sem.at[i])

    kept = [pltpu.make_async_copy(wout, wgrad_out, wout_sem.at[0])]
    for m in range(early):
        kept.append(pltpu.make_async_copy(done.at[pl.ds(m * local, local)], fgrad_out.at[m], done_sem.at[m]))
    for copy in kept:
        copy.start()
    for k in range(act.shape[0]):
        pltpu.make_async_copy(act.at[k], act_out.at[:, :, pl.ds(k * CHUNK, CHUNK)], act_sem.at[0]).start()
    bgrad_out[...] = bgrad_in[...]

    def step(i, carry):
        fout[i] = feature_tile(dims, wg, gp, adj_t, scale, local, lax.div(i, LATE), lax.rem(i, LATE))
        store(i).start()
        return carry

    lax.fori_loop(0, blocks * LATE, step, 0)
    for i in range(blocks * LATE):
        store(i).wait()
    pltpu.make_async_copy(act, act, act_sem.at[0]).wait()
    for copy in kept:
        copy.wait()


def kernel(
    dims, feat, cot, nbr, seg, live, weight, bias, act, wg, gp_l, pool_e, adj_l, scale_l, wout, bgrad_out,
    gp_e, pool_l, adj_e, scale_e, pool_t, ct, acc, csend, crecv, s1a, s1b, s2a, s2b, sz, r1a, r1b, r2a, r2b, rz,
    nbuf, sbuf, lbuf, bb, brow, bacc, bt, bsum, brc, br1, br2, brz,
    in_sem, ct_sem,
    gz_s, gz_r, g1a_s, g1a_r, g1b_s, g1b_r, g2a_s, g2a_r, g2b_s, g2b_r, gc_s, gc_r,
    rc_s, rc_r, p1a_s, p1a_r, p1b_s, p1b_r, p2a_s, p2a_r, p2b_s, p2b_r, pz_s, pz_r,
    bz_s, bz_r, b1_s, b1_r, b2_s, b2_r, bc_s, bc_r, dc_s, dc_r, d1_s, d1_r, d2_s, d2_r, dz_s, dz_r,
):
    A, B, Y, C = dims
    batches, local, D = feat.shape
    rows = weight.shape[0]
    slots = local // SLOT
    N = batches * local
    chunks = D // CHUNK
    groups = A * B * Y
    plane = groups * rows
    first = batches - LATE
    wide = D // A

    dp, rep = lax.axis_index("dp"), lax.axis_index("rep")
    a, b, y, c = lax.div(dp, B), lax.rem(dp, B), lax.div(rep, C), lax.rem(rep, C)
    oc = 1 - c

    def device(a_, b_, y_, c_):
        return (a_ * B + b_, y_ * C + c_)

    def columns(k):
        return pl.ds(k * CHUNK, CHUNK)

    def of(m, ref_e, ref_l):
        return (ref_e, m) if m < first else (ref_l, m - first)

    def rows_of(m, ref_e, ref_l):
        ref, at = of(m, ref_e, ref_l)
        return ref.at[pl.ds(at * local, local)]

    def up(v, d, n):
        return lax.rem(v + d, n)

    def down(v, d, n):
        return lax.rem(v + n - d, n)

    to_a = [(d, device(up(a, d, A), b, y, c)) for d in range(1, A)]
    to_b = [(d, device(a, up(b, d, B), y, c)) for d in range(1, B)]
    to_y = [(d, device(a, b, up(y, d, Y), c)) for d in range(1, Y)]
    to_c = device(a, b, y, oc)

    def remote(src, dst, ssem, rsem, dev):
        return pltpu.make_async_remote_copy(
            src_ref=src, dst_ref=dst, send_sem=ssem, recv_sem=rsem, device_id=dev, device_id_type=MESH
        )

    weight_loads = [
        pltpu.make_async_copy(
            weight.at[:, pl.ds((2 * k + h) * LANES, LANES)], wg.at[k, h, a, b, y, c], in_sem.at[0]
        )
        for k in range(chunks)
        for h in range(2)
    ]
    side_loads = [
        pltpu.make_async_copy(nbr, nbuf, in_sem.at[1]),
        pltpu.make_async_copy(seg, sbuf, in_sem.at[2]),
        pltpu.make_async_copy(live, lbuf, in_sem.at[3]),
    ]
    feat_loads = [
        pltpu.make_async_copy(feat.at[m], rows_of(m, gp_e, gp_l), in_sem.at[4 + m]) for m in range(batches)
    ]
    for copy in weight_loads:
        copy.start()
    for copy in side_loads:
        copy.start()
    for copy in feat_loads:
        copy.start()

    barrier = pltpu.get_barrier_semaphore()
    partners = [dev for _, dev in to_a + to_b + to_y] + [to_c]
    for dev in partners:
        pl.semaphore_signal(barrier, inc=1, device_id=dev, device_id_type=MESH)

    def cot_load(k):
        return pltpu.make_async_copy(cot.at[:, :, columns(k)], ct.at[k % 2], ct_sem.at[k % 2])

    pl.semaphore_wait(barrier, len(partners))

    def gather_z(k, d, dev):
        ref = wg.at[k, :, a, b, y, c]
        return remote(ref, ref, gz_s.at[0], gz_r.at[k], dev)

    def gather_1(k, mine):
        out = []
        for d, dev in to_b:
            ref = wg.at[k, 0, :, b if mine else down(b, d, B), y, c]
            out.append(remote(ref, ref, g1a_s.at[0, d - 1], g1a_r.at[k, d - 1], dev))
        for d, dev in to_y:
            ref = wg.at[k, 1, :, b, y if mine else down(y, d, Y), c]
            out.append(remote(ref, ref, g1b_s.at[0, d - 1], g1b_r.at[k, d - 1], dev))
        return out

    def gather_2(k, mine):
        out = []
        for d, dev in to_y:
            ref = wg.at[k, 0, :, :, y if mine else down(y, d, Y), c]
            out.append(remote(ref, ref, g2a_s.at[0, d - 1], g2a_r.at[k, d - 1], dev))
        for d, dev in to_b:
            ref = wg.at[k, 1, :, b if mine else down(b, d, B), :, c]
            out.append(remote(ref, ref, g2b_s.at[0, d - 1], g2b_r.at[k, d - 1], dev))
        return out

    def turned_1(k, mine):
        out = []
        for d, dev in to_b:
            ref = wg.at[k, 0, a, b if mine else down(b, d, B), y, c]
            out.append(remote(ref, ref, g1a_s.at[1, d - 1], g1a_r.at[k, d - 1], dev))
        for d, dev in to_y:
            ref = wg.at[k, 1, a, b, y if mine else down(y, d, Y), c]
            out.append(remote(ref, ref, g1b_s.at[1, d - 1], g1b_r.at[k, d - 1], dev))
        return out

    def turned_2(k, mine):
        out = []
        for d, dev in to_y:
            ref = wg.at[k, 0, a, :, y if mine else down(y, d, Y), c]
            out.append(remote(ref, ref, g2a_s.at[1, d - 1], g2a_r.at[k, d - 1], dev))
        for d, dev in to_b:
            ref = wg.at[k, 1, a, b if mine else down(b, d, B), :, c]
            out.append(remote(ref, ref, g2b_s.at[1, d - 1], g2b_r.at[k, d - 1], dev))
        return out

    def turned_z(k):
        out = []
        ref = wg.at[k, :, a, :, :, c]
        for d, dev in to_a:
            out.append(remote(ref, ref, gz_s.at[1], gz_r.at[k], dev))
        return out

    def gather_c(k, mine):
        ref = wg.at[k, :, :, :, :, c if mine else oc]
        return remote(ref, ref, gc_s.at[0], gc_r.at[k], to_c)

    def region(fn):
        pl.when(dp >= 0)(fn)

    def bias_z(d, dev):
        ref = bb.at[a, b, y, c]
        return remote(ref, ref, bz_s.at[0], bz_r.at[0], dev)

    def bias_1(d, dev, mine):
        ref = bb.at[:, b if mine else down(b, d, B), y, c]
        return remote(ref, ref, b1_s.at[d - 1], b1_r.at[d - 1], dev)

    def bias_2(d, dev, mine):
        ref = bb.at[:, :, y if mine else down(y, d, Y), c]
        return remote(ref, ref, b2_s.at[d - 1], b2_r.at[d - 1], dev)

    def bias_c(mine):
        ref = bb.at[:, :, :, c if mine else oc]
        return remote(ref, ref, bc_s.at[0], bc_r.at[0], to_c)

    def ag1(k):
        every = wg.at[k, :, : A - 1, b, y, c]
        remote(every, every, gz_s.at[0], gz_r.at[k], to_c).wait_recv()
        for copy in gather_1(k, True):
            copy.start()

    def ag2(k):
        for copy in gather_1(k, False):
            copy.wait_recv()
        for copy in gather_2(k, True):
            copy.start()

    def ag3(k):
        for copy in gather_2(k, False):
            copy.wait_recv()
        gather_c(k, True).start()

    def at1(k):
        for copy in turned_1(k, True):
            copy.start()

    def at2(k):
        for copy in turned_1(k, False):
            copy.wait_recv()
        for copy in turned_2(k, True):
            copy.start()

    def atz(k):
        for copy in turned_2(k, False):
            copy.wait_recv()
        for copy in turned_z(k):
            copy.start()

    def at3(k):
        every = wg.at[k, :, : A - 1, :, :, c]
        remote(every, every, gz_s.at[1], gz_r.at[k], to_c).wait_recv()
        gather_c(k, True).start()

    def bias_ag1():
        every = bb.at[: A - 1, b, y, c]
        remote(every, every, bz_s.at[0], bz_r.at[0], to_c).wait_recv()
        for d, dev in to_b:
            bias_1(d, dev, True).start()

    def bias_ag2():
        for d, dev in to_b:
            bias_1(d, dev, False).wait_recv()
        for d, dev in to_y:
            bias_2(d, dev, True).start()

    def bias_ag3():
        for d, dev in to_y:
            bias_2(d, dev, False).wait_recv()
        bias_c(True).start()

    def agz(k):
        for d, dev in to_a:
            gather_z(k, d, dev).start()

    def bias_agz():
        spread = lax.rem(lax.broadcasted_iota(jnp.int32, (rows, LANES), 1), rows)
        spread = (spread == lax.broadcasted_iota(jnp.int32, (rows, LANES), 0)).astype(F32).astype(BF16)
        own_bias = jnp.broadcast_to(bias[...], (8, rows))
        bb[a, b, y, c] = jnp.dot(own_bias, spread, preferred_element_type=F32)
        for d, dev in to_a:
            bias_z(d, dev).start()

    pltpu.make_async_copy(weight, weight, in_sem.at[0]).wait()
    bias_agz()
    agz(0)
    for k in LAST_GATHERED:
        at1(k)

    for copy in side_loads:
        copy.wait()
    cot_load(0).start()
    bacc[...] = jnp.zeros_like(bacc)

    def pooling(m, q):
        here = pl.multiple_of(q * SLOT, SLOT)
        flat = pl.multiple_of((m * slots + q) * SLOT, SLOT)
        listed = nbuf[m, :, pl.ds(here, SLOT)].astype(F32).astype(BF16)
        lane = lax.broadcasted_iota(jnp.int32, (SLOT, SLOT), 1)
        sub = lax.broadcasted_iota(jnp.int32, (SLOT, SLOT), 0)
        position = sub.astype(F32).astype(BF16)
        counted = jnp.zeros((SLOT, SLOT), BF16)
        for j in range(listed.shape[0]):
            counted = counted + jnp.where(listed[j : j + 1, :] == position, jnp.bfloat16(1), jnp.bfloat16(0))
        counted = counted.astype(F32).T
        ids, alive = sbuf[m : m + 1, pl.ds(here, SLOT)], lbuf[m : m + 1, pl.ds(here, SLOT)]
        along = jnp.where(alive > 0, ids, -1)
        down_ = jnp.broadcast_to(jnp.where(alive > 0, ids, -2), (SLOT, SLOT)).T
        adjacency = jnp.where(down_ == along, counted, 0.0)
        degree = jnp.sum(adjacency, axis=1, keepdims=True)
        factor = jnp.where(down_ >= 0, 1.0 / (degree + 1.0), 0.0)
        adjacency = jnp.where(lane == sub, (1.0 + ENHANCE) * (adjacency + 1.0), adjacency)
        adj, at = of(m, adj_e, adj_l)
        adj[at * slots + q] = adjacency.T.astype(BF16)
        rows_of(m, scale_e, scale_l)[pl.ds(here, SLOT), :] = factor
        block = rows_of(m, gp_e, gp_l)[pl.ds(here, SLOT), :]
        pooled = jnp.dot(adjacency.astype(BF16), block, preferred_element_type=F32)
        pooled = (pooled * jnp.concatenate([factor] * (D // SLOT), axis=1)).astype(BF16)
        rows_of(m, pool_e, pool_l)[pl.ds(here, SLOT), :] = pooled
        pool_t[:, :, :, pl.ds(flat, SLOT)] = pooled.T.reshape(groups, C, rows, SLOT)

    early = {
        2: [lambda: agz(1)],
        4: [bias_ag1, lambda: ag1(0)],
        6: [lambda: at2(6), lambda: at2(7), lambda: agz(2)],
        10: [bias_ag2, lambda: ag2(0), lambda: ag1(1), lambda: agz(3)],
    }
    for m in range(batches):
        feat_loads[m].wait()

        def step(q, carry, m=m):
            pooling(m, q)
            for at, events in early.items():
                if m * slots <= at < (m + 1) * slots:

                    @pl.when(q == at - m * slots)
                    def _(events=events):
                        for event in events:
                            event()

            return carry

        lax.fori_loop(0, slots, step, 0)

    agz(4)
    ag1(2)
    bias_ag3()
    ag3(0)
    agz(5)

    bias_c(False).wait_recv()
    tiles = bb[...].reshape(groups * C, 8, LANES)
    per = LANES // rows
    owner = lax.div(lax.broadcasted_iota(jnp.int32, (1, LANES), 1), rows)
    for j in range(D // LANES):
        row = jnp.zeros((1, LANES), F32)
        for p in range(per):
            row = jnp.where(owner == p, tiles[j * per + p, 0:1, :], row)
        brow[j] = jnp.broadcast_to(row, (8, LANES))

    def reduce_c(k):
        return remote(csend.at[k % 2], crecv.at[k], rc_s.at[k % 2], rc_r.at[k], to_c)

    def reduce_1(k):
        e = k % 2
        out_a = [
            remote(s1a.at[e, d - 1], r1a.at[k, d - 1], p1a_s.at[e, d - 1], p1a_r.at[k, d - 1], dev) for d, dev in to_y
        ]
        out_b = [
            remote(s1b.at[e, d - 1], r1b.at[k, d - 1], p1b_s.at[e, d - 1], p1b_r.at[k, d - 1], dev) for d, dev in to_b
        ]
        return out_a + out_b

    def reduce_2(k):
        e = k % 2
        out_a = [
            remote(s2a.at[e, d - 1], r2a.at[k, d - 1], p2a_s.at[e, d - 1], p2a_r.at[k, d - 1], dev) for d, dev in to_b
        ]
        out_b = [
            remote(s2b.at[e, d - 1], r2b.at[k, d - 1], p2b_s.at[e, d - 1], p2b_r.at[k, d - 1], dev) for d, dev in to_y
        ]
        return out_a + out_b

    def reduce_z(k):
        e = k % 2
        return [remote(sz.at[e, d - 1], rz.at[k, d - 1], pz_s.at[e], pz_r.at[k], dev) for d, dev in to_a]

    def reduce_z_sent(k):
        remote(sz.at[k % 2], rz.at[k], pz_s.at[k % 2], pz_r.at[k], to_c).wait_send()

    def ago(k, n, copies):
        if k >= n:
            for copy in copies(k - n):
                copy.wait_send()

    lo, hi = slice(0, LANES), slice(LANES, CHUNK)

    def rs1(k):
        t, e = k % SLOTS, k % 2
        reduce_c(k).wait_recv()
        ago(k, 2, reduce_1)
        for d, _ in to_y:
            v = up(y, d, Y)
            s1a[e, d - 1] = (acc[t, :, :, v, :, lo] + crecv[k, :, :, v, :, lo].astype(F32)).astype(BF16)
        for d, _ in to_b:
            v = up(b, d, B)
            s1b[e, d - 1] = (acc[t, :, v, :, :, hi] + crecv[k, :, v, :, :, hi].astype(F32)).astype(BF16)
        for copy in reduce_1(k):
            copy.start()
        acc[t, :, :, y, :, lo] = acc[t, :, :, y, :, lo] + crecv[k, :, :, y, :, lo].astype(F32)
        acc[t, :, b, :, :, hi] = acc[t, :, b, :, :, hi] + crecv[k, :, b, :, :, hi].astype(F32)

    def rs2(k):
        t, e = k % SLOTS, k % 2
        for copy in reduce_1(k):
            copy.wait_recv()
        ago(k, 2, reduce_2)

        def total_a(v):
            out = acc[t, :, v, y, :, lo]
            for d, _ in to_y:
                out = out + r1a[k, d - 1, :, v].astype(F32)
            return out

        def total_b(v):
            out = acc[t, :, b, v, :, hi]
            for d, _ in to_b:
                out = out + r1b[k, d - 1, :, v].astype(F32)
            return out

        for d, _ in to_b:
            s2a[e, d - 1] = total_a(up(b, d, B)).astype(BF16)
        for d, _ in to_y:
            s2b[e, d - 1] = total_b(up(y, d, Y)).astype(BF16)
        for copy in reduce_2(k):
            copy.start()
        acc[t, :, b, y, :, lo] = total_a(b)
        acc[t, :, b, y, :, hi] = total_b(y)

    def rs3(k):
        t, e = k % SLOTS, k % 2
        for copy in reduce_2(k):
            copy.wait_recv()
        if k >= 2:
            reduce_z_sent(k - 2)

        def total(v):
            left, right = acc[t, v, b, y, :, lo], acc[t, v, b, y, :, hi]
            for d, _ in to_b:
                left = left + r2a[k, d - 1, v].astype(F32)
            for d, _ in to_y:
                right = right + r2b[k, d - 1, v].astype(F32)
            return jnp.concatenate([left, right], axis=1)

        for d, _ in to_a:
            sz[e, d - 1] = total(up(a, d, A)).astype(BF16)
        for copy in reduce_z(k):
            copy.start()
        acc[t, a, b, y] = total(a)

    def rs4(k):
        t = k % SLOTS
        remote(sz.at[k % 2], rz.at[k], pz_s.at[k % 2], pz_r.at[k], to_c).wait_recv()
        out = acc[t, a, b, y]
        for d, _ in to_a:
            out = out + rz[k, d - 1].astype(F32)
        wout[:, columns(k)] = out

    def bred_c():
        return remote(bt.at[:, :, :, oc], brc, dc_s.at[0], dc_r.at[0], to_c)

    def bred_1():
        return [remote(bsum.at[:, :, up(y, d, Y)], br1.at[d - 1], d1_s.at[d - 1], d1_r.at[d - 1], dev) for d, dev in to_y]

    def bred_2():
        return [remote(bsum.at[:, up(b, d, B), y], br2.at[d - 1], d2_s.at[d - 1], d2_r.at[d - 1], dev) for d, dev in to_b]

    def bred_z():
        return [remote(bsum.at[up(a, d, A), b, y], brz.at[d - 1], dz_s.at[0], dz_r.at[0], dev) for d, dev in to_a]

    def bias_rs0():
        for a_ in range(A):
            for b_ in range(B):
                for y_ in range(Y):
                    for c_ in range(C):
                        block = (((a_ * B + b_) * Y + y_) * C + c_) * rows // LANES
                        bt[a_, b_, y_, c_] = bacc[:, block * LANES : (block + 1) * LANES]
        bred_c().start()

    def bias_rs1():
        bred_c().wait_recv()
        bsum[...] = bt[:, :, :, c] + brc[...]
        for copy in bred_1():
            copy.start()

    def bias_rs2():
        for copy in bred_1():
            copy.wait_recv()
        for d, _ in to_y:
            bsum[:, :, y] = bsum[:, :, y] + br1[d - 1]
        for copy in bred_2():
            copy.start()

    def bias_rs3():
        for copy in bred_2():
            copy.wait_recv()
        for d, _ in to_b:
            bsum[:, b, y] = bsum[:, b, y] + br2[d - 1]
        for copy in bred_z():
            copy.start()

    def bias_rs4():
        remote(brz, brz, dz_s.at[0], dz_r.at[0], to_c).wait_recv()
        out = bsum[a, b, y]
        for d, _ in to_a:
            out = out + brz[d - 1]
        out = jnp.sum(out, axis=0, keepdims=True)
        place = lax.rem((dp * (Y * C) + rep) * rows, LANES)
        mine = jnp.zeros((1, rows), F32)
        for p in range(per):
            mine = jnp.where(place == p * rows, out[:, p * rows : (p + 1) * rows], mine)
        bgrad_out[...] = mine

    def forward(k):
        e = k % 2
        w = jnp.concatenate([wg[k, h].reshape(D, LANES) for h in range(2)], axis=1)
        offset = jnp.concatenate([brow[2 * k + h][0:1] for h in range(2)], axis=1)
        sums = jnp.zeros((8, CHUNK), F32)
        for m in range(batches):
            preact = jnp.dot(rows_of(m, pool_e, pool_l)[...], w, preferred_element_type=F32) + offset
            squash = jax.nn.sigmoid(preact)
            active = preact * squash
            act[k, m] = active.astype(BF16)
            grad = (ct[e, m].astype(F32) * (squash + active * (1.0 - squash))).astype(BF16)
            rows_of(m, gp_e, gp_l)[:, columns(k)] = grad
            sums = sums + jnp.sum(grad.astype(F32).reshape(local // 8, 8, CHUNK), axis=0)
        bacc[:, columns(k)] = sums

    def weight_term(k, which):
        left = pool_t[:, which].reshape(plane, N)
        right = jnp.concatenate([gp_e[:, columns(k)], gp_l[:, columns(k)]], axis=0)
        return jnp.dot(left, right, preferred_element_type=F32).reshape(A, B, Y, rows, CHUNK)

    def forward_region(k):
        gather_c(k, False).wait_recv()
        cot_load(k).wait()
        if k + 1 < chunks:
            cot_load(k + 1).start()

    def weight_region(k):
        if k >= 2:
            reduce_c(k - 2).wait_send()

    def weight_terms(k):
        csend[k % 2] = weight_term(k, oc).astype(BF16)
        acc[k % SLOTS] = weight_term(k, c)

    regions = [(0, None), (None, 0), (1, None), (None, 1), (2, None)]
    regions += [(k, k - 1) for k in range(3, chunks)] + [(None, chunks - 1)]
    plan = [
        (lambda _: bias_rs0(), {0: 10}),
        (lambda _: bias_rs1(), {0: 11}),
        (ag2, {1: 0, 2: 1, 3: 2, 4: 3, 5: 5}),
        (ag1, {3: 0, 4: 1, 5: 3}),
        (ag3, {1: 1, 2: 3, 3: 4, 4: 5, 5: 6}),
        (at3, {6: 7, 7: 8}),
        (atz, {6: 0, 7: 4}),
        (rs4, {0: 9, 1: 10}),
        (rs3, {0: 8, 1: 9, 2: 10}),
        (rs2, {0: 7, 1: 8, 2: 9, 3: 10, 4: 11}),
        (rs1, {0: 5, 1: 6, 2: 7, 3: 8, 4: 9, 5: 10, 6: 11}),
    ]
    regions.append((None, None))
    for at, (f, w) in enumerate(regions):
        for stage, when in plan:
            for k, ahead in when.items():
                if ahead == at:
                    stage(k)
        if f is not None:
            forward_region(f)
        if w is not None:
            weight_region(w)
        if f is None and w is None:
            continue

        @region
        def _(f=f, w=w):
            if f is not None:
                forward(f)
            if w is not None:
                weight_terms(w)

        if w is not None:
            reduce_c(w).start()

    def feature_grad(i):
        n, m = lax.div(i, first), lax.rem(i, first)
        part, cols = pl.ds(pl.multiple_of(m * local, local), local), pl.ds(pl.multiple_of(n * wide, wide), wide)
        pool_e[part, cols] = feature_tile(dims, wg, gp_e, adj_e, scale_e, local, n, m)

    late = [
        (rs1, {7: 0}),
        (lambda _: bias_rs2(), {0: 1}),
        (rs2, {5: 1, 6: 2, 7: 4}),
        (rs3, {3: 0, 4: 2, 5: 4, 6: 5, 7: 6}),
        (lambda _: bias_rs3(), {0: 5}),
        (rs4, {2: 1, 3: 3, 4: 5, 5: 7, 6: 7, 7: 7}),
        (lambda _: bias_rs4(), {0: 7}),
    ]

    def last(i, carry):
        pl.when(i >= 0)(lambda: feature_grad(i))
        for stage, when in late:
            for k, at in when.items():
                pl.when(i == at)(functools.partial(stage, k))
        return carry

    lax.fori_loop(0, A * first, last, 0)

    for k in (chunks - 2, chunks - 1):
        for copy in [reduce_c(k)] + reduce_1(k) + reduce_2(k):
            copy.wait_send()
        reduce_z_sent(k)

    def drained(ref, sem, dev):
        remote(ref, ref, sem, sem, dev).wait_send()

    plain, turned = slice(0, LAST_GATHERED[0]), slice(LAST_GATHERED[0], chunks)
    drained(wg.at[plain, :, : A - 1, b, y, c], gz_s.at[0], to_c)
    drained(wg.at[turned, :, : A - 1, :, :, c], gz_s.at[1], to_c)
    for d, dev in to_b:
        drained(wg.at[plain, 0, :, b, y, c], g1a_s.at[0, d - 1], dev)
        drained(wg.at[plain, 1, :, b, :, c], g2b_s.at[0, d - 1], dev)
        drained(wg.at[turned, 0, a, b, y, c], g1a_s.at[1, d - 1], dev)
        drained(wg.at[turned, 1, a, b, :, c], g2b_s.at[1, d - 1], dev)
    for d, dev in to_y:
        drained(wg.at[plain, 1, :, b, y, c], g1b_s.at[0, d - 1], dev)
        drained(wg.at[plain, 0, :, :, y, c], g2a_s.at[0, d - 1], dev)
        drained(wg.at[turned, 1, a, b, y, c], g1b_s.at[1, d - 1], dev)
        drained(wg.at[turned, 0, a, :, y, c], g2a_s.at[1, d - 1], dev)
    drained(wg.at[:, :, :, :, :, c], gc_s.at[0], to_c)
    drained(bb.at[: A - 1, b, y, c], bz_s.at[0], to_c)
    for d, dev in to_b:
        bias_1(d, dev, True).wait_send()
    for d, dev in to_y:
        bias_2(d, dev, True).wait_send()
    bias_c(True).wait_send()
    for copy in [bred_c()] + bred_1() + bred_2():
        copy.wait_send()
    drained(brz, dz_s.at[0], to_c)


def per_device(dims, features, cotangent, neighbours, segments, live, weight, bias):
    A, B, Y, C = dims
    batches, local, D = features.shape
    rows = weight.shape[0]
    N = batches * local
    N_l = LATE * local
    N_e = N - N_l
    chunks = D // CHUNK
    groups = A * B * Y
    wide = D // A
    neighbours = jnp.swapaxes(neighbours, 1, 2)
    any_spec = pl.BlockSpec(memory_space=pl.ANY)
    vmem, dma = pltpu.VMEM, pltpu.SemaphoreType.DMA
    scratch = [
        vmem((N_e, D), BF16),
        vmem((N_l, D), BF16),
        vmem((N_e // SLOT, SLOT, SLOT), BF16),
        vmem((N_e, SLOT), F32),
        vmem((groups, C, rows, N), BF16),
        vmem((2, batches, local, CHUNK), BF16),
        vmem((SLOTS, A, B, Y, rows, CHUNK), F32),
        vmem((2, A, B, Y, rows, CHUNK), BF16),
        vmem((chunks, A, B, Y, rows, CHUNK), BF16),
        vmem((2, Y - 1, A, B, rows, LANES), BF16),
        vmem((2, B - 1, A, Y, rows, LANES), BF16),
        vmem((2, B - 1, A, rows, LANES), BF16),
        vmem((2, Y - 1, A, rows, LANES), BF16),
        vmem((2, A - 1, rows, CHUNK), BF16),
        vmem((chunks, Y - 1, A, B, rows, LANES), BF16),
        vmem((chunks, B - 1, A, Y, rows, LANES), BF16),
        vmem((chunks, B - 1, A, rows, LANES), BF16),
        vmem((chunks, Y - 1, A, rows, LANES), BF16),
        vmem((chunks, A - 1, rows, CHUNK), BF16),
        vmem(neighbours.shape, jnp.int32),
        vmem(segments.shape, jnp.int32),
        vmem(live.shape, jnp.int32),
        vmem((A, B, Y, C, 8, LANES), F32),
        vmem((D // LANES, 8, LANES), F32),
        vmem((8, D), F32),
        vmem((A, B, Y, C, 8, LANES), F32),
        vmem((A, B, Y, 8, LANES), F32),
        vmem((A, B, Y, 8, LANES), F32),
        vmem((Y - 1, A, B, 8, LANES), F32),
        vmem((B - 1, A, 8, LANES), F32),
        vmem((A - 1, 8, LANES), F32),
        dma((4 + batches,)),
        dma((2,)),
    ]
    for sent, received in (
        ((2,), (chunks,)),
        ((2, B - 1), (chunks, B - 1)),
        ((2, Y - 1), (chunks, Y - 1)),
        ((2, Y - 1), (chunks, Y - 1)),
        ((2, B - 1), (chunks, B - 1)),
        ((1,), (chunks,)),
        ((2,), (chunks,)),
        ((2, Y - 1), (chunks, Y - 1)),
        ((2, B - 1), (chunks, B - 1)),
        ((2, B - 1), (chunks, B - 1)),
        ((2, Y - 1), (chunks, Y - 1)),
        ((2,), (chunks,)),
        ((1,), (1,)),
        ((B - 1,), (B - 1,)),
        ((Y - 1,), (Y - 1,)),
        ((1,), (1,)),
        ((1,), (1,)),
        ((Y - 1,), (Y - 1,)),
        ((B - 1,), (B - 1,)),
        ((1,), (1,)),
    ):
        scratch += [dma(sent), dma(received)]
    vmem_spec = pl.BlockSpec(memory_space=pltpu.VMEM)
    kept = [
        vmem((chunks, batches, local, CHUNK), BF16),
        vmem((chunks, 2, A, B, Y, C, rows, LANES), BF16),
        vmem((N_l, D), BF16),
        vmem((N_e, D), BF16),
        vmem((N_l // SLOT, SLOT, SLOT), BF16),
        vmem((N_l, SLOT), F32),
        vmem((rows, D), F32),
        vmem((1, rows), F32),
    ]
    kept_arrays = pl.pallas_call(
        functools.partial(kernel, dims),
        out_shape=kept,
        in_specs=[any_spec] * 6 + [vmem_spec],
        out_specs=[vmem_spec] * len(kept),
        scratch_shapes=scratch,
        compiler_params=pltpu.CompilerParams(
            collective_id=0, has_side_effects=True, vmem_limit_bytes=39 * 2**20
        ),
        cost_estimate=pl.CostEstimate(
            flops=6 * N * D * D, bytes_accessed=8 * N * D, transcendentals=N * D
        ),
    )(features, cotangent, neighbours, segments, live, weight, bias.reshape(1, rows))
    act, fgrad, wgrad, bgrad = pl.pallas_call(
        functools.partial(finish, dims),
        out_shape=[
            jax.ShapeDtypeStruct(features.shape, BF16),
            jax.ShapeDtypeStruct(features.shape, BF16),
            jax.ShapeDtypeStruct(weight.shape, F32),
            jax.ShapeDtypeStruct((1, rows), F32),
        ],
        in_specs=[vmem_spec] * len(kept),
        out_specs=[any_spec] * 3 + [vmem_spec],
        scratch_shapes=[
            vmem((A * LATE, local, wide), BF16),
            dma((1,)), dma((batches - LATE,)), dma((A * LATE,)), dma((1,)),
        ],
        compiler_params=pltpu.CompilerParams(vmem_limit_bytes=8 * 2**20),
    )(
        *[pltpu.with_memory_space_constraint(x, pltpu.VMEM) for x in kept_arrays],
    )
    return act, fgrad, wgrad, bgrad.reshape(rows)


def solution(mesh):
    both = ("dp", "rep")
    dims = split_axes(mesh.shape["dp"], mesh.shape["rep"])
    return jax.shard_map(
        functools.partial(per_device, dims),
        mesh=mesh,
        in_specs=(
            P(None, both, None), P(None, both, None), P(None, both, None),
            P(None, both), P(None, both), P(both, None), P(both),
        ),
        out_specs=(P(None, both, None), P(None, both, None), P(both, None), P(both)),
        check_vma=False,
    )
```

```python
import functools

import jax
import jax.numpy as jnp
from jax import lax
from jax.experimental import pallas as pl
from jax.experimental.pallas import tpu as pltpu
from jax.sharding import PartitionSpec as P

SLOT = 128
LANES = 128
CHUNK = 256
MESH = pl.DeviceIdType.MESH
F32, BF16 = jnp.float32, jnp.bfloat16
ENHANCE = 1.0
LATE = 1
SLOTS, RECEIVED = 7, 6
LAST_GATHERED = (6, 7)


def split_axes(dp, rep):
    b = 2 ** ((dp.bit_length() - 1) // 2)
    return dp // b, b, rep // 2, 2


def feature_tile(dims, wg, gp, adj_t, scale, local, n, m):
    A, B, Y, C = dims
    chunks, rows = wg.shape[0], wg.shape[-2]
    wide = B * Y * C * rows
    slots = local // SLOT
    base = m * local if isinstance(m, int) else pl.multiple_of(m * local, local)
    w = jnp.concatenate([wg[k, h, n].reshape(wide, LANES) for k in range(chunks) for h in range(2)], axis=1)
    grad = lax.dot_general(gp[pl.ds(base, local), :], w, (((1,), (1,)), ((), ())), preferred_element_type=F32)
    grad = grad * jnp.concatenate([scale[pl.ds(base, local), :]] * (wide // LANES), axis=1)
    high = grad.astype(BF16)
    low = (grad - high.astype(F32)).astype(BF16)
    tiles = []
    for q in range(slots):
        left = adj_t[m * slots + q]
        part = slice(q * SLOT, (q + 1) * SLOT)
        right = jnp.concatenate([high[part], low[part]], axis=0)
        out = jnp.dot(jnp.concatenate([left, left], axis=1), right, preferred_element_type=F32)
        tiles.append(out.astype(BF16))
    return jnp.concatenate(tiles, axis=0)


def finish(
    dims, act, wg, gp, done, adj_t, scale, wout, bgrad_in, act_out, fgrad_out, wgrad_out, bgrad_out,
    fout, act_sem, done_sem, fout_sem, wout_sem,
):
    batches, local, D = fgrad_out.shape
    blocks, wide, early = dims[0], D // dims[0], batches - LATE

    def store(i):
        n, m = lax.div(i, LATE), early + lax.rem(i, LATE)
        cols = pl.ds(pl.multiple_of(n * wide, wide), wide)
        return pltpu.make_async_copy(fout.at[i], fgrad_out.at[m, :, cols], fout_sem.at[i])

    kept = [pltpu.make_async_copy(wout, wgrad_out, wout_sem.at[0])]
    for m in range(early):
        kept.append(pltpu.make_async_copy(done.at[pl.ds(m * local, local)], fgrad_out.at[m], done_sem.at[m]))
    for copy in kept:
        copy.start()
    for k in range(act.shape[0]):
        pltpu.make_async_copy(act.at[k], act_out.at[:, :, pl.ds(k * CHUNK, CHUNK)], act_sem.at[0]).start()
    bgrad_out[...] = bgrad_in[...]

    def step(i, carry):
        fout[i] = feature_tile(dims, wg, gp, adj_t, scale, local, lax.div(i, LATE), lax.rem(i, LATE))
        store(i).start()
        return carry

    lax.fori_loop(0, blocks * LATE, step, 0)
    for i in range(blocks * LATE):
        store(i).wait()
    pltpu.make_async_copy(act, act, act_sem.at[0]).wait()
    for copy in kept:
        copy.wait()


def kernel(
    dims, feat, cot, nbr, seg, live, weight, bias, act, wg, gp_l, pool_e, adj_l, scale_l, wout, bgrad_out,
    gp_e, pool_l, adj_e, scale_e, pool_t, ct, acc, csend, crecv, s1a, s1b, s2a, s2b, sz, r1a, r1b, r2a, r2b, rz,
    nbuf, sbuf, lbuf, bb, brow, bacc, bt, bsum, brc, br1, br2, brz,
    in_sem, ct_sem,
    gz_s, gz_r, g1a_s, g1a_r, g1b_s, g1b_r, g2a_s, g2a_r, g2b_s, g2b_r, gc_s, gc_r,
    rc_s, rc_r, p1a_s, p1a_r, p1b_s, p1b_r, p2a_s, p2a_r, p2b_s, p2b_r, pz_s, pz_r,
    bz_s, bz_r, b1_s, b1_r, b2_s, b2_r, bc_s, bc_r, dc_s, dc_r, d1_s, d1_r, d2_s, d2_r, dz_s, dz_r,
):
    A, B, Y, C = dims
    batches, local, D = feat.shape
    rows = weight.shape[0]
    slots = local // SLOT
    N = batches * local
    chunks = D // CHUNK
    groups = A * B * Y
    plane = groups * rows
    first = batches - LATE
    wide = D // A

    dp, rep = lax.axis_index("dp"), lax.axis_index("rep")
    a, b, y, c = lax.div(dp, B), lax.rem(dp, B), lax.div(rep, C), lax.rem(rep, C)
    oc = 1 - c

    def device(a_, b_, y_, c_):
        return (a_ * B + b_, y_ * C + c_)

    def columns(k):
        return pl.ds(k * CHUNK if isinstance(k, int) else pl.multiple_of(k * CHUNK, CHUNK), CHUNK)

    def of(m, ref_e, ref_l):
        return (ref_e, m) if m < first else (ref_l, m - first)

    def rows_of(m, ref_e, ref_l):
        ref, at = of(m, ref_e, ref_l)
        return ref.at[pl.ds(at * local, local)]

    def up(v, d, n):
        return lax.rem(v + d, n)

    def down(v, d, n):
        return lax.rem(v + n - d, n)

    to_a = [(d, device(up(a, d, A), b, y, c)) for d in range(1, A)]
    to_b = [(d, device(a, up(b, d, B), y, c)) for d in range(1, B)]
    to_y = [(d, device(a, b, up(y, d, Y), c)) for d in range(1, Y)]
    to_c = device(a, b, y, oc)

    def remote(src, dst, ssem, rsem, dev):
        return pltpu.make_async_remote_copy(
            src_ref=src, dst_ref=dst, send_sem=ssem, recv_sem=rsem, device_id=dev, device_id_type=MESH
        )

    weight_loads = [
        pltpu.make_async_copy(
            weight.at[:, pl.ds((2 * k + h) * LANES, LANES)], wg.at[k, h, a, b, y, c], in_sem.at[0]
        )
        for k in range(chunks)
        for h in range(2)
    ]
    side_loads = [
        pltpu.make_async_copy(nbr, nbuf, in_sem.at[1]),
        pltpu.make_async_copy(seg, sbuf, in_sem.at[2]),
        pltpu.make_async_copy(live, lbuf, in_sem.at[3]),
    ]
    feat_loads = [
        pltpu.make_async_copy(feat.at[m], rows_of(m, gp_e, gp_l), in_sem.at[4 + m]) for m in range(batches)
    ]
    for copy in weight_loads:
        copy.start()
    for copy in side_loads:
        copy.start()
    for copy in feat_loads:
        copy.start()

    barrier = pltpu.get_barrier_semaphore()
    partners = [dev for _, dev in to_a + to_b + to_y] + [to_c]
    for dev in partners:
        pl.semaphore_signal(barrier, inc=1, device_id=dev, device_id_type=MESH)

    def cot_load(k):
        return pltpu.make_async_copy(cot.at[:, :, columns(k)], ct.at[k % 2], ct_sem.at[k % 2])

    pl.semaphore_wait(barrier, len(partners))

    def gather_z(k, d, dev):
        ref = wg.at[k, :, a, b, y, c]
        return remote(ref, ref, gz_s.at[0], gz_r.at[k], dev)

    def gather_1(k, mine):
        out = []
        for d, dev in to_b:
            ref = wg.at[k, 0, :, b if mine else down(b, d, B), y, c]
            out.append(remote(ref, ref, g1a_s.at[0, d - 1], g1a_r.at[k, d - 1], dev))
        for d, dev in to_y:
            ref = wg.at[k, 1, :, b, y if mine else down(y, d, Y), c]
            out.append(remote(ref, ref, g1b_s.at[0, d - 1], g1b_r.at[k, d - 1], dev))
        return out

    def gather_2(k, mine):
        out = []
        for d, dev in to_y:
            ref = wg.at[k, 0, :, :, y if mine else down(y, d, Y), c]
            out.append(remote(ref, ref, g2a_s.at[0, d - 1], g2a_r.at[k, d - 1], dev))
        for d, dev in to_b:
            ref = wg.at[k, 1, :, b if mine else down(b, d, B), :, c]
            out.append(remote(ref, ref, g2b_s.at[0, d - 1], g2b_r.at[k, d - 1], dev))
        return out

    def turned_1(k, mine):
        out = []
        for d, dev in to_b:
            ref = wg.at[k, 0, a, b if mine else down(b, d, B), y, c]
            out.append(remote(ref, ref, g1a_s.at[1, d - 1], g1a_r.at[k, d - 1], dev))
        for d, dev in to_y:
            ref = wg.at[k, 1, a, b, y if mine else down(y, d, Y), c]
            out.append(remote(ref, ref, g1b_s.at[1, d - 1], g1b_r.at[k, d - 1], dev))
        return out

    def turned_2(k, mine):
        out = []
        for d, dev in to_y:
            ref = wg.at[k, 0, a, :, y if mine else down(y, d, Y), c]
            out.append(remote(ref, ref, g2a_s.at[1, d - 1], g2a_r.at[k, d - 1], dev))
        for d, dev in to_b:
            ref = wg.at[k, 1, a, b if mine else down(b, d, B), :, c]
            out.append(remote(ref, ref, g2b_s.at[1, d - 1], g2b_r.at[k, d - 1], dev))
        return out

    def turned_z(k):
        out = []
        ref = wg.at[k, :, a, :, :, c]
        for d, dev in to_a:
            out.append(remote(ref, ref, gz_s.at[1], gz_r.at[k], dev))
        return out

    def gather_c(k, mine):
        ref = wg.at[k, :, :, :, :, c if mine else oc]
        return remote(ref, ref, gc_s.at[0], gc_r.at[k], to_c)

    def region(fn):
        pl.when(dp >= 0)(fn)

    def bias_z(d, dev):
        ref = bb.at[a, b, y, c]
        return remote(ref, ref, bz_s.at[0], bz_r.at[0], dev)

    def bias_1(d, dev, mine):
        ref = bb.at[:, b if mine else down(b, d, B), y, c]
        return remote(ref, ref, b1_s.at[d - 1], b1_r.at[d - 1], dev)

    def bias_2(d, dev, mine):
        ref = bb.at[:, :, y if mine else down(y, d, Y), c]
        return remote(ref, ref, b2_s.at[d - 1], b2_r.at[d - 1], dev)

    def bias_c(mine):
        ref = bb.at[:, :, :, c if mine else oc]
        return remote(ref, ref, bc_s.at[0], bc_r.at[0], to_c)

    def ag1(k):
        every = wg.at[k, :, : A - 1, b, y, c]
        remote(every, every, gz_s.at[0], gz_r.at[k], to_c).wait_recv()
        for copy in gather_1(k, True):
            copy.start()

    def ag2(k):
        for copy in gather_1(k, False):
            copy.wait_recv()
        for copy in gather_2(k, True):
            copy.start()

    def ag3(k):
        for copy in gather_2(k, False):
            copy.wait_recv()
        gather_c(k, True).start()

    def at1(k):
        for copy in turned_1(k, True):
            copy.start()

    def at2(k):
        for copy in turned_1(k, False):
            copy.wait_recv()
        for copy in turned_2(k, True):
            copy.start()

    def atz(k):
        for copy in turned_2(k, False):
            copy.wait_recv()
        for copy in turned_z(k):
            copy.start()

    def at3(k):
        every = wg.at[k, :, : A - 1, :, :, c]
        remote(every, every, gz_s.at[1], gz_r.at[k], to_c).wait_recv()
        gather_c(k, True).start()

    def bias_ag1():
        every = bb.at[: A - 1, b, y, c]
        remote(every, every, bz_s.at[0], bz_r.at[0], to_c).wait_recv()
        for d, dev in to_b:
            bias_1(d, dev, True).start()

    def bias_ag2():
        for d, dev in to_b:
            bias_1(d, dev, False).wait_recv()
        for d, dev in to_y:
            bias_2(d, dev, True).start()

    def bias_ag3():
        for d, dev in to_y:
            bias_2(d, dev, False).wait_recv()
        bias_c(True).start()

    def agz(k):
        for d, dev in to_a:
            gather_z(k, d, dev).start()

    def bias_agz():
        spread = lax.rem(lax.broadcasted_iota(jnp.int32, (rows, LANES), 1), rows)
        spread = (spread == lax.broadcasted_iota(jnp.int32, (rows, LANES), 0)).astype(F32).astype(BF16)
        own_bias = jnp.broadcast_to(bias[...], (8, rows))
        bb[a, b, y, c] = jnp.dot(own_bias, spread, preferred_element_type=F32)
        for d, dev in to_a:
            bias_z(d, dev).start()

    pltpu.make_async_copy(weight, weight, in_sem.at[0]).wait()
    bias_agz()
    agz(0)
    for k in LAST_GATHERED:
        at1(k)

    for copy in side_loads:
        copy.wait()
    cot_load(0).start()
    bacc[...] = jnp.zeros_like(bacc)

    def pooling(m, q):
        here = pl.multiple_of(q * SLOT, SLOT)
        flat = pl.multiple_of((m * slots + q) * SLOT, SLOT)
        listed = nbuf[m, :, pl.ds(here, SLOT)].astype(F32).astype(BF16)
        lane = lax.broadcasted_iota(jnp.int32, (SLOT, SLOT), 1)
        sub = lax.broadcasted_iota(jnp.int32, (SLOT, SLOT), 0)
        position = sub.astype(F32).astype(BF16)
        counted = jnp.zeros((SLOT, SLOT), BF16)
        for j in range(listed.shape[0]):
            counted = counted + jnp.where(listed[j : j + 1, :] == position, jnp.bfloat16(1), jnp.bfloat16(0))
        counted = counted.astype(F32).T
        ids, alive = sbuf[m : m + 1, pl.ds(here, SLOT)], lbuf[m : m + 1, pl.ds(here, SLOT)]
        along = jnp.where(alive > 0, ids, -1)
        down_ = jnp.broadcast_to(jnp.where(alive > 0, ids, -2), (SLOT, SLOT)).T
        adjacency = jnp.where(down_ == along, counted, 0.0)
        degree = jnp.sum(adjacency, axis=1, keepdims=True)
        factor = jnp.where(down_ >= 0, 1.0 / (degree + 1.0), 0.0)
        adjacency = jnp.where(lane == sub, (1.0 + ENHANCE) * (adjacency + 1.0), adjacency)
        adj, at = of(m, adj_e, adj_l)
        adj[at * slots + q] = adjacency.T.astype(BF16)
        rows_of(m, scale_e, scale_l)[pl.ds(here, SLOT), :] = factor
        block = rows_of(m, gp_e, gp_l)[pl.ds(here, SLOT), :]
        pooled = jnp.dot(adjacency.astype(BF16), block, preferred_element_type=F32)
        pooled = (pooled * jnp.concatenate([factor] * (D // SLOT), axis=1)).astype(BF16)
        rows_of(m, pool_e, pool_l)[pl.ds(here, SLOT), :] = pooled
        pool_t[:, :, :, pl.ds(flat, SLOT)] = pooled.T.reshape(groups, C, rows, SLOT)

    early = {
        2: [lambda: agz(1)],
        4: [bias_ag1, lambda: ag1(0)],
        6: [lambda: at2(6), lambda: at2(7), lambda: agz(2)],
        10: [bias_ag2, lambda: ag2(0), lambda: ag1(1), lambda: agz(3)],
    }
    for m in range(batches):
        feat_loads[m].wait()

        def step(q, carry, m=m):
            pooling(m, q)
            for at, events in early.items():
                if m * slots <= at < (m + 1) * slots:

                    @pl.when(q == at - m * slots)
                    def _(events=events):
                        for event in events:
                            event()

            return carry

        lax.fori_loop(0, slots, step, 0)

    agz(4)
    ag1(2)
    bias_ag3()
    ag3(0)
    agz(5)

    bias_c(False).wait_recv()
    tiles = bb[...].reshape(groups * C, 8, LANES)
    per = LANES // rows
    owner = lax.div(lax.broadcasted_iota(jnp.int32, (1, LANES), 1), rows)
    for j in range(D // LANES):
        row = jnp.zeros((1, LANES), F32)
        for p in range(per):
            row = jnp.where(owner == p, tiles[j * per + p, 0:1, :], row)
        brow[j] = jnp.broadcast_to(row, (8, LANES))

    def reduce_c(k):
        return remote(csend.at[k % 2], crecv.at[k % RECEIVED], rc_s.at[k % 2], rc_r.at[k], to_c)

    def reduce_1(k):
        e = k % 2
        out_a = [
            remote(s1a.at[e, d - 1], r1a.at[k, d - 1], p1a_s.at[e, d - 1], p1a_r.at[k, d - 1], dev) for d, dev in to_y
        ]
        out_b = [
            remote(s1b.at[e, d - 1], r1b.at[k, d - 1], p1b_s.at[e, d - 1], p1b_r.at[k, d - 1], dev) for d, dev in to_b
        ]
        return out_a + out_b

    def reduce_2(k):
        e = k % 2
        out_a = [
            remote(s2a.at[e, d - 1], r2a.at[k, d - 1], p2a_s.at[e, d - 1], p2a_r.at[k, d - 1], dev) for d, dev in to_b
        ]
        out_b = [
            remote(s2b.at[e, d - 1], r2b.at[k, d - 1], p2b_s.at[e, d - 1], p2b_r.at[k, d - 1], dev) for d, dev in to_y
        ]
        return out_a + out_b

    def reduce_z(k):
        e = k % 2
        return [remote(sz.at[e, d - 1], rz.at[k, d - 1], pz_s.at[e], pz_r.at[k], dev) for d, dev in to_a]

    def reduce_z_sent(k):
        remote(sz.at[k % 2], rz.at[k], pz_s.at[k % 2], pz_r.at[k], to_c).wait_send()

    def ago(k, n, copies):
        if k >= n:
            for copy in copies(k - n):
                copy.wait_send()

    lo, hi = slice(0, LANES), slice(LANES, CHUNK)

    def rs1(k):
        t, e = k % SLOTS, k % 2
        reduce_c(k).wait_recv()
        ago(k, 2, reduce_1)
        for d, _ in to_y:
            v = up(y, d, Y)
            s1a[e, d - 1] = (acc[t, :, :, v, :, lo] + crecv[k % RECEIVED, :, :, v, :, lo].astype(F32)).astype(BF16)
        for d, _ in to_b:
            v = up(b, d, B)
            s1b[e, d - 1] = (acc[t, :, v, :, :, hi] + crecv[k % RECEIVED, :, v, :, :, hi].astype(F32)).astype(BF16)
        for copy in reduce_1(k):
            copy.start()
        acc[t, :, :, y, :, lo] = acc[t, :, :, y, :, lo] + crecv[k % RECEIVED, :, :, y, :, lo].astype(F32)
        acc[t, :, b, :, :, hi] = acc[t, :, b, :, :, hi] + crecv[k % RECEIVED, :, b, :, :, hi].astype(F32)

    def rs2(k):
        t, e = k % SLOTS, k % 2
        for copy in reduce_1(k):
            copy.wait_recv()
        ago(k, 2, reduce_2)

        def total_a(v):
            out = acc[t, :, v, y, :, lo]
            for d, _ in to_y:
                out = out + r1a[k, d - 1, :, v].astype(F32)
            return out

        def total_b(v):
            out = acc[t, :, b, v, :, hi]
            for d, _ in to_b:
                out = out + r1b[k, d - 1, :, v].astype(F32)
            return out

        for d, _ in to_b:
            s2a[e, d - 1] = total_a(up(b, d, B)).astype(BF16)
        for d, _ in to_y:
            s2b[e, d - 1] = total_b(up(y, d, Y)).astype(BF16)
        for copy in reduce_2(k):
            copy.start()
        acc[t, :, b, y, :, lo] = total_a(b)
        acc[t, :, b, y, :, hi] = total_b(y)

    def rs3(k):
        t, e = k % SLOTS, k % 2
        for copy in reduce_2(k):
            copy.wait_recv()
        if k >= 2:
            reduce_z_sent(k - 2)

        def total(v):
            left, right = acc[t, v, b, y, :, lo], acc[t, v, b, y, :, hi]
            for d, _ in to_b:
                left = left + r2a[k, d - 1, v].astype(F32)
            for d, _ in to_y:
                right = right + r2b[k, d - 1, v].astype(F32)
            return jnp.concatenate([left, right], axis=1)

        for d, _ in to_a:
            sz[e, d - 1] = total(up(a, d, A)).astype(BF16)
        for copy in reduce_z(k):
            copy.start()
        acc[t, a, b, y] = total(a)

    def rs4(k):
        t = k % SLOTS
        remote(sz.at[k % 2], rz.at[k], pz_s.at[k % 2], pz_r.at[k], to_c).wait_recv()
        out = acc[t, a, b, y]
        for d, _ in to_a:
            out = out + rz[k, d - 1].astype(F32)
        wout[:, columns(k)] = out

    def bred_c():
        return remote(bt.at[:, :, :, oc], brc, dc_s.at[0], dc_r.at[0], to_c)

    def bred_1():
        return [remote(bsum.at[:, :, up(y, d, Y)], br1.at[d - 1], d1_s.at[d - 1], d1_r.at[d - 1], dev) for d, dev in to_y]

    def bred_2():
        return [remote(bsum.at[:, up(b, d, B), y], br2.at[d - 1], d2_s.at[d - 1], d2_r.at[d - 1], dev) for d, dev in to_b]

    def bred_z():
        return [remote(bsum.at[up(a, d, A), b, y], brz.at[d - 1], dz_s.at[0], dz_r.at[0], dev) for d, dev in to_a]

    def bias_rs0():
        for a_ in range(A):
            for b_ in range(B):
                for y_ in range(Y):
                    for c_ in range(C):
                        block = (((a_ * B + b_) * Y + y_) * C + c_) * rows // LANES
                        bt[a_, b_, y_, c_] = bacc[:, block * LANES : (block + 1) * LANES]
        bred_c().start()

    def bias_rs1():
        bred_c().wait_recv()
        bsum[...] = bt[:, :, :, c] + brc[...]
        for copy in bred_1():
            copy.start()

    def bias_rs2():
        for copy in bred_1():
            copy.wait_recv()
        for d, _ in to_y:
            bsum[:, :, y] = bsum[:, :, y] + br1[d - 1]
        for copy in bred_2():
            copy.start()

    def bias_rs3():
        for copy in bred_2():
            copy.wait_recv()
        for d, _ in to_b:
            bsum[:, b, y] = bsum[:, b, y] + br2[d - 1]
        for copy in bred_z():
            copy.start()

    def bias_rs4():
        remote(brz, brz, dz_s.at[0], dz_r.at[0], to_c).wait_recv()
        out = bsum[a, b, y]
        for d, _ in to_a:
            out = out + brz[d - 1]
        out = jnp.sum(out, axis=0, keepdims=True)
        place = lax.rem((dp * (Y * C) + rep) * rows, LANES)
        mine = jnp.zeros((1, rows), F32)
        for p in range(per):
            mine = jnp.where(place == p * rows, out[:, p * rows : (p + 1) * rows], mine)
        bgrad_out[...] = mine

    def forward(k, parts):
        e = k % 2
        w = jnp.concatenate([wg[k, h].reshape(D, LANES) for h in range(2)], axis=1)
        offset = jnp.concatenate([brow[2 * k + h][0:1] for h in range(2)], axis=1)
        sums = jnp.zeros((8, CHUNK), F32)
        for m in parts:
            preact = jnp.dot(rows_of(m, pool_e, pool_l)[...], w, preferred_element_type=F32) + offset
            squash = jax.nn.sigmoid(preact)
            active = preact * squash
            act[k, m] = active.astype(BF16)
            grad = (ct[e, m].astype(F32) * (squash + active * (1.0 - squash))).astype(BF16)
            rows_of(m, gp_e, gp_l)[:, columns(k)] = grad
            sums = sums + jnp.sum(grad.astype(F32).reshape(local // 8, 8, CHUNK), axis=0)
        bacc[:, columns(k)] = sums if parts[0] == 0 else bacc[:, columns(k)] + sums

    def weight_term(k, which):
        left = pool_t[:, which].reshape(plane, N)
        right = jnp.concatenate([gp_e[:, columns(k)], gp_l[:, columns(k)]], axis=0)
        return jnp.dot(left, right, preferred_element_type=F32).reshape(A, B, Y, rows, CHUNK)

    def forward_region(k):
        gather_c(k, False).wait_recv()
        cot_load(k).wait()
        if not isinstance(k, int) or k + 1 < chunks:
            cot_load(k + 1).start()

    def weight_region(k):
        if k >= 2:
            reduce_c(k - 2).wait_send()

    def weight_other(k):
        csend[k % 2] = weight_term(k, oc).astype(BF16)

    def weight_own(k):
        acc[k % SLOTS] = weight_term(k, c)

    whole = list(range(batches))

    regions = [(0, None), (None, 0), (1, None), (None, 1), (2, None)]
    regions += [(k, k - 1) for k in range(3, chunks - 1)]
    regions += [(None, chunks - 2), (chunks - 1, None), (None, chunks - 1)]
    plan = [
        (lambda _: bias_rs0(), {0: 11}),
        (lambda _: bias_rs1(), {0: 12}),
        (ag2, {1: 0, 2: 1, 3: 2, 4: 3, 5: 5}),
        (ag1, {3: 0, 4: 1, 5: 3}),
        (ag3, {1: 1, 2: 3, 3: 4, 4: 5, 5: 6}),
        (at3, {6: 7, 7: 8}),
        (atz, {6: 0, 7: 4}),
        (rs4, {0: 10, 1: 12}),
        (rs3, {0: 8.5, 1: 9, 2: 10, 3: 11, 4: 12}),
        (rs2, {0: 7, 1: 7.5, 2: 8, 3: 9, 4: 10, 5: 12}),
        (rs1, {0: 5.5, 1: 6, 2: 6.5, 3: 7, 4: 8, 5: 9, 6: 10}),
    ]

    def ahead_of(at):
        return [(stage, k) for stage, when in plan for k, ahead in when.items() if ahead == at]

    def opening(j, carry):
        for place in range(2):
            for step in range(2):
                for stage, k in ahead_of(2 * step + place):
                    pl.when(j == step)(functools.partial(stage, k))
            if place == 0:
                forward_region(j)
                region(lambda: forward(j, whole))
            else:
                region(lambda: weight_other(j))
                reduce_c(j).start()
                region(lambda: weight_own(j))
        return carry

    lax.fori_loop(0, 2, opening, 0)
    for at, (f, w) in enumerate(regions):
        if at < 4:
            continue
        for stage, k in ahead_of(at):
            stage(k)
        if f is not None:
            forward_region(f)
        if w is not None:
            weight_region(w)
        merged = f is not None and w is not None

        @region
        def _(f=f, w=w, merged=merged):
            if f is not None:
                forward(f, whole[:1] if merged else whole)
            if w is not None:
                weight_other(w)

        if w is not None:
            reduce_c(w).start()
            for stage, k in ahead_of(at + 0.5):
                stage(k)

            @region
            def _(f=f, w=w, merged=merged):
                if merged:
                    forward(f, whole[1:])
                weight_own(w)

    for stage, k in ahead_of(len(regions)):
        stage(k)

    def feature_grad(i):
        n, m = lax.div(i, first), lax.rem(i, first)
        part, cols = pl.ds(pl.multiple_of(m * local, local), local), pl.ds(pl.multiple_of(n * wide, wide), wide)
        pool_e[part, cols] = feature_tile(dims, wg, gp_e, adj_e, scale_e, local, n, m)

    late = [
        (rs1, {7: 0}),
        (lambda _: bias_rs2(), {0: 1}),
        (rs2, {6: 1, 7: 3}),
        (rs3, {5: 1, 6: 4, 7: 5}),
        (lambda _: bias_rs3(), {0: 3}),
        (rs4, {2: 0, 3: 1, 4: 3, 5: 5, 6: 7, 7: 7}),
        (lambda _: bias_rs4(), {0: 7}),
    ]

    def last(i, carry):
        pl.when(i >= 0)(lambda: feature_grad(i))
        for stage, when in late:
            for k, at in when.items():
                pl.when(i == at)(functools.partial(stage, k))
        return carry

    lax.fori_loop(0, A * first, last, 0)

    for k in (chunks - 2, chunks - 1):
        for copy in [reduce_c(k)] + reduce_1(k) + reduce_2(k):
            copy.wait_send()
        reduce_z_sent(k)

    def drained(ref, sem, dev):
        remote(ref, ref, sem, sem, dev).wait_send()

    plain, turned = slice(0, LAST_GATHERED[0]), slice(LAST_GATHERED[0], chunks)
    drained(wg.at[plain, :, : A - 1, b, y, c], gz_s.at[0], to_c)
    drained(wg.at[turned, :, : A - 1, :, :, c], gz_s.at[1], to_c)
    for d, dev in to_b:
        drained(wg.at[plain, 0, :, b, y, c], g1a_s.at[0, d - 1], dev)
        drained(wg.at[plain, 1, :, b, :, c], g2b_s.at[0, d - 1], dev)
        drained(wg.at[turned, 0, a, b, y, c], g1a_s.at[1, d - 1], dev)
        drained(wg.at[turned, 1, a, b, :, c], g2b_s.at[1, d - 1], dev)
    for d, dev in to_y:
        drained(wg.at[plain, 1, :, b, y, c], g1b_s.at[0, d - 1], dev)
        drained(wg.at[plain, 0, :, :, y, c], g2a_s.at[0, d - 1], dev)
        drained(wg.at[turned, 1, a, b, y, c], g1b_s.at[1, d - 1], dev)
        drained(wg.at[turned, 0, a, :, y, c], g2a_s.at[1, d - 1], dev)
    drained(wg.at[:, :, :, :, :, c], gc_s.at[0], to_c)
    drained(bb.at[: A - 1, b, y, c], bz_s.at[0], to_c)
    for d, dev in to_b:
        bias_1(d, dev, True).wait_send()
    for d, dev in to_y:
        bias_2(d, dev, True).wait_send()
    bias_c(True).wait_send()
    for copy in [bred_c()] + bred_1() + bred_2():
        copy.wait_send()
    drained(brz, dz_s.at[0], to_c)


def per_device(dims, features, cotangent, neighbours, segments, live, weight, bias):
    A, B, Y, C = dims
    batches, local, D = features.shape
    rows = weight.shape[0]
    N = batches * local
    N_l = LATE * local
    N_e = N - N_l
    chunks = D // CHUNK
    groups = A * B * Y
    wide = D // A
    neighbours = jnp.swapaxes(neighbours, 1, 2)
    any_spec = pl.BlockSpec(memory_space=pl.ANY)
    vmem, dma = pltpu.VMEM, pltpu.SemaphoreType.DMA
    scratch = [
        vmem((N_e, D), BF16),
        vmem((N_l, D), BF16),
        vmem((N_e // SLOT, SLOT, SLOT), BF16),
        vmem((N_e, SLOT), F32),
        vmem((groups, C, rows, N), BF16),
        vmem((2, batches, local, CHUNK), BF16),
        vmem((SLOTS, A, B, Y, rows, CHUNK), F32),
        vmem((2, A, B, Y, rows, CHUNK), BF16),
        vmem((RECEIVED, A, B, Y, rows, CHUNK), BF16),
        vmem((2, Y - 1, A, B, rows, LANES), BF16),
        vmem((2, B - 1, A, Y, rows, LANES), BF16),
        vmem((2, B - 1, A, rows, LANES), BF16),
        vmem((2, Y - 1, A, rows, LANES), BF16),
        vmem((2, A - 1, rows, CHUNK), BF16),
        vmem((chunks, Y - 1, A, B, rows, LANES), BF16),
        vmem((chunks, B - 1, A, Y, rows, LANES), BF16),
        vmem((chunks, B - 1, A, rows, LANES), BF16),
        vmem((chunks, Y - 1, A, rows, LANES), BF16),
        vmem((chunks, A - 1, rows, CHUNK), BF16),
        vmem(neighbours.shape, jnp.int32),
        vmem(segments.shape, jnp.int32),
        vmem(live.shape, jnp.int32),
        vmem((A, B, Y, C, 8, LANES), F32),
        vmem((D // LANES, 8, LANES), F32),
        vmem((8, D), F32),
        vmem((A, B, Y, C, 8, LANES), F32),
        vmem((A, B, Y, 8, LANES), F32),
        vmem((A, B, Y, 8, LANES), F32),
        vmem((Y - 1, A, B, 8, LANES), F32),
        vmem((B - 1, A, 8, LANES), F32),
        vmem((A - 1, 8, LANES), F32),
        dma((4 + batches,)),
        dma((2,)),
    ]
    for sent, received in (
        ((2,), (chunks,)),
        ((2, B - 1), (chunks, B - 1)),
        ((2, Y - 1), (chunks, Y - 1)),
        ((2, Y - 1), (chunks, Y - 1)),
        ((2, B - 1), (chunks, B - 1)),
        ((1,), (chunks,)),
        ((2,), (chunks,)),
        ((2, Y - 1), (chunks, Y - 1)),
        ((2, B - 1), (chunks, B - 1)),
        ((2, B - 1), (chunks, B - 1)),
        ((2, Y - 1), (chunks, Y - 1)),
        ((2,), (chunks,)),
        ((1,), (1,)),
        ((B - 1,), (B - 1,)),
        ((Y - 1,), (Y - 1,)),
        ((1,), (1,)),
        ((1,), (1,)),
        ((Y - 1,), (Y - 1,)),
        ((B - 1,), (B - 1,)),
        ((1,), (1,)),
    ):
        scratch += [dma(sent), dma(received)]
    vmem_spec = pl.BlockSpec(memory_space=pltpu.VMEM)
    kept = [
        vmem((chunks, batches, local, CHUNK), BF16),
        vmem((chunks, 2, A, B, Y, C, rows, LANES), BF16),
        vmem((N_l, D), BF16),
        vmem((N_e, D), BF16),
        vmem((N_l // SLOT, SLOT, SLOT), BF16),
        vmem((N_l, SLOT), F32),
        vmem((rows, D), F32),
        vmem((1, rows), F32),
    ]
    kept_arrays = pl.pallas_call(
        functools.partial(kernel, dims),
        out_shape=kept,
        in_specs=[any_spec] * 6 + [vmem_spec],
        out_specs=[vmem_spec] * len(kept),
        scratch_shapes=scratch,
        compiler_params=pltpu.CompilerParams(
            collective_id=0, has_side_effects=True, vmem_limit_bytes=39 * 2**20
        ),
        cost_estimate=pl.CostEstimate(
            flops=6 * N * D * D, bytes_accessed=8 * N * D, transcendentals=N * D
        ),
    )(features, cotangent, neighbours, segments, live, weight, bias.reshape(1, rows))
    act, fgrad, wgrad, bgrad = pl.pallas_call(
        functools.partial(finish, dims),
        out_shape=[
            jax.ShapeDtypeStruct(features.shape, BF16),
            jax.ShapeDtypeStruct(features.shape, BF16),
            jax.ShapeDtypeStruct(weight.shape, F32),
            jax.ShapeDtypeStruct((1, rows), F32),
        ],
        in_specs=[vmem_spec] * len(kept),
        out_specs=[any_spec] * 3 + [vmem_spec],
        scratch_shapes=[
            vmem((A * LATE, local, wide), BF16),
            dma((1,)), dma((batches - LATE,)), dma((A * LATE,)), dma((1,)),
        ],
        compiler_params=pltpu.CompilerParams(vmem_limit_bytes=8 * 2**20),
    )(
        *[pltpu.with_memory_space_constraint(x, pltpu.VMEM) for x in kept_arrays],
    )
    return act, fgrad, wgrad, bgrad.reshape(rows)


def solution(mesh):
    both = ("dp", "rep")
    dims = split_axes(mesh.shape["dp"], mesh.shape["rep"])
    return jax.shard_map(
        functools.partial(per_device, dims),
        mesh=mesh,
        in_specs=(
            P(None, both, None), P(None, both, None), P(None, both, None),
            P(None, both), P(None, both), P(both, None), P(both),
        ),
        out_specs=(P(None, both, None), P(None, both, None), P(both, None), P(both)),
        check_vma=False,
    )
```

```python
import functools

import jax
import jax.numpy as jnp
from jax import lax
from jax.experimental import pallas as pl
from jax.experimental.pallas import tpu as pltpu
from jax.sharding import PartitionSpec as P

SLOT = 128
LANES = 128
CHUNK = 256
MESH = pl.DeviceIdType.MESH
F32, BF16 = jnp.float32, jnp.bfloat16
ENHANCE = 1.0
LATE = 1
SLOTS, RECEIVED = 7, 6
LAST_GATHERED = (6, 7)


def split_axes(dp, rep):
    b = 2 ** ((dp.bit_length() - 1) // 2)
    return dp // b, b, rep // 2, 2


def feature_tile(dims, wg, gp, adj_t, scale, local, n, m):
    A, B, Y, C = dims
    chunks, rows = wg.shape[0], wg.shape[-2]
    wide = B * Y * C * rows
    slots = local // SLOT
    base = m * local if isinstance(m, int) else pl.multiple_of(m * local, local)
    w = jnp.concatenate([wg[k, h, n].reshape(wide, LANES) for k in range(chunks) for h in range(2)], axis=1)
    grad = lax.dot_general(gp[pl.ds(base, local), :], w, (((1,), (1,)), ((), ())), preferred_element_type=F32)
    grad = grad * jnp.concatenate([scale[pl.ds(base, local), :]] * (wide // LANES), axis=1)
    high = grad.astype(BF16)
    low = (grad - high.astype(F32)).astype(BF16)
    tiles = []
    for q in range(slots):
        left = adj_t[m * slots + q]
        part = slice(q * SLOT, (q + 1) * SLOT)
        right = jnp.concatenate([high[part], low[part]], axis=0)
        out = jnp.dot(jnp.concatenate([left, left], axis=1), right, preferred_element_type=F32)
        tiles.append(out.astype(BF16))
    return jnp.concatenate(tiles, axis=0)


def finish(
    dims, act, wg, gp, done, adj_t, scale, wout, bgrad_in, act_out, fgrad_out, wgrad_out, bgrad_out,
    fout, act_sem, done_sem, fout_sem, wout_sem,
):
    batches, local, D = fgrad_out.shape
    blocks, wide, early = dims[0], D // dims[0], batches - LATE

    def store(i):
        n, m = lax.div(i, LATE), early + lax.rem(i, LATE)
        cols = pl.ds(pl.multiple_of(n * wide, wide), wide)
        return pltpu.make_async_copy(fout.at[i], fgrad_out.at[m, :, cols], fout_sem.at[i])

    kept = [pltpu.make_async_copy(wout, wgrad_out, wout_sem.at[0])]
    for m in range(early):
        kept.append(pltpu.make_async_copy(done.at[pl.ds(m * local, local)], fgrad_out.at[m], done_sem.at[m]))
    for copy in kept:
        copy.start()
    for k in range(act.shape[0]):
        pltpu.make_async_copy(act.at[k], act_out.at[:, :, pl.ds(k * CHUNK, CHUNK)], act_sem.at[0]).start()
    bgrad_out[...] = bgrad_in[...]

    def step(i, carry):
        fout[i] = feature_tile(dims, wg, gp, adj_t, scale, local, lax.div(i, LATE), lax.rem(i, LATE))
        store(i).start()
        return carry

    lax.fori_loop(0, blocks * LATE, step, 0)
    for i in range(blocks * LATE):
        store(i).wait()
    pltpu.make_async_copy(act, act, act_sem.at[0]).wait()
    for copy in kept:
        copy.wait()


def kernel(
    dims, feat, cot, nbr, seg, live, weight, bias, act, wg, gp_l, pool_e, adj_l, scale_l, wout, bgrad_out,
    gp_e, pool_l, adj_e, scale_e, pool_t, ct, acc, csend, crecv, s1a, s1b, s2a, s2b, sz, r1a, r1b, r2a, r2b, rz,
    nbuf, sbuf, lbuf, bb, brow, bacc, bt, bsum, brc, br1, br2, brz,
    in_sem, ct_sem,
    gz_s, gz_r, g1a_s, g1a_r, g1b_s, g1b_r, g2a_s, g2a_r, g2b_s, g2b_r, gc_s, gc_r,
    rc_s, rc_r, p1a_s, p1a_r, p1b_s, p1b_r, p2a_s, p2a_r, p2b_s, p2b_r, pz_s, pz_r,
    ha_r, hb_r, bz_s, bz_r, b1_s, b1_r, b2_s, b2_r, bc_s, bc_r, dc_s, dc_r, d1_s, d1_r, d2_s, d2_r, dz_s, dz_r,
):
    A, B, Y, C = dims
    batches, local, D = feat.shape
    rows = weight.shape[0]
    slots = local // SLOT
    N = batches * local
    chunks = D // CHUNK
    groups = A * B * Y
    plane = groups * rows
    first = batches - LATE
    wide = D // A

    dp, rep = lax.axis_index("dp"), lax.axis_index("rep")
    a, b, y, c = lax.div(dp, B), lax.rem(dp, B), lax.div(rep, C), lax.rem(rep, C)
    oc = 1 - c

    def device(a_, b_, y_, c_):
        return (a_ * B + b_, y_ * C + c_)

    def columns(k):
        return pl.ds(k * CHUNK if isinstance(k, int) else pl.multiple_of(k * CHUNK, CHUNK), CHUNK)

    def of(m, ref_e, ref_l):
        return (ref_e, m) if m < first else (ref_l, m - first)

    def rows_of(m, ref_e, ref_l):
        ref, at = of(m, ref_e, ref_l)
        return ref.at[pl.ds(at * local, local)]

    def up(v, d, n):
        return lax.rem(v + d, n)

    def down(v, d, n):
        return lax.rem(v + n - d, n)

    to_a = [(d, device(up(a, d, A), b, y, c)) for d in range(1, A)]
    to_b = [(d, device(a, up(b, d, B), y, c)) for d in range(1, B)]
    to_y = [(d, device(a, b, up(y, d, Y), c)) for d in range(1, Y)]
    to_c = device(a, b, y, oc)

    def remote(src, dst, ssem, rsem, dev):
        return pltpu.make_async_remote_copy(
            src_ref=src, dst_ref=dst, send_sem=ssem, recv_sem=rsem, device_id=dev, device_id_type=MESH
        )

    weight_loads = [
        pltpu.make_async_copy(
            weight.at[:, pl.ds((2 * k + h) * LANES, LANES)], wg.at[k, h, a, b, y, c], in_sem.at[0]
        )
        for k in range(chunks)
        for h in range(2)
    ]
    side_loads = [
        pltpu.make_async_copy(nbr, nbuf, in_sem.at[1]),
        pltpu.make_async_copy(seg, sbuf, in_sem.at[2]),
        pltpu.make_async_copy(live, lbuf, in_sem.at[3]),
    ]
    feat_loads = [
        pltpu.make_async_copy(feat.at[m], rows_of(m, gp_e, gp_l), in_sem.at[4 + m]) for m in range(batches)
    ]
    for copy in weight_loads:
        copy.start()
    for copy in side_loads:
        copy.start()
    for copy in feat_loads:
        copy.start()

    barrier = pltpu.get_barrier_semaphore()
    partners = [dev for _, dev in to_a + to_b + to_y] + [to_c]
    for dev in partners:
        pl.semaphore_signal(barrier, inc=1, device_id=dev, device_id_type=MESH)

    def cot_load(k):
        return pltpu.make_async_copy(cot.at[:, :, columns(k)], ct.at[k % 2], ct_sem.at[k % 2])

    pl.semaphore_wait(barrier, len(partners))

    def gather_z(k, d, dev):
        ref = wg.at[k, :, a, b, y, c]
        return remote(ref, ref, gz_s.at[0], gz_r.at[k], dev)

    def gather_1(k, mine):
        out = []
        for d, dev in to_b:
            ref = wg.at[k, 0, :, b if mine else down(b, d, B), y, c]
            out.append(remote(ref, ref, g1a_s.at[0, d - 1], g1a_r.at[k, d - 1], dev))
        for d, dev in to_y:
            ref = wg.at[k, 1, :, b, y if mine else down(y, d, Y), c]
            out.append(remote(ref, ref, g1b_s.at[0, d - 1], g1b_r.at[k, d - 1], dev))
        return out

    def gather_2(k, mine):
        out = []
        for d, dev in to_y:
            ref = wg.at[k, 0, :, :, y if mine else down(y, d, Y), c]
            out.append(remote(ref, ref, g2a_s.at[0, d - 1], g2a_r.at[k, d - 1], dev))
        for d, dev in to_b:
            ref = wg.at[k, 1, :, b if mine else down(b, d, B), :, c]
            out.append(remote(ref, ref, g2b_s.at[0, d - 1], g2b_r.at[k, d - 1], dev))
        return out

    def turned_1(k, mine):
        out = []
        for d, dev in to_b:
            ref = wg.at[k, 0, a, b if mine else down(b, d, B), y, c]
            out.append(remote(ref, ref, g1a_s.at[1, d - 1], g1a_r.at[k, d - 1], dev))
        for d, dev in to_y:
            ref = wg.at[k, 1, a, b, y if mine else down(y, d, Y), c]
            out.append(remote(ref, ref, g1b_s.at[1, d - 1], g1b_r.at[k, d - 1], dev))
        return out

    def turned_2(k, mine):
        out = []
        for d, dev in to_y:
            ref = wg.at[k, 0, a, :, y if mine else down(y, d, Y), c]
            out.append(remote(ref, ref, g2a_s.at[1, d - 1], g2a_r.at[k, d - 1], dev))
        for d, dev in to_b:
            ref = wg.at[k, 1, a, b if mine else down(b, d, B), :, c]
            out.append(remote(ref, ref, g2b_s.at[1, d - 1], g2b_r.at[k, d - 1], dev))
        return out

    def turned_z(k):
        out = []
        ref = wg.at[k, :, a, :, :, c]
        for d, dev in to_a:
            out.append(remote(ref, ref, gz_s.at[1], gz_r.at[k], dev))
        return out

    def half_step(mine):
        out = []
        for d, dev in to_y:
            ref = wg.at[0, 0, :, b, y if mine else down(y, d, Y), c]
            out.append(remote(ref, ref, g2a_s.at[0, d - 1], ha_r.at[d - 1], dev))
        for d, dev in to_b:
            ref = wg.at[0, 1, :, b if mine else down(b, d, B), y, c]
            out.append(remote(ref, ref, g2b_s.at[0, d - 1], hb_r.at[d - 1], dev))
        return out

    def ag2a():
        for copy in half_step(True):
            copy.start()

    def ag2b():
        for copy in gather_1(0, False):
            copy.wait_recv()
        for d, dev in to_y:
            for e in range(1, B):
                ref = wg.at[0, 0, :, down(b, e, B), y, c]
                remote(ref, ref, g2a_s.at[0, d - 1], g2a_r.at[0, d - 1], dev).start()
        for d, dev in to_b:
            for e in range(1, Y):
                ref = wg.at[0, 1, :, b, down(y, e, Y), c]
                remote(ref, ref, g2b_s.at[0, d - 1], g2b_r.at[0, d - 1], dev).start()

    def ag3_first():
        for copy in half_step(False):
            copy.wait_recv()
        for d, dev in to_y:
            ref = wg.at[0, 0, :, : B - 1, y, c]
            remote(ref, ref, g2a_s.at[0, d - 1], g2a_r.at[0, d - 1], dev).wait_recv()
        for d, dev in to_b:
            ref = wg.at[0, 1, :, b, : Y - 1, c]
            remote(ref, ref, g2b_s.at[0, d - 1], g2b_r.at[0, d - 1], dev).wait_recv()
        gather_c(0, True).start()

    def gather_c(k, mine):
        ref = wg.at[k, :, :, :, :, c if mine else oc]
        return remote(ref, ref, gc_s.at[0], gc_r.at[k], to_c)

    def region(fn):
        pl.when(dp >= 0)(fn)

    def bias_z(d, dev):
        ref = bb.at[a, b, y, c]
        return remote(ref, ref, bz_s.at[0], bz_r.at[0], dev)

    def bias_1(d, dev, mine):
        ref = bb.at[:, b if mine else down(b, d, B), y, c]
        return remote(ref, ref, b1_s.at[d - 1], b1_r.at[d - 1], dev)

    def bias_2(d, dev, mine):
        ref = bb.at[:, :, y if mine else down(y, d, Y), c]
        return remote(ref, ref, b2_s.at[d - 1], b2_r.at[d - 1], dev)

    def bias_c(mine):
        ref = bb.at[:, :, :, c if mine else oc]
        return remote(ref, ref, bc_s.at[0], bc_r.at[0], to_c)

    def ag1(k):
        every = wg.at[k, :, : A - 1, b, y, c]
        remote(every, every, gz_s.at[0], gz_r.at[k], to_c).wait_recv()
        for copy in gather_1(k, True):
            copy.start()

    def ag2(k):
        for copy in gather_1(k, False):
            copy.wait_recv()
        for copy in gather_2(k, True):
            copy.start()

    def ag3(k):
        for copy in gather_2(k, False):
            copy.wait_recv()
        gather_c(k, True).start()

    def at1(k):
        for copy in turned_1(k, True):
            copy.start()

    def at2(k):
        for copy in turned_1(k, False):
            copy.wait_recv()
        for copy in turned_2(k, True):
            copy.start()

    def atz(k):
        for copy in turned_2(k, False):
            copy.wait_recv()
        for copy in turned_z(k):
            copy.start()

    def at3(k):
        every = wg.at[k, :, : A - 1, :, :, c]
        remote(every, every, gz_s.at[1], gz_r.at[k], to_c).wait_recv()
        gather_c(k, True).start()

    def bias_ag1():
        every = bb.at[: A - 1, b, y, c]
        remote(every, every, bz_s.at[0], bz_r.at[0], to_c).wait_recv()
        for d, dev in to_b:
            bias_1(d, dev, True).start()

    def bias_ag2():
        for d, dev in to_b:
            bias_1(d, dev, False).wait_recv()
        for d, dev in to_y:
            bias_2(d, dev, True).start()

    def bias_ag3():
        for d, dev in to_y:
            bias_2(d, dev, False).wait_recv()
        bias_c(True).start()

    def agz(k):
        for d, dev in to_a:
            gather_z(k, d, dev).start()

    def bias_agz():
        spread = lax.rem(lax.broadcasted_iota(jnp.int32, (rows, LANES), 1), rows)
        spread = (spread == lax.broadcasted_iota(jnp.int32, (rows, LANES), 0)).astype(F32).astype(BF16)
        own_bias = jnp.broadcast_to(bias[...], (8, rows))
        bb[a, b, y, c] = jnp.dot(own_bias, spread, preferred_element_type=F32)
        for d, dev in to_a:
            bias_z(d, dev).start()

    pltpu.make_async_copy(weight, weight, in_sem.at[0]).wait()
    bias_agz()
    agz(0)
    for k in LAST_GATHERED:
        at1(k)

    for copy in side_loads:
        copy.wait()
    cot_load(0).start()
    bacc[...] = jnp.zeros_like(bacc)

    def pooling(m, q):
        here = pl.multiple_of(q * SLOT, SLOT)
        flat = pl.multiple_of((m * slots + q) * SLOT, SLOT)
        listed = nbuf[m, :, pl.ds(here, SLOT)].astype(F32).astype(BF16)
        lane = lax.broadcasted_iota(jnp.int32, (SLOT, SLOT), 1)
        sub = lax.broadcasted_iota(jnp.int32, (SLOT, SLOT), 0)
        position = sub.astype(F32).astype(BF16)
        counted = jnp.zeros((SLOT, SLOT), BF16)
        for j in range(listed.shape[0]):
            counted = counted + jnp.where(listed[j : j + 1, :] == position, jnp.bfloat16(1), jnp.bfloat16(0))
        counted = counted.astype(F32).T
        ids, alive = sbuf[m : m + 1, pl.ds(here, SLOT)], lbuf[m : m + 1, pl.ds(here, SLOT)]
        along = jnp.where(alive > 0, ids, -1)
        down_ = jnp.broadcast_to(jnp.where(alive > 0, ids, -2), (SLOT, SLOT)).T
        adjacency = jnp.where(down_ == along, counted, 0.0)
        degree = jnp.sum(adjacency, axis=1, keepdims=True)
        factor = jnp.where(down_ >= 0, 1.0 / (degree + 1.0), 0.0)
        adjacency = jnp.where(lane == sub, (1.0 + ENHANCE) * (adjacency + 1.0), adjacency)
        adj, at = of(m, adj_e, adj_l)
        adj[at * slots + q] = adjacency.T.astype(BF16)
        rows_of(m, scale_e, scale_l)[pl.ds(here, SLOT), :] = factor
        block = rows_of(m, gp_e, gp_l)[pl.ds(here, SLOT), :]
        pooled = jnp.dot(adjacency.astype(BF16), block, preferred_element_type=F32)
        pooled = (pooled * jnp.concatenate([factor] * (D // SLOT), axis=1)).astype(BF16)
        rows_of(m, pool_e, pool_l)[pl.ds(here, SLOT), :] = pooled
        pool_t[:, :, :, pl.ds(flat, SLOT)] = pooled.T.reshape(groups, C, rows, SLOT)

    early = {
        2: [lambda: agz(1)],
        4: [bias_ag1, lambda: ag1(0)],
        6: [ag2a, lambda: agz(2)],
        8: [lambda: at2(6), lambda: at2(7)],
        10: [bias_ag2, ag2b, lambda: ag1(1), lambda: agz(3)],
    }
    for m in range(batches):
        feat_loads[m].wait()

        def step(q, carry, m=m):
            pooling(m, q)
            for at, events in early.items():
                if m * slots <= at < (m + 1) * slots:

                    @pl.when(q == at - m * slots)
                    def _(events=events):
                        for event in events:
                            event()

            return carry

        lax.fori_loop(0, slots, step, 0)

    agz(4)
    ag1(2)
    bias_ag3()
    ag3_first()
    agz(5)

    bias_c(False).wait_recv()
    tiles = bb[...].reshape(groups * C, 8, LANES)
    per = LANES // rows
    owner = lax.div(lax.broadcasted_iota(jnp.int32, (1, LANES), 1), rows)
    for j in range(D // LANES):
        row = jnp.zeros((1, LANES), F32)
        for p in range(per):
            row = jnp.where(owner == p, tiles[j * per + p, 0:1, :], row)
        brow[j] = jnp.broadcast_to(row, (8, LANES))

    def reduce_c(k):
        return remote(csend.at[k % 2], crecv.at[k % RECEIVED], rc_s.at[k % 2], rc_r.at[k], to_c)

    def reduce_1(k):
        e = k % 2
        out_a = [
            remote(s1a.at[e, d - 1], r1a.at[k, d - 1], p1a_s.at[e, d - 1], p1a_r.at[k, d - 1], dev) for d, dev in to_y
        ]
        out_b = [
            remote(s1b.at[e, d - 1], r1b.at[k, d - 1], p1b_s.at[e, d - 1], p1b_r.at[k, d - 1], dev) for d, dev in to_b
        ]
        return out_a + out_b

    def reduce_2(k):
        e = k % 2
        out_a = [
            remote(s2a.at[e, d - 1], r2a.at[k, d - 1], p2a_s.at[e, d - 1], p2a_r.at[k, d - 1], dev) for d, dev in to_b
        ]
        out_b = [
            remote(s2b.at[e, d - 1], r2b.at[k, d - 1], p2b_s.at[e, d - 1], p2b_r.at[k, d - 1], dev) for d, dev in to_y
        ]
        return out_a + out_b

    def reduce_z(k):
        e = k % 2
        return [remote(sz.at[e, d - 1], rz.at[k, d - 1], pz_s.at[e], pz_r.at[k], dev) for d, dev in to_a]

    def reduce_z_sent(k):
        remote(sz.at[k % 2], rz.at[k], pz_s.at[k % 2], pz_r.at[k], to_c).wait_send()

    def ago(k, n, copies):
        if k >= n:
            for copy in copies(k - n):
                copy.wait_send()

    lo, hi = slice(0, LANES), slice(LANES, CHUNK)

    def rs1(k):
        t, e = k % SLOTS, k % 2
        reduce_c(k).wait_recv()
        ago(k, 2, reduce_1)
        for d, _ in to_y:
            v = up(y, d, Y)
            s1a[e, d - 1] = (acc[t, :, :, v, :, lo] + crecv[k % RECEIVED, :, :, v, :, lo].astype(F32)).astype(BF16)
        for d, _ in to_b:
            v = up(b, d, B)
            s1b[e, d - 1] = (acc[t, :, v, :, :, hi] + crecv[k % RECEIVED, :, v, :, :, hi].astype(F32)).astype(BF16)
        for copy in reduce_1(k):
            copy.start()
        acc[t, :, :, y, :, lo] = acc[t, :, :, y, :, lo] + crecv[k % RECEIVED, :, :, y, :, lo].astype(F32)
        acc[t, :, b, :, :, hi] = acc[t, :, b, :, :, hi] + crecv[k % RECEIVED, :, b, :, :, hi].astype(F32)

    def rs2(k):
        t, e = k % SLOTS, k % 2
        for copy in reduce_1(k):
            copy.wait_recv()
        ago(k, 2, reduce_2)

        def total_a(v):
            out = acc[t, :, v, y, :, lo]
            for d, _ in to_y:
                out = out + r1a[k, d - 1, :, v].astype(F32)
            return out

        def total_b(v):
            out = acc[t, :, b, v, :, hi]
            for d, _ in to_b:
                out = out + r1b[k, d - 1, :, v].astype(F32)
            return out

        for d, _ in to_b:
            s2a[e, d - 1] = total_a(up(b, d, B)).astype(BF16)
        for d, _ in to_y:
            s2b[e, d - 1] = total_b(up(y, d, Y)).astype(BF16)
        for copy in reduce_2(k):
            copy.start()
        acc[t, :, b, y, :, lo] = total_a(b)
        acc[t, :, b, y, :, hi] = total_b(y)

    def rs3(k):
        t, e = k % SLOTS, k % 2
        for copy in reduce_2(k):
            copy.wait_recv()
        if k >= 2:
            reduce_z_sent(k - 2)

        def total(v):
            left, right = acc[t, v, b, y, :, lo], acc[t, v, b, y, :, hi]
            for d, _ in to_b:
                left = left + r2a[k, d - 1, v].astype(F32)
            for d, _ in to_y:
                right = right + r2b[k, d - 1, v].astype(F32)
            return jnp.concatenate([left, right], axis=1)

        for d, _ in to_a:
            sz[e, d - 1] = total(up(a, d, A)).astype(BF16)
        for copy in reduce_z(k):
            copy.start()
        acc[t, a, b, y] = total(a)

    def rs4(k):
        t = k % SLOTS
        remote(sz.at[k % 2], rz.at[k], pz_s.at[k % 2], pz_r.at[k], to_c).wait_recv()
        out = acc[t, a, b, y]
        for d, _ in to_a:
            out = out + rz[k, d - 1].astype(F32)
        wout[:, columns(k)] = out

    def bred_c():
        return remote(bt.at[:, :, :, oc], brc, dc_s.at[0], dc_r.at[0], to_c)

    def bred_1():
        return [remote(bsum.at[:, :, up(y, d, Y)], br1.at[d - 1], d1_s.at[d - 1], d1_r.at[d - 1], dev) for d, dev in to_y]

    def bred_2():
        return [remote(bsum.at[:, up(b, d, B), y], br2.at[d - 1], d2_s.at[d - 1], d2_r.at[d - 1], dev) for d, dev in to_b]

    def bred_z():
        return [remote(bsum.at[up(a, d, A), b, y], brz.at[d - 1], dz_s.at[0], dz_r.at[0], dev) for d, dev in to_a]

    def bias_rs0():
        for a_ in range(A):
            for b_ in range(B):
                for y_ in range(Y):
                    for c_ in range(C):
                        block = (((a_ * B + b_) * Y + y_) * C + c_) * rows // LANES
                        bt[a_, b_, y_, c_] = bacc[:, block * LANES : (block + 1) * LANES]
        bred_c().start()

    def bias_rs1():
        bred_c().wait_recv()
        bsum[...] = bt[:, :, :, c] + brc[...]
        for copy in bred_1():
            copy.start()

    def bias_rs2():
        for copy in bred_1():
            copy.wait_recv()
        for d, _ in to_y:
            bsum[:, :, y] = bsum[:, :, y] + br1[d - 1]
        for copy in bred_2():
            copy.start()

    def bias_rs3():
        for copy in bred_2():
            copy.wait_recv()
        for d, _ in to_b:
            bsum[:, b, y] = bsum[:, b, y] + br2[d - 1]
        for copy in bred_z():
            copy.start()

    def bias_rs4():
        remote(brz, brz, dz_s.at[0], dz_r.at[0], to_c).wait_recv()
        out = bsum[a, b, y]
        for d, _ in to_a:
            out = out + brz[d - 1]
        out = jnp.sum(out, axis=0, keepdims=True)
        place = lax.rem((dp * (Y * C) + rep) * rows, LANES)
        mine = jnp.zeros((1, rows), F32)
        for p in range(per):
            mine = jnp.where(place == p * rows, out[:, p * rows : (p + 1) * rows], mine)
        bgrad_out[...] = mine

    def forward(k, parts):
        e = k % 2
        w = jnp.concatenate([wg[k, h].reshape(D, LANES) for h in range(2)], axis=1)
        offset = jnp.concatenate([brow[2 * k + h][0:1] for h in range(2)], axis=1)
        sums = jnp.zeros((8, CHUNK), F32)
        for m in parts:
            preact = jnp.dot(rows_of(m, pool_e, pool_l)[...], w, preferred_element_type=F32) + offset
            squash = jax.nn.sigmoid(preact)
            active = preact * squash
            act[k, m] = active.astype(BF16)
            grad = (ct[e, m].astype(F32) * (squash + active * (1.0 - squash))).astype(BF16)
            rows_of(m, gp_e, gp_l)[:, columns(k)] = grad
            sums = sums + jnp.sum(grad.astype(F32).reshape(local // 8, 8, CHUNK), axis=0)
        bacc[:, columns(k)] = sums if parts[0] == 0 else bacc[:, columns(k)] + sums

    def weight_term(k, which):
        left = pool_t[:, which].reshape(plane, N)
        right = jnp.concatenate([gp_e[:, columns(k)], gp_l[:, columns(k)]], axis=0)
        return jnp.dot(left, right, preferred_element_type=F32).reshape(A, B, Y, rows, CHUNK)

    def forward_region(k):
        gather_c(k, False).wait_recv()
        cot_load(k).wait()
        if not isinstance(k, int) or k + 1 < chunks:
            cot_load(k + 1).start()

    def weight_region(k):
        if k >= 2:
            reduce_c(k - 2).wait_send()

    def weight_other(k):
        csend[k % 2] = weight_term(k, oc).astype(BF16)

    def weight_own(k):
        acc[k % SLOTS] = weight_term(k, c)

    whole = list(range(batches))

    regions = [(0, None), (None, 0), (1, None), (None, 1), (2, None)]
    regions += [(k, k - 1) for k in range(3, chunks - 1)]
    regions += [(None, chunks - 2), (chunks - 1, None), (None, chunks - 1)]
    plan = [
        (lambda _: bias_rs0(), {0: 11}),
        (lambda _: bias_rs1(), {0: 11.5}),
        (ag2, {1: 0, 2: 1, 3: 2, 4: 3, 5: 5}),
        (ag1, {3: 0, 4: 1, 5: 3}),
        (ag3, {1: 1, 2: 3, 3: 4, 4: 5, 5: 6}),
        (at3, {6: 7, 7: 8}),
        (atz, {6: 0, 7: 4}),
        (rs4, {0: 10, 1: 12}),
        (rs3, {0: 8.5, 1: 9, 2: 10, 3: 11, 4: 12}),
        (rs2, {0: 7, 1: 7.5, 2: 8, 3: 9, 4: 10, 5: 12}),
        (rs1, {0: 5.5, 1: 6, 2: 6.5, 3: 7, 4: 8, 5: 9, 6: 10}),
    ]

    def ahead_of(at):
        return [(stage, k) for stage, when in plan for k, ahead in when.items() if ahead == at]

    def opening(j, carry):
        for place in range(2):
            for step in range(2):
                for stage, k in ahead_of(2 * step + place):
                    pl.when(j == step)(functools.partial(stage, k))
            if place == 0:
                forward_region(j)
                region(lambda: forward(j, whole))
            else:
                region(lambda: weight_other(j))
                reduce_c(j).start()
                region(lambda: weight_own(j))
        return carry

    lax.fori_loop(0, 2, opening, 0)
    for at, (f, w) in enumerate(regions):
        if at < 4:
            continue
        for stage, k in ahead_of(at):
            stage(k)
        if f is not None:
            forward_region(f)
        if w is not None:
            weight_region(w)
        merged = f is not None and w is not None

        @region
        def _(f=f, w=w, merged=merged):
            if f is not None:
                forward(f, whole[:1] if merged else whole)
            if w is not None:
                weight_other(w)

        if w is not None:
            reduce_c(w).start()
            for stage, k in ahead_of(at + 0.5):
                stage(k)

            @region
            def _(f=f, w=w, merged=merged):
                if merged:
                    forward(f, whole[1:])
                weight_own(w)

    for stage, k in ahead_of(len(regions)):
        stage(k)

    def feature_grad(i):
        n, m = lax.div(i, first), lax.rem(i, first)
        part, cols = pl.ds(pl.multiple_of(m * local, local), local), pl.ds(pl.multiple_of(n * wide, wide), wide)
        pool_e[part, cols] = feature_tile(dims, wg, gp_e, adj_e, scale_e, local, n, m)

    late = [
        (rs1, {7: 0}),
        (rs2, {6: 0, 7: 2}),
        (lambda _: bias_rs2(), {0: 1}),
        (lambda _: bias_rs3(), {0: 3}),
        (rs3, {5: 1, 6: 3, 7: 4}),
        (rs4, {2: 0, 3: 1, 4: 3, 5: 5, 6: 7, 7: 7}),
        (lambda _: bias_rs4(), {0: 7}),
    ]

    def last(i, carry):
        pl.when(i >= 0)(lambda: feature_grad(i))
        for stage, when in late:
            for k, at in when.items():
                pl.when(i == at)(functools.partial(stage, k))
        return carry

    lax.fori_loop(0, A * first, last, 0)

    for k in (chunks - 2, chunks - 1):
        for copy in [reduce_c(k)] + reduce_1(k) + reduce_2(k):
            copy.wait_send()
        reduce_z_sent(k)

    def drained(ref, sem, dev):
        remote(ref, ref, sem, sem, dev).wait_send()

    plain, turned = slice(0, LAST_GATHERED[0]), slice(LAST_GATHERED[0], chunks)
    drained(wg.at[plain, :, : A - 1, b, y, c], gz_s.at[0], to_c)
    drained(wg.at[turned, :, : A - 1, :, :, c], gz_s.at[1], to_c)
    for d, dev in to_b:
        drained(wg.at[plain, 0, :, b, y, c], g1a_s.at[0, d - 1], dev)
        drained(wg.at[plain, 1, :, b, :, c], g2b_s.at[0, d - 1], dev)
        drained(wg.at[turned, 0, a, b, y, c], g1a_s.at[1, d - 1], dev)
        drained(wg.at[turned, 1, a, b, :, c], g2b_s.at[1, d - 1], dev)
    for d, dev in to_y:
        drained(wg.at[plain, 1, :, b, y, c], g1b_s.at[0, d - 1], dev)
        drained(wg.at[plain, 0, :, :, y, c], g2a_s.at[0, d - 1], dev)
        drained(wg.at[turned, 1, a, b, y, c], g1b_s.at[1, d - 1], dev)
        drained(wg.at[turned, 0, a, :, y, c], g2a_s.at[1, d - 1], dev)
    drained(wg.at[:, :, :, :, :, c], gc_s.at[0], to_c)
    drained(bb.at[: A - 1, b, y, c], bz_s.at[0], to_c)
    for d, dev in to_b:
        bias_1(d, dev, True).wait_send()
    for d, dev in to_y:
        bias_2(d, dev, True).wait_send()
    bias_c(True).wait_send()
    for copy in [bred_c()] + bred_1() + bred_2():
        copy.wait_send()
    drained(brz, dz_s.at[0], to_c)


def per_device(dims, features, cotangent, neighbours, segments, live, weight, bias):
    A, B, Y, C = dims
    batches, local, D = features.shape
    rows = weight.shape[0]
    N = batches * local
    N_l = LATE * local
    N_e = N - N_l
    chunks = D // CHUNK
    groups = A * B * Y
    wide = D // A
    neighbours = jnp.swapaxes(neighbours, 1, 2)
    any_spec = pl.BlockSpec(memory_space=pl.ANY)
    vmem, dma = pltpu.VMEM, pltpu.SemaphoreType.DMA
    scratch = [
        vmem((N_e, D), BF16),
        vmem((N_l, D), BF16),
        vmem((N_e // SLOT, SLOT, SLOT), BF16),
        vmem((N_e, SLOT), F32),
        vmem((groups, C, rows, N), BF16),
        vmem((2, batches, local, CHUNK), BF16),
        vmem((SLOTS, A, B, Y, rows, CHUNK), F32),
        vmem((2, A, B, Y, rows, CHUNK), BF16),
        vmem((RECEIVED, A, B, Y, rows, CHUNK), BF16),
        vmem((2, Y - 1, A, B, rows, LANES), BF16),
        vmem((2, B - 1, A, Y, rows, LANES), BF16),
        vmem((2, B - 1, A, rows, LANES), BF16),
        vmem((2, Y - 1, A, rows, LANES), BF16),
        vmem((2, A - 1, rows, CHUNK), BF16),
        vmem((chunks, Y - 1, A, B, rows, LANES), BF16),
        vmem((chunks, B - 1, A, Y, rows, LANES), BF16),
        vmem((chunks, B - 1, A, rows, LANES), BF16),
        vmem((chunks, Y - 1, A, rows, LANES), BF16),
        vmem((chunks, A - 1, rows, CHUNK), BF16),
        vmem(neighbours.shape, jnp.int32),
        vmem(segments.shape, jnp.int32),
        vmem(live.shape, jnp.int32),
        vmem((A, B, Y, C, 8, LANES), F32),
        vmem((D // LANES, 8, LANES), F32),
        vmem((8, D), F32),
        vmem((A, B, Y, C, 8, LANES), F32),
        vmem((A, B, Y, 8, LANES), F32),
        vmem((A, B, Y, 8, LANES), F32),
        vmem((Y - 1, A, B, 8, LANES), F32),
        vmem((B - 1, A, 8, LANES), F32),
        vmem((A - 1, 8, LANES), F32),
        dma((4 + batches,)),
        dma((2,)),
    ]
    scratch_tail = [dma((Y - 1,)), dma((B - 1,))]
    for sent, received in (
        ((2,), (chunks,)),
        ((2, B - 1), (chunks, B - 1)),
        ((2, Y - 1), (chunks, Y - 1)),
        ((2, Y - 1), (chunks, Y - 1)),
        ((2, B - 1), (chunks, B - 1)),
        ((1,), (chunks,)),
        ((2,), (chunks,)),
        ((2, Y - 1), (chunks, Y - 1)),
        ((2, B - 1), (chunks, B - 1)),
        ((2, B - 1), (chunks, B - 1)),
        ((2, Y - 1), (chunks, Y - 1)),
        ((2,), (chunks,)),
        (None, scratch_tail),
        ((1,), (1,)),
        ((B - 1,), (B - 1,)),
        ((Y - 1,), (Y - 1,)),
        ((1,), (1,)),
        ((1,), (1,)),
        ((Y - 1,), (Y - 1,)),
        ((B - 1,), (B - 1,)),
        ((1,), (1,)),
    ):
        scratch += received if sent is None else [dma(sent), dma(received)]
    vmem_spec = pl.BlockSpec(memory_space=pltpu.VMEM)
    kept = [
        vmem((chunks, batches, local, CHUNK), BF16),
        vmem((chunks, 2, A, B, Y, C, rows, LANES), BF16),
        vmem((N_l, D), BF16),
        vmem((N_e, D), BF16),
        vmem((N_l // SLOT, SLOT, SLOT), BF16),
        vmem((N_l, SLOT), F32),
        vmem((rows, D), F32),
        vmem((1, rows), F32),
    ]
    kept_arrays = pl.pallas_call(
        functools.partial(kernel, dims),
        out_shape=kept,
        in_specs=[any_spec] * 6 + [vmem_spec],
        out_specs=[vmem_spec] * len(kept),
        scratch_shapes=scratch,
        compiler_params=pltpu.CompilerParams(
            collective_id=0, has_side_effects=True, vmem_limit_bytes=39 * 2**20
        ),
        cost_estimate=pl.CostEstimate(
            flops=6 * N * D * D, bytes_accessed=8 * N * D, transcendentals=N * D
        ),
    )(features, cotangent, neighbours, segments, live, weight, bias.reshape(1, rows))
    act, fgrad, wgrad, bgrad = pl.pallas_call(
        functools.partial(finish, dims),
        out_shape=[
            jax.ShapeDtypeStruct(features.shape, BF16),
            jax.ShapeDtypeStruct(features.shape, BF16),
            jax.ShapeDtypeStruct(weight.shape, F32),
            jax.ShapeDtypeStruct((1, rows), F32),
        ],
        in_specs=[vmem_spec] * len(kept),
        out_specs=[any_spec] * 3 + [vmem_spec],
        scratch_shapes=[
            vmem((A * LATE, local, wide), BF16),
            dma((1,)), dma((batches - LATE,)), dma((A * LATE,)), dma((1,)),
        ],
        compiler_params=pltpu.CompilerParams(vmem_limit_bytes=8 * 2**20),
    )(
        *[pltpu.with_memory_space_constraint(x, pltpu.VMEM) for x in kept_arrays],
    )
    return act, fgrad, wgrad, bgrad.reshape(rows)


def solution(mesh):
    both = ("dp", "rep")
    dims = split_axes(mesh.shape["dp"], mesh.shape["rep"])
    return jax.shard_map(
        functools.partial(per_device, dims),
        mesh=mesh,
        in_specs=(
            P(None, both, None), P(None, both, None), P(None, both, None),
            P(None, both), P(None, both), P(both, None), P(both),
        ),
        out_specs=(P(None, both, None), P(None, both, None), P(both, None), P(both)),
        check_vma=False,
    )
```

```python
import functools

import jax
import jax.numpy as jnp
from jax import lax
from jax.experimental import pallas as pl
from jax.experimental.pallas import tpu as pltpu
from jax.sharding import PartitionSpec as P

SLOT = 128
LANES = 128
CHUNK = 256
MESH = pl.DeviceIdType.MESH
F32, BF16 = jnp.float32, jnp.bfloat16
ENHANCE = 1.0
LATE = 1
SLOTS, RECEIVED = 7, 6
LAST_GATHERED = (6, 7)


def split_axes(dp, rep):
    b = 2 ** ((dp.bit_length() - 1) // 2)
    return dp // b, b, rep // 2, 2


def feature_tile(dims, wg, gp, adj_t, scale, local, n, m):
    A, B, Y, C = dims
    chunks, rows = wg.shape[0], wg.shape[-2]
    wide = B * Y * C * rows
    slots = local // SLOT
    base = m * local if isinstance(m, int) else pl.multiple_of(m * local, local)
    w = jnp.concatenate([wg[k, h, n].reshape(wide, LANES) for k in range(chunks) for h in range(2)], axis=1)
    grad = lax.dot_general(gp[pl.ds(base, local), :], w, (((1,), (1,)), ((), ())), preferred_element_type=F32)
    grad = grad * jnp.concatenate([scale[pl.ds(base, local), :]] * (wide // LANES), axis=1)
    high = grad.astype(BF16)
    low = (grad - high.astype(F32)).astype(BF16)
    tiles = []
    for q in range(slots):
        left = adj_t[m * slots + q]
        part = slice(q * SLOT, (q + 1) * SLOT)
        right = jnp.concatenate([high[part], low[part]], axis=0)
        out = jnp.dot(jnp.concatenate([left, left], axis=1), right, preferred_element_type=F32)
        tiles.append(out.astype(BF16))
    return jnp.concatenate(tiles, axis=0)


def finish(
    dims, act, wg, gp, done, adj_t, scale, wout, bgrad_in, act_out, fgrad_out, wgrad_out, bgrad_out,
    fout, act_sem, done_sem, fout_sem, wout_sem,
):
    batches, local, D = fgrad_out.shape
    blocks, wide, early = dims[0], D // dims[0], batches - LATE

    def store(i):
        n, m = lax.div(i, LATE), early + lax.rem(i, LATE)
        cols = pl.ds(pl.multiple_of(n * wide, wide), wide)
        return pltpu.make_async_copy(fout.at[i], fgrad_out.at[m, :, cols], fout_sem.at[i])

    kept = [pltpu.make_async_copy(wout, wgrad_out, wout_sem.at[0])]
    for m in range(early):
        kept.append(pltpu.make_async_copy(done.at[pl.ds(m * local, local)], fgrad_out.at[m], done_sem.at[m]))
    for copy in kept:
        copy.start()
    for k in range(act.shape[0]):
        pltpu.make_async_copy(act.at[k], act_out.at[:, :, pl.ds(k * CHUNK, CHUNK)], act_sem.at[0]).start()
    bgrad_out[...] = bgrad_in[...]

    def step(i, carry):
        fout[i] = feature_tile(dims, wg, gp, adj_t, scale, local, lax.div(i, LATE), lax.rem(i, LATE))
        store(i).start()
        return carry

    lax.fori_loop(0, blocks * LATE, step, 0)
    for i in range(blocks * LATE):
        store(i).wait()
    pltpu.make_async_copy(act, act, act_sem.at[0]).wait()
    for copy in kept:
        copy.wait()


def kernel(
    dims, feat, cot, nbr, seg, live, weight, bias, act, wg, gp_l, pool_e, adj_l, scale_l, wout, bgrad_out,
    gp_e, pool_l, adj_e, scale_e, pool_t, ct, acc, csend, crecv, s1a, s1b, s2a, s2b, sz, r1a, r1b, r2a, r2b, rz,
    nbuf, sbuf, lbuf, bb, brow, bacc, bt, bsum, brc, br1, br2, brz,
    in_sem, ct_sem,
    gz_s, gz_r, g1a_s, g1a_r, g1b_s, g1b_r, g2a_s, g2a_r, g2b_s, g2b_r, gc_s, gc_r,
    rc_s, rc_r, p1a_s, p1a_r, p1b_s, p1b_r, p2a_s, p2a_r, p2b_s, p2b_r, pz_s, pz_r,
    ha_r, hb_r, bz_s, bz_r, b1_s, b1_r, b2_s, b2_r, bc_s, bc_r, dc_s, dc_r, d1_s, d1_r, d2_s, d2_r, dz_s, dz_r,
):
    A, B, Y, C = dims
    batches, local, D = feat.shape
    rows = weight.shape[0]
    slots = local // SLOT
    N = batches * local
    chunks = D // CHUNK
    groups = A * B * Y
    plane = groups * rows
    first = batches - LATE
    wide = D // A

    dp, rep = lax.axis_index("dp"), lax.axis_index("rep")
    a, b, y, c = lax.div(dp, B), lax.rem(dp, B), lax.div(rep, C), lax.rem(rep, C)
    oc = 1 - c

    def device(a_, b_, y_, c_):
        return (a_ * B + b_, y_ * C + c_)

    def columns(k):
        return pl.ds(k * CHUNK if isinstance(k, int) else pl.multiple_of(k * CHUNK, CHUNK), CHUNK)

    def of(m, ref_e, ref_l):
        return (ref_e, m) if m < first else (ref_l, m - first)

    def rows_of(m, ref_e, ref_l):
        ref, at = of(m, ref_e, ref_l)
        return ref.at[pl.ds(at * local, local)]

    def up(v, d, n):
        return lax.rem(v + d, n)

    def down(v, d, n):
        return lax.rem(v + n - d, n)

    to_a = [(d, device(up(a, d, A), b, y, c)) for d in range(1, A)]
    to_b = [(d, device(a, up(b, d, B), y, c)) for d in range(1, B)]
    to_y = [(d, device(a, b, up(y, d, Y), c)) for d in range(1, Y)]
    to_c = device(a, b, y, oc)

    def remote(src, dst, ssem, rsem, dev):
        return pltpu.make_async_remote_copy(
            src_ref=src, dst_ref=dst, send_sem=ssem, recv_sem=rsem, device_id=dev, device_id_type=MESH
        )

    weight_loads = [
        pltpu.make_async_copy(
            weight.at[:, pl.ds((2 * k + h) * LANES, LANES)], wg.at[k, h, a, b, y, c], in_sem.at[0]
        )
        for k in range(chunks)
        for h in range(2)
    ]
    side_loads = [
        pltpu.make_async_copy(nbr, nbuf, in_sem.at[1]),
        pltpu.make_async_copy(seg, sbuf, in_sem.at[2]),
        pltpu.make_async_copy(live, lbuf, in_sem.at[3]),
    ]
    feat_loads = [
        pltpu.make_async_copy(feat.at[m], rows_of(m, gp_e, gp_l), in_sem.at[4 + m]) for m in range(batches)
    ]
    for copy in weight_loads:
        copy.start()
    for copy in side_loads:
        copy.start()
    for copy in feat_loads:
        copy.start()

    barrier = pltpu.get_barrier_semaphore()
    partners = [dev for _, dev in to_a + to_b + to_y] + [to_c]
    for dev in partners:
        pl.semaphore_signal(barrier, inc=1, device_id=dev, device_id_type=MESH)

    def cot_load(k):
        return pltpu.make_async_copy(cot.at[:, :, columns(k)], ct.at[k % 2], ct_sem.at[k % 2])

    pl.semaphore_wait(barrier, len(partners))

    def gather_z(k, d, dev):
        ref = wg.at[k, :, a, b, y, c]
        return remote(ref, ref, gz_s.at[0], gz_r.at[k], dev)

    def gather_1(k, mine):
        out = []
        for d, dev in to_b:
            ref = wg.at[k, 0, :, b if mine else down(b, d, B), y, c]
            out.append(remote(ref, ref, g1a_s.at[0, d - 1], g1a_r.at[k, d - 1], dev))
        for d, dev in to_y:
            ref = wg.at[k, 1, :, b, y if mine else down(y, d, Y), c]
            out.append(remote(ref, ref, g1b_s.at[0, d - 1], g1b_r.at[k, d - 1], dev))
        return out

    def gather_2(k, mine):
        out = []
        for d, dev in to_y:
            ref = wg.at[k, 0, :, :, y if mine else down(y, d, Y), c]
            out.append(remote(ref, ref, g2a_s.at[0, d - 1], g2a_r.at[k, d - 1], dev))
        for d, dev in to_b:
            ref = wg.at[k, 1, :, b if mine else down(b, d, B), :, c]
            out.append(remote(ref, ref, g2b_s.at[0, d - 1], g2b_r.at[k, d - 1], dev))
        return out

    def turned_1(k, mine):
        out = []
        for d, dev in to_b:
            ref = wg.at[k, 0, a, b if mine else down(b, d, B), y, c]
            out.append(remote(ref, ref, g1a_s.at[1, d - 1], g1a_r.at[k, d - 1], dev))
        for d, dev in to_y:
            ref = wg.at[k, 1, a, b, y if mine else down(y, d, Y), c]
            out.append(remote(ref, ref, g1b_s.at[1, d - 1], g1b_r.at[k, d - 1], dev))
        return out

    def turned_2(k, mine):
        out = []
        for d, dev in to_y:
            ref = wg.at[k, 0, a, :, y if mine else down(y, d, Y), c]
            out.append(remote(ref, ref, g2a_s.at[1, d - 1], g2a_r.at[k, d - 1], dev))
        for d, dev in to_b:
            ref = wg.at[k, 1, a, b if mine else down(b, d, B), :, c]
            out.append(remote(ref, ref, g2b_s.at[1, d - 1], g2b_r.at[k, d - 1], dev))
        return out

    def turned_z(k):
        out = []
        ref = wg.at[k, :, a, :, :, c]
        for d, dev in to_a:
            out.append(remote(ref, ref, gz_s.at[1], gz_r.at[k], dev))
        return out

    def half_step(mine):
        out = []
        for d, dev in to_y:
            ref = wg.at[0, 0, :, b, y if mine else down(y, d, Y), c]
            out.append(remote(ref, ref, g2a_s.at[0, d - 1], ha_r.at[d - 1], dev))
        for d, dev in to_b:
            ref = wg.at[0, 1, :, b if mine else down(b, d, B), y, c]
            out.append(remote(ref, ref, g2b_s.at[0, d - 1], hb_r.at[d - 1], dev))
        return out

    def ag2a():
        for copy in half_step(True):
            copy.start()

    def ag2b():
        for copy in gather_1(0, False):
            copy.wait_recv()
        for d, dev in to_y:
            for e in range(1, B):
                ref = wg.at[0, 0, :, down(b, e, B), y, c]
                remote(ref, ref, g2a_s.at[0, d - 1], g2a_r.at[0, d - 1], dev).start()
        for d, dev in to_b:
            for e in range(1, Y):
                ref = wg.at[0, 1, :, b, down(y, e, Y), c]
                remote(ref, ref, g2b_s.at[0, d - 1], g2b_r.at[0, d - 1], dev).start()

    def ag3_first():
        for copy in half_step(False):
            copy.wait_recv()
        for d, dev in to_y:
            ref = wg.at[0, 0, :, : B - 1, y, c]
            remote(ref, ref, g2a_s.at[0, d - 1], g2a_r.at[0, d - 1], dev).wait_recv()
        for d, dev in to_b:
            ref = wg.at[0, 1, :, b, : Y - 1, c]
            remote(ref, ref, g2b_s.at[0, d - 1], g2b_r.at[0, d - 1], dev).wait_recv()
        gather_c(0, True).start()

    def gather_c(k, mine):
        ref = wg.at[k, :, :, :, :, c if mine else oc]
        return remote(ref, ref, gc_s.at[0], gc_r.at[k], to_c)

    def region(fn):
        pl.when(dp >= 0)(fn)

    def bias_z(d, dev):
        ref = bb.at[a, b, y, c]
        return remote(ref, ref, bz_s.at[0], bz_r.at[0], dev)

    def bias_1(d, dev, mine):
        ref = bb.at[:, b if mine else down(b, d, B), y, c]
        return remote(ref, ref, b1_s.at[d - 1], b1_r.at[d - 1], dev)

    def bias_2(d, dev, mine):
        ref = bb.at[:, :, y if mine else down(y, d, Y), c]
        return remote(ref, ref, b2_s.at[d - 1], b2_r.at[d - 1], dev)

    def bias_c(mine):
        ref = bb.at[:, :, :, c if mine else oc]
        return remote(ref, ref, bc_s.at[0], bc_r.at[0], to_c)

    def ag1(k):
        every = wg.at[k, :, : A - 1, b, y, c]
        remote(every, every, gz_s.at[0], gz_r.at[k], to_c).wait_recv()
        for copy in gather_1(k, True):
            copy.start()

    def ag2(k):
        for copy in gather_1(k, False):
            copy.wait_recv()
        for copy in gather_2(k, True):
            copy.start()

    def ag3(k):
        for copy in gather_2(k, False):
            copy.wait_recv()
        gather_c(k, True).start()

    def at1(k):
        for copy in turned_1(k, True):
            copy.start()

    def at2(k):
        for copy in turned_1(k, False):
            copy.wait_recv()
        for copy in turned_2(k, True):
            copy.start()

    def atz(k):
        for copy in turned_2(k, False):
            copy.wait_recv()
        for copy in turned_z(k):
            copy.start()

    def at3(k):
        every = wg.at[k, :, : A - 1, :, :, c]
        remote(every, every, gz_s.at[1], gz_r.at[k], to_c).wait_recv()
        gather_c(k, True).start()

    def bias_ag1():
        every = bb.at[: A - 1, b, y, c]
        remote(every, every, bz_s.at[0], bz_r.at[0], to_c).wait_recv()
        for d, dev in to_b:
            bias_1(d, dev, True).start()

    def bias_ag2():
        for d, dev in to_b:
            bias_1(d, dev, False).wait_recv()
        for d, dev in to_y:
            bias_2(d, dev, True).start()

    def bias_ag3():
        for d, dev in to_y:
            bias_2(d, dev, False).wait_recv()
        bias_c(True).start()

    def agz(k):
        for d, dev in to_a:
            gather_z(k, d, dev).start()

    def bias_agz():
        spread = lax.rem(lax.broadcasted_iota(jnp.int32, (rows, LANES), 1), rows)
        spread = (spread == lax.broadcasted_iota(jnp.int32, (rows, LANES), 0)).astype(F32).astype(BF16)
        own_bias = jnp.broadcast_to(bias[...], (8, rows))
        bb[a, b, y, c] = jnp.dot(own_bias, spread, preferred_element_type=F32)
        for d, dev in to_a:
            bias_z(d, dev).start()

    pltpu.make_async_copy(weight, weight, in_sem.at[0]).wait()
    bias_agz()
    agz(0)
    for k in LAST_GATHERED:
        at1(k)

    for copy in side_loads:
        copy.wait()
    cot_load(0).start()
    bacc[...] = jnp.zeros_like(bacc)

    def pooling(m, q):
        here = pl.multiple_of(q * SLOT, SLOT)
        flat = pl.multiple_of((m * slots + q) * SLOT, SLOT)
        listed = nbuf[m, :, pl.ds(here, SLOT)].astype(F32).astype(BF16)
        lane = lax.broadcasted_iota(jnp.int32, (SLOT, SLOT), 1)
        sub = lax.broadcasted_iota(jnp.int32, (SLOT, SLOT), 0)
        position = sub.astype(F32).astype(BF16)
        counted = jnp.zeros((SLOT, SLOT), BF16)
        for j in range(listed.shape[0]):
            counted = counted + jnp.where(listed[j : j + 1, :] == position, jnp.bfloat16(1), jnp.bfloat16(0))
        counted = counted.astype(F32).T
        ids, alive = sbuf[m : m + 1, pl.ds(here, SLOT)], lbuf[m : m + 1, pl.ds(here, SLOT)]
        along = jnp.where(alive > 0, ids, -1)
        down_ = jnp.broadcast_to(jnp.where(alive > 0, ids, -2), (SLOT, SLOT)).T
        adjacency = jnp.where(down_ == along, counted, 0.0)
        degree = jnp.sum(adjacency, axis=1, keepdims=True)
        factor = jnp.where(down_ >= 0, 1.0 / (degree + 1.0), 0.0)
        adjacency = jnp.where(lane == sub, (1.0 + ENHANCE) * (adjacency + 1.0), adjacency)
        adj, at = of(m, adj_e, adj_l)
        adj[at * slots + q] = adjacency.T.astype(BF16)
        rows_of(m, scale_e, scale_l)[pl.ds(here, SLOT), :] = factor
        block = rows_of(m, gp_e, gp_l)[pl.ds(here, SLOT), :]
        pooled = jnp.dot(adjacency.astype(BF16), block, preferred_element_type=F32)
        pooled = (pooled * jnp.concatenate([factor] * (D // SLOT), axis=1)).astype(BF16)
        rows_of(m, pool_e, pool_l)[pl.ds(here, SLOT), :] = pooled
        pool_t[:, :, :, pl.ds(flat, SLOT)] = pooled.T.reshape(groups, C, rows, SLOT)

    early = {
        2: [lambda: agz(1)],
        4: [bias_ag1, lambda: ag1(0)],
        6: [ag2a, lambda: agz(2)],
        8: [lambda: at2(6), lambda: at2(7)],
        10: [bias_ag2, ag2b, lambda: ag1(1), lambda: agz(3)],
    }
    for m in range(batches):
        feat_loads[m].wait()

        def step(q, carry, m=m):
            pooling(m, q)
            for at, events in early.items():
                if m * slots <= at < (m + 1) * slots:

                    @pl.when(q == at - m * slots)
                    def _(events=events):
                        for event in events:
                            event()

            return carry

        lax.fori_loop(0, slots, step, 0)

    agz(4)
    ag1(2)
    bias_ag3()
    ag3_first()
    agz(5)

    bias_c(False).wait_recv()
    tiles = bb[...].reshape(groups * C, 8, LANES)
    per = LANES // rows
    owner = lax.div(lax.broadcasted_iota(jnp.int32, (1, LANES), 1), rows)
    for j in range(D // LANES):
        row = jnp.zeros((1, LANES), F32)
        for p in range(per):
            row = jnp.where(owner == p, tiles[j * per + p, 0:1, :], row)
        brow[j] = jnp.broadcast_to(row, (8, LANES))

    def reduce_c(k):
        return remote(csend.at[k % 2], crecv.at[k % RECEIVED], rc_s.at[k % 2], rc_r.at[k], to_c)

    def reduce_1(k):
        e = k % 2
        out_a = [
            remote(s1a.at[e, d - 1], r1a.at[k, d - 1], p1a_s.at[e, d - 1], p1a_r.at[k, d - 1], dev) for d, dev in to_y
        ]
        out_b = [
            remote(s1b.at[e, d - 1], r1b.at[k, d - 1], p1b_s.at[e, d - 1], p1b_r.at[k, d - 1], dev) for d, dev in to_b
        ]
        return out_a + out_b

    def reduce_2(k):
        e = k % 2
        out_a = [
            remote(s2a.at[e, d - 1], r2a.at[k, d - 1], p2a_s.at[e, d - 1], p2a_r.at[k, d - 1], dev) for d, dev in to_b
        ]
        out_b = [
            remote(s2b.at[e, d - 1], r2b.at[k, d - 1], p2b_s.at[e, d - 1], p2b_r.at[k, d - 1], dev) for d, dev in to_y
        ]
        return out_a + out_b

    def reduce_z(k):
        e = k % 2
        return [remote(sz.at[e, d - 1], rz.at[k, d - 1], pz_s.at[e], pz_r.at[k], dev) for d, dev in to_a]

    def reduce_z_sent(k):
        remote(sz.at[k % 2], rz.at[k], pz_s.at[k % 2], pz_r.at[k], to_c).wait_send()

    def ago(k, n, copies):
        if k >= n:
            for copy in copies(k - n):
                copy.wait_send()

    lo, hi = slice(0, LANES), slice(LANES, CHUNK)

    def rs1(k):
        t, e = k % SLOTS, k % 2
        reduce_c(k).wait_recv()
        ago(k, 2, reduce_1)
        for d, _ in to_y:
            v = up(y, d, Y)
            s1a[e, d - 1] = (acc[t, :, :, v, :, lo] + crecv[k % RECEIVED, :, :, v, :, lo].astype(F32)).astype(BF16)
        for d, _ in to_b:
            v = up(b, d, B)
            s1b[e, d - 1] = (acc[t, :, v, :, :, hi] + crecv[k % RECEIVED, :, v, :, :, hi].astype(F32)).astype(BF16)
        for copy in reduce_1(k):
            copy.start()
        acc[t, :, :, y, :, lo] = acc[t, :, :, y, :, lo] + crecv[k % RECEIVED, :, :, y, :, lo].astype(F32)
        acc[t, :, b, :, :, hi] = acc[t, :, b, :, :, hi] + crecv[k % RECEIVED, :, b, :, :, hi].astype(F32)

    def rs2(k):
        t, e = k % SLOTS, k % 2
        for copy in reduce_1(k):
            copy.wait_recv()
        ago(k, 2, reduce_2)

        def total_a(v):
            out = acc[t, :, v, y, :, lo]
            for d, _ in to_y:
                out = out + r1a[k, d - 1, :, v].astype(F32)
            return out

        def total_b(v):
            out = acc[t, :, b, v, :, hi]
            for d, _ in to_b:
                out = out + r1b[k, d - 1, :, v].astype(F32)
            return out

        for d, _ in to_b:
            s2a[e, d - 1] = total_a(up(b, d, B)).astype(BF16)
        for d, _ in to_y:
            s2b[e, d - 1] = total_b(up(y, d, Y)).astype(BF16)
        for copy in reduce_2(k):
            copy.start()
        acc[t, :, b, y, :, lo] = total_a(b)
        acc[t, :, b, y, :, hi] = total_b(y)

    def rs3(k):
        t, e = k % SLOTS, k % 2
        for copy in reduce_2(k):
            copy.wait_recv()
        if k >= 2:
            reduce_z_sent(k - 2)

        def total(v):
            left, right = acc[t, v, b, y, :, lo], acc[t, v, b, y, :, hi]
            for d, _ in to_b:
                left = left + r2a[k, d - 1, v].astype(F32)
            for d, _ in to_y:
                right = right + r2b[k, d - 1, v].astype(F32)
            return jnp.concatenate([left, right], axis=1)

        for d, _ in to_a:
            sz[e, d - 1] = total(up(a, d, A)).astype(BF16)
        for copy in reduce_z(k):
            copy.start()
        acc[t, a, b, y] = total(a)

    def rs4(k):
        t = k % SLOTS
        remote(sz.at[k % 2], rz.at[k], pz_s.at[k % 2], pz_r.at[k], to_c).wait_recv()
        out = acc[t, a, b, y]
        for d, _ in to_a:
            out = out + rz[k, d - 1].astype(F32)
        wout[:, columns(k)] = out

    def bred_c():
        return remote(bt.at[:, :, :, oc], brc, dc_s.at[0], dc_r.at[0], to_c)

    def bred_1():
        return [remote(bsum.at[:, :, up(y, d, Y)], br1.at[d - 1], d1_s.at[d - 1], d1_r.at[d - 1], dev) for d, dev in to_y]

    def bred_2():
        return [remote(bsum.at[:, up(b, d, B), y], br2.at[d - 1], d2_s.at[d - 1], d2_r.at[d - 1], dev) for d, dev in to_b]

    def bred_z():
        return [remote(bsum.at[up(a, d, A), b, y], brz.at[d - 1], dz_s.at[0], dz_r.at[0], dev) for d, dev in to_a]

    def bias_rs0():
        for a_ in range(A):
            for b_ in range(B):
                for y_ in range(Y):
                    for c_ in range(C):
                        block = (((a_ * B + b_) * Y + y_) * C + c_) * rows // LANES
                        bt[a_, b_, y_, c_] = bacc[:, block * LANES : (block + 1) * LANES]
        bred_c().start()

    def bias_rs1():
        bred_c().wait_recv()
        bsum[...] = bt[:, :, :, c] + brc[...]
        for copy in bred_1():
            copy.start()

    def bias_rs2():
        for copy in bred_1():
            copy.wait_recv()
        for d, _ in to_y:
            bsum[:, :, y] = bsum[:, :, y] + br1[d - 1]
        for copy in bred_2():
            copy.start()

    def bias_rs3():
        for copy in bred_2():
            copy.wait_recv()
        for d, _ in to_b:
            bsum[:, b, y] = bsum[:, b, y] + br2[d - 1]
        for copy in bred_z():
            copy.start()

    def bias_rs4():
        remote(brz, brz, dz_s.at[0], dz_r.at[0], to_c).wait_recv()
        out = bsum[a, b, y]
        for d, _ in to_a:
            out = out + brz[d - 1]
        out = jnp.sum(out, axis=0, keepdims=True)
        place = lax.rem((dp * (Y * C) + rep) * rows, LANES)
        mine = jnp.zeros((1, rows), F32)
        for p in range(per):
            mine = jnp.where(place == p * rows, out[:, p * rows : (p + 1) * rows], mine)
        bgrad_out[...] = mine

    def forward(k, parts):
        e = k % 2
        w = jnp.concatenate([wg[k, h].reshape(D, LANES) for h in range(2)], axis=1)
        offset = jnp.concatenate([brow[2 * k + h][0:1] for h in range(2)], axis=1)
        sums = jnp.zeros((8, CHUNK), F32)
        for m in parts:
            preact = jnp.dot(rows_of(m, pool_e, pool_l)[...], w, preferred_element_type=F32) + offset
            squash = jax.nn.sigmoid(preact)
            active = preact * squash
            act[k, m] = active.astype(BF16)
            grad = (ct[e, m].astype(F32) * (squash + active * (1.0 - squash))).astype(BF16)
            rows_of(m, gp_e, gp_l)[:, columns(k)] = grad
            sums = sums + jnp.sum(grad.astype(F32).reshape(local // 8, 8, CHUNK), axis=0)
        bacc[:, columns(k)] = sums if parts[0] == 0 else bacc[:, columns(k)] + sums

    def weight_term(k, which):
        left = pool_t[:, which].reshape(plane, N)
        right = jnp.concatenate([gp_e[:, columns(k)], gp_l[:, columns(k)]], axis=0)
        return jnp.dot(left, right, preferred_element_type=F32).reshape(A, B, Y, rows, CHUNK)

    def forward_region(k):
        gather_c(k, False).wait_recv()
        cot_load(k).wait()
        if not isinstance(k, int) or k + 1 < chunks:
            cot_load(k + 1).start()

    def weight_region(k):
        if k >= 2:
            reduce_c(k - 2).wait_send()

    def weight_other(k):
        csend[k % 2] = weight_term(k, oc).astype(BF16)

    def weight_own(k):
        acc[k % SLOTS] = weight_term(k, c)

    whole = list(range(batches))

    regions = [(0, None), (None, 0), (1, None), (None, 1), (2, None)]
    regions += [(k, k - 1) for k in range(3, chunks - 1)]
    regions += [(None, chunks - 2), (chunks - 1, None), (None, chunks - 1)]
    plan = [
        (lambda _: bias_rs0(), {0: 11}),
        (lambda _: bias_rs1(), {0: 11.5}),
        (ag2, {1: 0, 2: 1, 3: 2, 4: 3, 5: 5}),
        (ag1, {3: 0, 4: 1, 5: 3}),
        (ag3, {1: 1, 2: 3, 3: 4, 4: 5, 5: 6}),
        (at3, {6: 7, 7: 8}),
        (atz, {6: 0, 7: 4}),
        (rs4, {0: 11, 1: 12}),
        (rs3, {0: 8.5, 1: 9, 2: 10, 3: 11, 4: 12}),
        (rs2, {0: 7, 1: 7.5, 2: 8, 3: 9, 4: 10, 5: 11.5}),
        (rs1, {0: 5.5, 1: 6, 2: 6.5, 3: 7, 4: 8, 5: 9, 6: 10, 7: 12}),
    ]

    def ahead_of(at):
        return [(stage, k) for stage, when in plan for k, ahead in when.items() if ahead == at]

    def opening(j, carry):
        for place in range(2):
            for step in range(2):
                for stage, k in ahead_of(2 * step + place):
                    pl.when(j == step)(functools.partial(stage, k))
            if place == 0:
                forward_region(j)
                region(lambda: forward(j, whole))
            else:
                region(lambda: weight_other(j))
                reduce_c(j).start()
                region(lambda: weight_own(j))
        return carry

    lax.fori_loop(0, 2, opening, 0)
    for at, (f, w) in enumerate(regions):
        if at < 4:
            continue
        for stage, k in ahead_of(at):
            stage(k)
        if f is not None:
            forward_region(f)
        if w is not None:
            weight_region(w)
        merged = f is not None and w is not None

        @region
        def _(f=f, w=w, merged=merged):
            if f is not None:
                forward(f, whole[:1] if merged else whole)
            if w is not None:
                weight_other(w)

        if w is not None:
            reduce_c(w).start()
            for stage, k in ahead_of(at + 0.5):
                stage(k)

            @region
            def _(f=f, w=w, merged=merged):
                if merged:
                    forward(f, whole[1:])
                weight_own(w)

    for stage, k in ahead_of(len(regions)):
        stage(k)

    def feature_grad(i):
        n, m = lax.div(i, first), lax.rem(i, first)
        part, cols = pl.ds(pl.multiple_of(m * local, local), local), pl.ds(pl.multiple_of(n * wide, wide), wide)
        pool_e[part, cols] = feature_tile(dims, wg, gp_e, adj_e, scale_e, local, n, m)

    late = [
        (rs2, {6: 0, 7: 2}),
        (lambda _: bias_rs2(), {0: 1}),
        (lambda _: bias_rs3(), {0: 3}),
        (rs3, {5: 1, 6: 3, 7: 4}),
        (rs4, {2: 0, 3: 1, 4: 3, 5: 5, 6: 7, 7: 7}),
        (lambda _: bias_rs4(), {0: 7}),
    ]

    def last(i, carry):
        pl.when(i >= 0)(lambda: feature_grad(i))
        for stage, when in late:
            for k, at in when.items():
                pl.when(i == at)(functools.partial(stage, k))
        return carry

    lax.fori_loop(0, A * first, last, 0)

    for k in (chunks - 2, chunks - 1):
        for copy in [reduce_c(k)] + reduce_1(k) + reduce_2(k):
            copy.wait_send()
        reduce_z_sent(k)

    def drained(ref, sem, dev):
        remote(ref, ref, sem, sem, dev).wait_send()

    plain, turned = slice(0, LAST_GATHERED[0]), slice(LAST_GATHERED[0], chunks)
    drained(wg.at[plain, :, : A - 1, b, y, c], gz_s.at[0], to_c)
    drained(wg.at[turned, :, : A - 1, :, :, c], gz_s.at[1], to_c)
    for d, dev in to_b:
        drained(wg.at[plain, 0, :, b, y, c], g1a_s.at[0, d - 1], dev)
        drained(wg.at[plain, 1, :, b, :, c], g2b_s.at[0, d - 1], dev)
        drained(wg.at[turned, 0, a, b, y, c], g1a_s.at[1, d - 1], dev)
        drained(wg.at[turned, 1, a, b, :, c], g2b_s.at[1, d - 1], dev)
    for d, dev in to_y:
        drained(wg.at[plain, 1, :, b, y, c], g1b_s.at[0, d - 1], dev)
        drained(wg.at[plain, 0, :, :, y, c], g2a_s.at[0, d - 1], dev)
        drained(wg.at[turned, 1, a, b, y, c], g1b_s.at[1, d - 1], dev)
        drained(wg.at[turned, 0, a, :, y, c], g2a_s.at[1, d - 1], dev)
    drained(wg.at[:, :, :, :, :, c], gc_s.at[0], to_c)
    drained(bb.at[: A - 1, b, y, c], bz_s.at[0], to_c)
    for d, dev in to_b:
        bias_1(d, dev, True).wait_send()
    for d, dev in to_y:
        bias_2(d, dev, True).wait_send()
    bias_c(True).wait_send()
    for copy in [bred_c()] + bred_1() + bred_2():
        copy.wait_send()
    drained(brz, dz_s.at[0], to_c)


def per_device(dims, features, cotangent, neighbours, segments, live, weight, bias):
    A, B, Y, C = dims
    batches, local, D = features.shape
    rows = weight.shape[0]
    N = batches * local
    N_l = LATE * local
    N_e = N - N_l
    chunks = D // CHUNK
    groups = A * B * Y
    wide = D // A
    neighbours = jnp.swapaxes(neighbours, 1, 2)
    any_spec = pl.BlockSpec(memory_space=pl.ANY)
    vmem, dma = pltpu.VMEM, pltpu.SemaphoreType.DMA
    scratch = [
        vmem((N_e, D), BF16),
        vmem((N_l, D), BF16),
        vmem((N_e // SLOT, SLOT, SLOT), BF16),
        vmem((N_e, SLOT), F32),
        vmem((groups, C, rows, N), BF16),
        vmem((2, batches, local, CHUNK), BF16),
        vmem((SLOTS, A, B, Y, rows, CHUNK), F32),
        vmem((2, A, B, Y, rows, CHUNK), BF16),
        vmem((RECEIVED, A, B, Y, rows, CHUNK), BF16),
        vmem((2, Y - 1, A, B, rows, LANES), BF16),
        vmem((2, B - 1, A, Y, rows, LANES), BF16),
        vmem((2, B - 1, A, rows, LANES), BF16),
        vmem((2, Y - 1, A, rows, LANES), BF16),
        vmem((2, A - 1, rows, CHUNK), BF16),
        vmem((chunks, Y - 1, A, B, rows, LANES), BF16),
        vmem((chunks, B - 1, A, Y, rows, LANES), BF16),
        vmem((chunks, B - 1, A, rows, LANES), BF16),
        vmem((chunks, Y - 1, A, rows, LANES), BF16),
        vmem((chunks, A - 1, rows, CHUNK), BF16),
        vmem(neighbours.shape, jnp.int32),
        vmem(segments.shape, jnp.int32),
        vmem(live.shape, jnp.int32),
        vmem((A, B, Y, C, 8, LANES), F32),
        vmem((D // LANES, 8, LANES), F32),
        vmem((8, D), F32),
        vmem((A, B, Y, C, 8, LANES), F32),
        vmem((A, B, Y, 8, LANES), F32),
        vmem((A, B, Y, 8, LANES), F32),
        vmem((Y - 1, A, B, 8, LANES), F32),
        vmem((B - 1, A, 8, LANES), F32),
        vmem((A - 1, 8, LANES), F32),
        dma((4 + batches,)),
        dma((2,)),
    ]
    scratch_tail = [dma((Y - 1,)), dma((B - 1,))]
    for sent, received in (
        ((2,), (chunks,)),
        ((2, B - 1), (chunks, B - 1)),
        ((2, Y - 1), (chunks, Y - 1)),
        ((2, Y - 1), (chunks, Y - 1)),
        ((2, B - 1), (chunks, B - 1)),
        ((1,), (chunks,)),
        ((2,), (chunks,)),
        ((2, Y - 1), (chunks, Y - 1)),
        ((2, B - 1), (chunks, B - 1)),
        ((2, B - 1), (chunks, B - 1)),
        ((2, Y - 1), (chunks, Y - 1)),
        ((2,), (chunks,)),
        (None, scratch_tail),
        ((1,), (1,)),
        ((B - 1,), (B - 1,)),
        ((Y - 1,), (Y - 1,)),
        ((1,), (1,)),
        ((1,), (1,)),
        ((Y - 1,), (Y - 1,)),
        ((B - 1,), (B - 1,)),
        ((1,), (1,)),
    ):
        scratch += received if sent is None else [dma(sent), dma(received)]
    vmem_spec = pl.BlockSpec(memory_space=pltpu.VMEM)
    kept = [
        vmem((chunks, batches, local, CHUNK), BF16),
        vmem((chunks, 2, A, B, Y, C, rows, LANES), BF16),
        vmem((N_l, D), BF16),
        vmem((N_e, D), BF16),
        vmem((N_l // SLOT, SLOT, SLOT), BF16),
        vmem((N_l, SLOT), F32),
        vmem((rows, D), F32),
        vmem((1, rows), F32),
    ]
    kept_arrays = pl.pallas_call(
        functools.partial(kernel, dims),
        out_shape=kept,
        in_specs=[any_spec] * 6 + [vmem_spec],
        out_specs=[vmem_spec] * len(kept),
        scratch_shapes=scratch,
        compiler_params=pltpu.CompilerParams(
            collective_id=0, has_side_effects=True, vmem_limit_bytes=39 * 2**20
        ),
        cost_estimate=pl.CostEstimate(
            flops=6 * N * D * D, bytes_accessed=8 * N * D, transcendentals=N * D
        ),
    )(features, cotangent, neighbours, segments, live, weight, bias.reshape(1, rows))
    act, fgrad, wgrad, bgrad = pl.pallas_call(
        functools.partial(finish, dims),
        out_shape=[
            jax.ShapeDtypeStruct(features.shape, BF16),
            jax.ShapeDtypeStruct(features.shape, BF16),
            jax.ShapeDtypeStruct(weight.shape, F32),
            jax.ShapeDtypeStruct((1, rows), F32),
        ],
        in_specs=[vmem_spec] * len(kept),
        out_specs=[any_spec] * 3 + [vmem_spec],
        scratch_shapes=[
            vmem((A * LATE, local, wide), BF16),
            dma((1,)), dma((batches - LATE,)), dma((A * LATE,)), dma((1,)),
        ],
        compiler_params=pltpu.CompilerParams(vmem_limit_bytes=8 * 2**20),
    )(
        *[pltpu.with_memory_space_constraint(x, pltpu.VMEM) for x in kept_arrays],
    )
    return act, fgrad, wgrad, bgrad.reshape(rows)


def solution(mesh):
    both = ("dp", "rep")
    dims = split_axes(mesh.shape["dp"], mesh.shape["rep"])
    return jax.shard_map(
        functools.partial(per_device, dims),
        mesh=mesh,
        in_specs=(
            P(None, both, None), P(None, both, None), P(None, both, None),
            P(None, both), P(None, both), P(both, None), P(both),
        ),
        out_specs=(P(None, both, None), P(None, both, None), P(both, None), P(both)),
        check_vma=False,
    )
```

```python
import functools

import jax
import jax.numpy as jnp
from jax import lax
from jax.experimental import pallas as pl
from jax.experimental.pallas import tpu as pltpu
from jax.sharding import PartitionSpec as P

SLOT = 128
LANES = 128
CHUNK = 256
MESH = pl.DeviceIdType.MESH
F32, BF16 = jnp.float32, jnp.bfloat16
ENHANCE = 1.0
LATE = 1
SLOTS, RECEIVED = 7, 6
LAST_GATHERED = (6, 7)


def split_axes(dp, rep):
    b = 2 ** ((dp.bit_length() - 1) // 2)
    return dp // b, b, rep // 2, 2


def feature_tile(dims, wg, gp, adj_t, scale, local, n, m):
    A, B, Y, C = dims
    chunks, rows = wg.shape[0], wg.shape[-2]
    wide = B * Y * C * rows
    slots = local // SLOT
    base = m * local if isinstance(m, int) else pl.multiple_of(m * local, local)
    w = jnp.concatenate([wg[k, h, n].reshape(wide, LANES) for k in range(chunks) for h in range(2)], axis=1)
    grad = lax.dot_general(gp[pl.ds(base, local), :], w, (((1,), (1,)), ((), ())), preferred_element_type=F32)
    grad = grad * jnp.concatenate([scale[pl.ds(base, local), :]] * (wide // LANES), axis=1)
    high = grad.astype(BF16)
    low = (grad - high.astype(F32)).astype(BF16)
    tiles = []
    for q in range(slots):
        left = adj_t[m * slots + q]
        part = slice(q * SLOT, (q + 1) * SLOT)
        right = jnp.concatenate([high[part], low[part]], axis=0)
        out = jnp.dot(jnp.concatenate([left, left], axis=1), right, preferred_element_type=F32)
        tiles.append(out.astype(BF16))
    return jnp.concatenate(tiles, axis=0)


def finish(
    dims, act, wg, gp, done, adj_t, scale, wout, bgrad_in, act_out, fgrad_out, wgrad_out, bgrad_out,
    fout, act_sem, done_sem, fout_sem, wout_sem,
):
    batches, local, D = fgrad_out.shape
    blocks, wide, early = dims[0], D // dims[0], batches - LATE

    def store(i):
        n, m = lax.div(i, LATE), early + lax.rem(i, LATE)
        cols = pl.ds(pl.multiple_of(n * wide, wide), wide)
        return pltpu.make_async_copy(fout.at[i], fgrad_out.at[m, :, cols], fout_sem.at[i])

    kept = [pltpu.make_async_copy(wout, wgrad_out, wout_sem.at[0])]
    for m in range(early):
        kept.append(pltpu.make_async_copy(done.at[pl.ds(m * local, local)], fgrad_out.at[m], done_sem.at[m]))
    for copy in kept:
        copy.start()
    for k in range(act.shape[0]):
        pltpu.make_async_copy(act.at[k], act_out.at[:, :, pl.ds(k * CHUNK, CHUNK)], act_sem.at[0]).start()
    bgrad_out[...] = bgrad_in[...]

    def step(i, carry):
        fout[i] = feature_tile(dims, wg, gp, adj_t, scale, local, lax.div(i, LATE), lax.rem(i, LATE))
        store(i).start()
        return carry

    lax.fori_loop(0, blocks * LATE, step, 0)
    for i in range(blocks * LATE):
        store(i).wait()
    pltpu.make_async_copy(act, act, act_sem.at[0]).wait()
    for copy in kept:
        copy.wait()


def kernel(
    dims, feat, cot, nbr, seg, live, weight, bias, act, wg, gp_l, pool_e, adj_l, scale_l, wout, bgrad_out,
    gp_e, pool_l, adj_e, scale_e, pool_t, ct, acc, csend, crecv, s1a, s1b, s2a, s2b, sz, r1a, r1b, r2a, r2b, rz,
    nbuf, sbuf, lbuf, bb, brow, bacc, bt, bsum, brc, br1, br2, brz,
    in_sem, ct_sem,
    gz_s, gz_r, g1a_s, g1a_r, g1b_s, g1b_r, g2a_s, g2a_r, g2b_s, g2b_r, gc_s, gc_r,
    rc_s, rc_r, p1a_s, p1a_r, p1b_s, p1b_r, p2a_s, p2a_r, p2b_s, p2b_r, pz_s, pz_r,
    ha_r, hb_r, bz_s, bz_r, b1_s, b1_r, b2_s, b2_r, bc_s, bc_r, dc_s, dc_r, d1_s, d1_r, d2_s, d2_r, dz_s, dz_r,
):
    A, B, Y, C = dims
    batches, local, D = feat.shape
    rows = weight.shape[0]
    slots = local // SLOT
    N = batches * local
    chunks = D // CHUNK
    groups = A * B * Y
    plane = groups * rows
    first = batches - LATE
    wide = D // A

    dp, rep = lax.axis_index("dp"), lax.axis_index("rep")
    a, b, y, c = lax.div(dp, B), lax.rem(dp, B), lax.div(rep, C), lax.rem(rep, C)
    oc = 1 - c

    def device(a_, b_, y_, c_):
        return (a_ * B + b_, y_ * C + c_)

    def columns(k):
        return pl.ds(k * CHUNK if isinstance(k, int) else pl.multiple_of(k * CHUNK, CHUNK), CHUNK)

    def of(m, ref_e, ref_l):
        return (ref_e, m) if m < first else (ref_l, m - first)

    def rows_of(m, ref_e, ref_l):
        ref, at = of(m, ref_e, ref_l)
        return ref.at[pl.ds(at * local, local)]

    def up(v, d, n):
        return lax.rem(v + d, n)

    def down(v, d, n):
        return lax.rem(v + n - d, n)

    to_a = [(d, device(up(a, d, A), b, y, c)) for d in range(1, A)]
    to_b = [(d, device(a, up(b, d, B), y, c)) for d in range(1, B)]
    to_y = [(d, device(a, b, up(y, d, Y), c)) for d in range(1, Y)]
    to_c = device(a, b, y, oc)

    def remote(src, dst, ssem, rsem, dev):
        return pltpu.make_async_remote_copy(
            src_ref=src, dst_ref=dst, send_sem=ssem, recv_sem=rsem, device_id=dev, device_id_type=MESH
        )

    weight_loads = [
        pltpu.make_async_copy(
            weight.at[:, pl.ds((2 * k + h) * LANES, LANES)], wg.at[k, h, a, b, y, c], in_sem.at[0]
        )
        for k in range(chunks)
        for h in range(2)
    ]
    side_loads = [
        pltpu.make_async_copy(nbr, nbuf, in_sem.at[1]),
        pltpu.make_async_copy(seg, sbuf, in_sem.at[2]),
        pltpu.make_async_copy(live, lbuf, in_sem.at[3]),
    ]
    feat_loads = [
        pltpu.make_async_copy(feat.at[m], rows_of(m, gp_e, gp_l), in_sem.at[4 + m]) for m in range(batches)
    ]
    for copy in weight_loads:
        copy.start()
    for copy in side_loads:
        copy.start()
    for copy in feat_loads:
        copy.start()

    barrier = pltpu.get_barrier_semaphore()
    partners = [dev for _, dev in to_a + to_b + to_y] + [to_c]
    for dev in partners:
        pl.semaphore_signal(barrier, inc=1, device_id=dev, device_id_type=MESH)

    def cot_load(k):
        return pltpu.make_async_copy(cot.at[:, :, columns(k)], ct.at[k % 2], ct_sem.at[k % 2])

    pl.semaphore_wait(barrier, len(partners))

    def gather_z(k, d, dev):
        ref = wg.at[k, :, a, b, y, c]
        return remote(ref, ref, gz_s.at[0], gz_r.at[k], dev)

    def gather_1(k, mine):
        out = []
        for d, dev in to_b:
            ref = wg.at[k, 0, :, b if mine else down(b, d, B), y, c]
            out.append(remote(ref, ref, g1a_s.at[0, d - 1], g1a_r.at[k, d - 1], dev))
        for d, dev in to_y:
            ref = wg.at[k, 1, :, b, y if mine else down(y, d, Y), c]
            out.append(remote(ref, ref, g1b_s.at[0, d - 1], g1b_r.at[k, d - 1], dev))
        return out

    def gather_2(k, mine):
        out = []
        for d, dev in to_y:
            ref = wg.at[k, 0, :, :, y if mine else down(y, d, Y), c]
            out.append(remote(ref, ref, g2a_s.at[0, d - 1], g2a_r.at[k, d - 1], dev))
        for d, dev in to_b:
            ref = wg.at[k, 1, :, b if mine else down(b, d, B), :, c]
            out.append(remote(ref, ref, g2b_s.at[0, d - 1], g2b_r.at[k, d - 1], dev))
        return out

    def turned_1(k, mine):
        out = []
        for d, dev in to_b:
            ref = wg.at[k, 0, a, b if mine else down(b, d, B), y, c]
            out.append(remote(ref, ref, g1a_s.at[1, d - 1], g1a_r.at[k, d - 1], dev))
        for d, dev in to_y:
            ref = wg.at[k, 1, a, b, y if mine else down(y, d, Y), c]
            out.append(remote(ref, ref, g1b_s.at[1, d - 1], g1b_r.at[k, d - 1], dev))
        return out

    def turned_2(k, mine):
        out = []
        for d, dev in to_y:
            ref = wg.at[k, 0, a, :, y if mine else down(y, d, Y), c]
            out.append(remote(ref, ref, g2a_s.at[1, d - 1], g2a_r.at[k, d - 1], dev))
        for d, dev in to_b:
            ref = wg.at[k, 1, a, b if mine else down(b, d, B), :, c]
            out.append(remote(ref, ref, g2b_s.at[1, d - 1], g2b_r.at[k, d - 1], dev))
        return out

    def turned_z(k):
        out = []
        ref = wg.at[k, :, a, :, :, c]
        for d, dev in to_a:
            out.append(remote(ref, ref, gz_s.at[1], gz_r.at[k], dev))
        return out

    def half_step(mine):
        out = []
        for d, dev in to_y:
            ref = wg.at[0, 0, :, b, y if mine else down(y, d, Y), c]
            out.append(remote(ref, ref, g2a_s.at[0, d - 1], ha_r.at[d - 1], dev))
        for d, dev in to_b:
            ref = wg.at[0, 1, :, b if mine else down(b, d, B), y, c]
            out.append(remote(ref, ref, g2b_s.at[0, d - 1], hb_r.at[d - 1], dev))
        return out

    def ag2a():
        for copy in half_step(True):
            copy.start()

    def ag2b():
        for copy in gather_1(0, False):
            copy.wait_recv()
        for d, dev in to_y:
            for e in range(1, B):
                ref = wg.at[0, 0, :, down(b, e, B), y, c]
                remote(ref, ref, g2a_s.at[0, d - 1], g2a_r.at[0, d - 1], dev).start()
        for d, dev in to_b:
            for e in range(1, Y):
                ref = wg.at[0, 1, :, b, down(y, e, Y), c]
                remote(ref, ref, g2b_s.at[0, d - 1], g2b_r.at[0, d - 1], dev).start()

    def ag3_first():
        for copy in half_step(False):
            copy.wait_recv()
        for d, dev in to_y:
            ref = wg.at[0, 0, :, : B - 1, y, c]
            remote(ref, ref, g2a_s.at[0, d - 1], g2a_r.at[0, d - 1], dev).wait_recv()
        for d, dev in to_b:
            ref = wg.at[0, 1, :, b, : Y - 1, c]
            remote(ref, ref, g2b_s.at[0, d - 1], g2b_r.at[0, d - 1], dev).wait_recv()
        gather_c(0, True).start()

    def gather_c(k, mine):
        ref = wg.at[k, :, :, :, :, c if mine else oc]
        return remote(ref, ref, gc_s.at[0], gc_r.at[k], to_c)

    def region(fn):
        pl.when(dp >= 0)(fn)

    def bias_z(d, dev):
        ref = bb.at[a, b, y, c]
        return remote(ref, ref, bz_s.at[0], bz_r.at[0], dev)

    def bias_1(d, dev, mine):
        ref = bb.at[:, b if mine else down(b, d, B), y, c]
        return remote(ref, ref, b1_s.at[d - 1], b1_r.at[d - 1], dev)

    def bias_2(d, dev, mine):
        ref = bb.at[:, :, y if mine else down(y, d, Y), c]
        return remote(ref, ref, b2_s.at[d - 1], b2_r.at[d - 1], dev)

    def bias_c(mine):
        ref = bb.at[:, :, :, c if mine else oc]
        return remote(ref, ref, bc_s.at[0], bc_r.at[0], to_c)

    def ag1(k):
        every = wg.at[k, :, : A - 1, b, y, c]
        remote(every, every, gz_s.at[0], gz_r.at[k], to_c).wait_recv()
        for copy in gather_1(k, True):
            copy.start()

    def ag2(k):
        for copy in gather_1(k, False):
            copy.wait_recv()
        for copy in gather_2(k, True):
            copy.start()

    def ag3(k):
        for copy in gather_2(k, False):
            copy.wait_recv()
        gather_c(k, True).start()

    def at1(k):
        for copy in turned_1(k, True):
            copy.start()

    def at2(k):
        for copy in turned_1(k, False):
            copy.wait_recv()
        for copy in turned_2(k, True):
            copy.start()

    def atz(k):
        for copy in turned_2(k, False):
            copy.wait_recv()
        for copy in turned_z(k):
            copy.start()

    def at3(k):
        every = wg.at[k, :, : A - 1, :, :, c]
        remote(every, every, gz_s.at[1], gz_r.at[k], to_c).wait_recv()
        gather_c(k, True).start()

    def bias_ag1():
        every = bb.at[: A - 1, b, y, c]
        remote(every, every, bz_s.at[0], bz_r.at[0], to_c).wait_recv()
        for d, dev in to_b:
            bias_1(d, dev, True).start()

    def bias_ag2():
        for d, dev in to_b:
            bias_1(d, dev, False).wait_recv()
        for d, dev in to_y:
            bias_2(d, dev, True).start()

    def bias_ag3():
        for d, dev in to_y:
            bias_2(d, dev, False).wait_recv()
        bias_c(True).start()

    def agz(k):
        for d, dev in to_a:
            gather_z(k, d, dev).start()

    def bias_agz():
        spread = lax.rem(lax.broadcasted_iota(jnp.int32, (rows, LANES), 1), rows)
        spread = (spread == lax.broadcasted_iota(jnp.int32, (rows, LANES), 0)).astype(F32).astype(BF16)
        own_bias = jnp.broadcast_to(bias[...], (8, rows))
        bb[a, b, y, c] = jnp.dot(own_bias, spread, preferred_element_type=F32)
        for d, dev in to_a:
            bias_z(d, dev).start()

    pltpu.make_async_copy(weight, weight, in_sem.at[0]).wait()
    bias_agz()
    agz(0)
    for k in LAST_GATHERED:
        at1(k)

    for copy in side_loads:
        copy.wait()
    cot_load(0).start()
    bacc[...] = jnp.zeros_like(bacc)

    def pooling(m, q):
        here = pl.multiple_of(q * SLOT, SLOT)
        flat = pl.multiple_of((m * slots + q) * SLOT, SLOT)
        listed = nbuf[m, :, pl.ds(here, SLOT)].astype(F32).astype(BF16)
        lane = lax.broadcasted_iota(jnp.int32, (SLOT, SLOT), 1)
        sub = lax.broadcasted_iota(jnp.int32, (SLOT, SLOT), 0)
        position = sub.astype(F32).astype(BF16)
        counted = jnp.zeros((SLOT, SLOT), BF16)
        for j in range(listed.shape[0]):
            counted = counted + jnp.where(listed[j : j + 1, :] == position, jnp.bfloat16(1), jnp.bfloat16(0))
        counted = counted.astype(F32).T
        ids, alive = sbuf[m : m + 1, pl.ds(here, SLOT)], lbuf[m : m + 1, pl.ds(here, SLOT)]
        along = jnp.where(alive > 0, ids, -1)
        down_ = jnp.broadcast_to(jnp.where(alive > 0, ids, -2), (SLOT, SLOT)).T
        adjacency = jnp.where(down_ == along, counted, 0.0)
        degree = jnp.sum(adjacency, axis=1, keepdims=True)
        factor = jnp.where(down_ >= 0, 1.0 / (degree + 1.0), 0.0)
        adjacency = jnp.where(lane == sub, (1.0 + ENHANCE) * (adjacency + 1.0), adjacency)
        adj, at = of(m, adj_e, adj_l)
        adj[at * slots + q] = adjacency.T.astype(BF16)
        rows_of(m, scale_e, scale_l)[pl.ds(here, SLOT), :] = factor
        block = rows_of(m, gp_e, gp_l)[pl.ds(here, SLOT), :]
        pooled = jnp.dot(adjacency.astype(BF16), block, preferred_element_type=F32)
        pooled = (pooled * jnp.concatenate([factor] * (D // SLOT), axis=1)).astype(BF16)
        rows_of(m, pool_e, pool_l)[pl.ds(here, SLOT), :] = pooled
        pool_t[:, :, :, pl.ds(flat, SLOT)] = pooled.T.reshape(groups, C, rows, SLOT)

    early = {
        2: [lambda: agz(1)],
        4: [bias_ag1, lambda: ag1(0)],
        6: [ag2a, lambda: agz(2)],
        8: [lambda: at2(6), lambda: at2(7)],
        10: [bias_ag2, ag2b, lambda: ag1(1), lambda: agz(3)],
    }
    for m in range(batches):
        feat_loads[m].wait()

        def step(q, carry, m=m):
            pooling(m, q)
            for at, events in early.items():
                if m * slots <= at < (m + 1) * slots:

                    @pl.when(q == at - m * slots)
                    def _(events=events):
                        for event in events:
                            event()

            return carry

        lax.fori_loop(0, slots, step, 0)

    agz(4)
    ag1(2)
    bias_ag3()
    ag3_first()
    agz(5)

    bias_c(False).wait_recv()
    tiles = bb[...].reshape(groups * C, 8, LANES)
    per = LANES // rows
    owner = lax.div(lax.broadcasted_iota(jnp.int32, (1, LANES), 1), rows)
    for j in range(D // LANES):
        row = jnp.zeros((1, LANES), F32)
        for p in range(per):
            row = jnp.where(owner == p, tiles[j * per + p, 0:1, :], row)
        brow[j] = jnp.broadcast_to(row, (8, LANES))

    def reduce_c(k):
        return remote(csend.at[k % 2], crecv.at[k % RECEIVED], rc_s.at[k % 2], rc_r.at[k], to_c)

    def reduce_1(k):
        e = k % 2
        out_a = [
            remote(s1a.at[e, d - 1], r1a.at[k, d - 1], p1a_s.at[e, d - 1], p1a_r.at[k, d - 1], dev) for d, dev in to_y
        ]
        out_b = [
            remote(s1b.at[e, d - 1], r1b.at[k, d - 1], p1b_s.at[e, d - 1], p1b_r.at[k, d - 1], dev) for d, dev in to_b
        ]
        return out_a + out_b

    def reduce_2(k):
        e = k % 2
        out_a = [
            remote(s2a.at[e, d - 1], r2a.at[k, d - 1], p2a_s.at[e, d - 1], p2a_r.at[k, d - 1], dev) for d, dev in to_b
        ]
        out_b = [
            remote(s2b.at[e, d - 1], r2b.at[k, d - 1], p2b_s.at[e, d - 1], p2b_r.at[k, d - 1], dev) for d, dev in to_y
        ]
        return out_a + out_b

    def reduce_z(k):
        e = k % 2
        return [remote(sz.at[e, d - 1], rz.at[k, d - 1], pz_s.at[e], pz_r.at[k], dev) for d, dev in to_a]

    def reduce_z_sent(k):
        remote(sz.at[k % 2], rz.at[k], pz_s.at[k % 2], pz_r.at[k], to_c).wait_send()

    def ago(k, n, copies):
        if k >= n:
            for copy in copies(k - n):
                copy.wait_send()

    lo, hi = slice(0, LANES), slice(LANES, CHUNK)

    def rs1(k):
        t, e = k % SLOTS, k % 2
        reduce_c(k).wait_recv()
        ago(k, 2, reduce_1)
        for d, _ in to_y:
            v = up(y, d, Y)
            s1a[e, d - 1] = (acc[t, :, :, v, :, lo] + crecv[k % RECEIVED, :, :, v, :, lo].astype(F32)).astype(BF16)
        for d, _ in to_b:
            v = up(b, d, B)
            s1b[e, d - 1] = (acc[t, :, v, :, :, hi] + crecv[k % RECEIVED, :, v, :, :, hi].astype(F32)).astype(BF16)
        for copy in reduce_1(k):
            copy.start()
        acc[t, :, :, y, :, lo] = acc[t, :, :, y, :, lo] + crecv[k % RECEIVED, :, :, y, :, lo].astype(F32)
        acc[t, :, b, :, :, hi] = acc[t, :, b, :, :, hi] + crecv[k % RECEIVED, :, b, :, :, hi].astype(F32)

    def rs2(k):
        t, e = k % SLOTS, k % 2
        for copy in reduce_1(k):
            copy.wait_recv()
        ago(k, 2, reduce_2)

        def total_a(v):
            out = acc[t, :, v, y, :, lo]
            for d, _ in to_y:
                out = out + r1a[k, d - 1, :, v].astype(F32)
            return out

        def total_b(v):
            out = acc[t, :, b, v, :, hi]
            for d, _ in to_b:
                out = out + r1b[k, d - 1, :, v].astype(F32)
            return out

        for d, _ in to_b:
            s2a[e, d - 1] = total_a(up(b, d, B)).astype(BF16)
        for d, _ in to_y:
            s2b[e, d - 1] = total_b(up(y, d, Y)).astype(BF16)
        for copy in reduce_2(k):
            copy.start()
        acc[t, :, b, y, :, lo] = total_a(b)
        acc[t, :, b, y, :, hi] = total_b(y)

    def rs3(k):
        t, e = k % SLOTS, k % 2
        for copy in reduce_2(k):
            copy.wait_recv()
        if k >= 2:
            reduce_z_sent(k - 2)

        def total(v):
            left, right = acc[t, v, b, y, :, lo], acc[t, v, b, y, :, hi]
            for d, _ in to_b:
                left = left + r2a[k, d - 1, v].astype(F32)
            for d, _ in to_y:
                right = right + r2b[k, d - 1, v].astype(F32)
            return jnp.concatenate([left, right], axis=1)

        for d, _ in to_a:
            sz[e, d - 1] = total(up(a, d, A)).astype(BF16)
        for copy in reduce_z(k):
            copy.start()
        acc[t, a, b, y] = total(a)

    def rs4(k):
        t = k % SLOTS
        remote(sz.at[k % 2], rz.at[k], pz_s.at[k % 2], pz_r.at[k], to_c).wait_recv()
        out = acc[t, a, b, y]
        for d, _ in to_a:
            out = out + rz[k, d - 1].astype(F32)
        wout[:, columns(k)] = out

    def bred_c():
        return remote(bt.at[:, :, :, oc], brc, dc_s.at[0], dc_r.at[0], to_c)

    def bred_1():
        return [remote(bsum.at[:, :, up(y, d, Y)], br1.at[d - 1], d1_s.at[d - 1], d1_r.at[d - 1], dev) for d, dev in to_y]

    def bred_2():
        return [remote(bsum.at[:, up(b, d, B), y], br2.at[d - 1], d2_s.at[d - 1], d2_r.at[d - 1], dev) for d, dev in to_b]

    def bred_z():
        return [remote(bsum.at[up(a, d, A), b, y], brz.at[d - 1], dz_s.at[0], dz_r.at[0], dev) for d, dev in to_a]

    def bias_rs0():
        for a_ in range(A):
            for b_ in range(B):
                for y_ in range(Y):
                    for c_ in range(C):
                        block = (((a_ * B + b_) * Y + y_) * C + c_) * rows // LANES
                        bt[a_, b_, y_, c_] = bacc[:, block * LANES : (block + 1) * LANES]
        bred_c().start()

    def bias_rs1():
        bred_c().wait_recv()
        bsum[...] = bt[:, :, :, c] + brc[...]
        for copy in bred_1():
            copy.start()

    def bias_rs2():
        for copy in bred_1():
            copy.wait_recv()
        for d, _ in to_y:
            bsum[:, :, y] = bsum[:, :, y] + br1[d - 1]
        for copy in bred_2():
            copy.start()

    def bias_rs3():
        for copy in bred_2():
            copy.wait_recv()
        for d, _ in to_b:
            bsum[:, b, y] = bsum[:, b, y] + br2[d - 1]
        for copy in bred_z():
            copy.start()

    def bias_rs4():
        remote(brz, brz, dz_s.at[0], dz_r.at[0], to_c).wait_recv()
        out = bsum[a, b, y]
        for d, _ in to_a:
            out = out + brz[d - 1]
        out = jnp.sum(out, axis=0, keepdims=True)
        place = lax.rem((dp * (Y * C) + rep) * rows, LANES)
        mine = jnp.zeros((1, rows), F32)
        for p in range(per):
            mine = jnp.where(place == p * rows, out[:, p * rows : (p + 1) * rows], mine)
        bgrad_out[...] = mine

    def forward(k, parts):
        e = k % 2
        w = jnp.concatenate([wg[k, h].reshape(D, LANES) for h in range(2)], axis=1)
        offset = jnp.concatenate([brow[2 * k + h][0:1] for h in range(2)], axis=1)
        sums = jnp.zeros((8, CHUNK), F32)
        for m in parts:
            preact = jnp.dot(rows_of(m, pool_e, pool_l)[...], w, preferred_element_type=F32) + offset
            squash = jax.nn.sigmoid(preact)
            active = preact * squash
            act[k, m] = active.astype(BF16)
            grad = (ct[e, m].astype(F32) * (squash + active * (1.0 - squash))).astype(BF16)
            rows_of(m, gp_e, gp_l)[:, columns(k)] = grad
            sums = sums + jnp.sum(grad.astype(F32).reshape(local // 8, 8, CHUNK), axis=0)
        bacc[:, columns(k)] = sums if parts[0] == 0 else bacc[:, columns(k)] + sums

    def weight_term(k, which):
        left = pool_t[:, which].reshape(plane, N)
        right = jnp.concatenate([gp_e[:, columns(k)], gp_l[:, columns(k)]], axis=0)
        return jnp.dot(left, right, preferred_element_type=F32).reshape(A, B, Y, rows, CHUNK)

    def forward_region(k):
        gather_c(k, False).wait_recv()
        cot_load(k).wait()
        if not isinstance(k, int) or k + 1 < chunks:
            cot_load(k + 1).start()

    def weight_region(k):
        if k >= 2:
            reduce_c(k - 2).wait_send()

    def weight_other(k):
        csend[k % 2] = weight_term(k, oc).astype(BF16)

    def weight_own(k):
        acc[k % SLOTS] = weight_term(k, c)

    whole = list(range(batches))

    regions = [(0, None), (None, 0), (1, None), (None, 1), (2, None)]
    regions += [(k, k - 1) for k in range(3, chunks - 1)]
    regions += [(None, chunks - 2), (chunks - 1, None), (None, chunks - 1)]
    plan = [
        (lambda _: bias_rs0(), {0: 11}),
        (lambda _: bias_rs1(), {0: 11.5}),
        (ag2, {1: 0, 2: 1, 3: 2, 4: 3, 5: 5}),
        (ag1, {3: 0, 4: 1, 5: 3}),
        (ag3, {1: 1, 2: 3, 3: 4, 4: 5, 5: 6}),
        (at3, {6: 7, 7: 8}),
        (atz, {6: 0, 7: 4}),
        (rs4, {0: 11, 1: 12}),
        (rs3, {0: 8.5, 1: 9, 2: 10, 3: 11, 4: 12}),
        (rs2, {0: 7, 1: 7.5, 2: 8, 3: 9, 4: 10, 5: 11.5}),
        (rs1, {0: 5.5, 1: 6, 2: 6.5, 3: 7, 4: 8, 5: 9, 6: 10, 7: 12}),
    ]

    def ahead_of(at):
        return [(stage, k) for stage, when in plan for k, ahead in when.items() if ahead == at]

    def opening(j, carry):
        for place in range(2):
            for step in range(2):
                for stage, k in ahead_of(2 * step + place):
                    pl.when(j == step)(functools.partial(stage, k))
            if place == 0:
                forward_region(j)
                region(lambda: forward(j, whole))
            else:

                @region
                def _():
                    weight_other(j)
                    weight_own(j)

                reduce_c(j).start()
        return carry

    lax.fori_loop(0, 2, opening, 0)
    for at, (f, w) in enumerate(regions):
        if at < 4:
            continue
        for stage, k in ahead_of(at):
            stage(k)
        if f is not None:
            forward_region(f)
        if w is not None:
            weight_region(w)
        merged = f is not None and w is not None

        @region
        def _(f=f, w=w, merged=merged):
            if f is not None:
                forward(f, whole[:1] if merged else whole)
            if w is not None:
                weight_other(w)

        if w is not None:
            reduce_c(w).start()
            for stage, k in ahead_of(at + 0.5):
                stage(k)

            @region
            def _(f=f, w=w, merged=merged):
                if merged:
                    forward(f, whole[1:])
                weight_own(w)

    for stage, k in ahead_of(len(regions)):
        stage(k)

    def feature_grad(i):
        n, m = lax.div(i, first), lax.rem(i, first)
        part, cols = pl.ds(pl.multiple_of(m * local, local), local), pl.ds(pl.multiple_of(n * wide, wide), wide)
        pool_e[part, cols] = feature_tile(dims, wg, gp_e, adj_e, scale_e, local, n, m)

    late = [
        (rs2, {6: 0, 7: 2}),
        (lambda _: bias_rs2(), {0: 1}),
        (lambda _: bias_rs3(), {0: 3}),
        (rs3, {5: 1, 6: 3, 7: 4}),
        (rs4, {2: 0, 3: 1, 4: 3, 5: 5, 6: 7, 7: 7}),
        (lambda _: bias_rs4(), {0: 7}),
    ]

    def last(i, carry):
        pl.when(i >= 0)(lambda: feature_grad(i))
        for stage, when in late:
            for k, at in when.items():
                pl.when(i == at)(functools.partial(stage, k))
        return carry

    lax.fori_loop(0, A * first, last, 0)

    for k in (chunks - 2, chunks - 1):
        for copy in [reduce_c(k)] + reduce_1(k) + reduce_2(k):
            copy.wait_send()
        reduce_z_sent(k)

    def drained(ref, sem, dev):
        remote(ref, ref, sem, sem, dev).wait_send()

    plain, turned = slice(0, LAST_GATHERED[0]), slice(LAST_GATHERED[0], chunks)
    drained(wg.at[plain, :, : A - 1, b, y, c], gz_s.at[0], to_c)
    drained(wg.at[turned, :, : A - 1, :, :, c], gz_s.at[1], to_c)
    for d, dev in to_b:
        drained(wg.at[plain, 0, :, b, y, c], g1a_s.at[0, d - 1], dev)
        drained(wg.at[plain, 1, :, b, :, c], g2b_s.at[0, d - 1], dev)
        drained(wg.at[turned, 0, a, b, y, c], g1a_s.at[1, d - 1], dev)
        drained(wg.at[turned, 1, a, b, :, c], g2b_s.at[1, d - 1], dev)
    for d, dev in to_y:
        drained(wg.at[plain, 1, :, b, y, c], g1b_s.at[0, d - 1], dev)
        drained(wg.at[plain, 0, :, :, y, c], g2a_s.at[0, d - 1], dev)
        drained(wg.at[turned, 1, a, b, y, c], g1b_s.at[1, d - 1], dev)
        drained(wg.at[turned, 0, a, :, y, c], g2a_s.at[1, d - 1], dev)
    drained(wg.at[:, :, :, :, :, c], gc_s.at[0], to_c)
    drained(bb.at[: A - 1, b, y, c], bz_s.at[0], to_c)
    for d, dev in to_b:
        bias_1(d, dev, True).wait_send()
    for d, dev in to_y:
        bias_2(d, dev, True).wait_send()
    bias_c(True).wait_send()
    for copy in [bred_c()] + bred_1() + bred_2():
        copy.wait_send()
    drained(brz, dz_s.at[0], to_c)


def per_device(dims, features, cotangent, neighbours, segments, live, weight, bias):
    A, B, Y, C = dims
    batches, local, D = features.shape
    rows = weight.shape[0]
    N = batches * local
    N_l = LATE * local
    N_e = N - N_l
    chunks = D // CHUNK
    groups = A * B * Y
    wide = D // A
    neighbours = jnp.swapaxes(neighbours, 1, 2)
    any_spec = pl.BlockSpec(memory_space=pl.ANY)
    vmem, dma = pltpu.VMEM, pltpu.SemaphoreType.DMA
    scratch = [
        vmem((N_e, D), BF16),
        vmem((N_l, D), BF16),
        vmem((N_e // SLOT, SLOT, SLOT), BF16),
        vmem((N_e, SLOT), F32),
        vmem((groups, C, rows, N), BF16),
        vmem((2, batches, local, CHUNK), BF16),
        vmem((SLOTS, A, B, Y, rows, CHUNK), F32),
        vmem((2, A, B, Y, rows, CHUNK), BF16),
        vmem((RECEIVED, A, B, Y, rows, CHUNK), BF16),
        vmem((2, Y - 1, A, B, rows, LANES), BF16),
        vmem((2, B - 1, A, Y, rows, LANES), BF16),
        vmem((2, B - 1, A, rows, LANES), BF16),
        vmem((2, Y - 1, A, rows, LANES), BF16),
        vmem((2, A - 1, rows, CHUNK), BF16),
        vmem((chunks, Y - 1, A, B, rows, LANES), BF16),
        vmem((chunks, B - 1, A, Y, rows, LANES), BF16),
        vmem((chunks, B - 1, A, rows, LANES), BF16),
        vmem((chunks, Y - 1, A, rows, LANES), BF16),
        vmem((chunks, A - 1, rows, CHUNK), BF16),
        vmem(neighbours.shape, jnp.int32),
        vmem(segments.shape, jnp.int32),
        vmem(live.shape, jnp.int32),
        vmem((A, B, Y, C, 8, LANES), F32),
        vmem((D // LANES, 8, LANES), F32),
        vmem((8, D), F32),
        vmem((A, B, Y, C, 8, LANES), F32),
        vmem((A, B, Y, 8, LANES), F32),
        vmem((A, B, Y, 8, LANES), F32),
        vmem((Y - 1, A, B, 8, LANES), F32),
        vmem((B - 1, A, 8, LANES), F32),
        vmem((A - 1, 8, LANES), F32),
        dma((4 + batches,)),
        dma((2,)),
    ]
    scratch_tail = [dma((Y - 1,)), dma((B - 1,))]
    for sent, received in (
        ((2,), (chunks,)),
        ((2, B - 1), (chunks, B - 1)),
        ((2, Y - 1), (chunks, Y - 1)),
        ((2, Y - 1), (chunks, Y - 1)),
        ((2, B - 1), (chunks, B - 1)),
        ((1,), (chunks,)),
        ((2,), (chunks,)),
        ((2, Y - 1), (chunks, Y - 1)),
        ((2, B - 1), (chunks, B - 1)),
        ((2, B - 1), (chunks, B - 1)),
        ((2, Y - 1), (chunks, Y - 1)),
        ((2,), (chunks,)),
        (None, scratch_tail),
        ((1,), (1,)),
        ((B - 1,), (B - 1,)),
        ((Y - 1,), (Y - 1,)),
        ((1,), (1,)),
        ((1,), (1,)),
        ((Y - 1,), (Y - 1,)),
        ((B - 1,), (B - 1,)),
        ((1,), (1,)),
    ):
        scratch += received if sent is None else [dma(sent), dma(received)]
    vmem_spec = pl.BlockSpec(memory_space=pltpu.VMEM)
    kept = [
        vmem((chunks, batches, local, CHUNK), BF16),
        vmem((chunks, 2, A, B, Y, C, rows, LANES), BF16),
        vmem((N_l, D), BF16),
        vmem((N_e, D), BF16),
        vmem((N_l // SLOT, SLOT, SLOT), BF16),
        vmem((N_l, SLOT), F32),
        vmem((rows, D), F32),
        vmem((1, rows), F32),
    ]
    kept_arrays = pl.pallas_call(
        functools.partial(kernel, dims),
        out_shape=kept,
        in_specs=[any_spec] * 6 + [vmem_spec],
        out_specs=[vmem_spec] * len(kept),
        scratch_shapes=scratch,
        compiler_params=pltpu.CompilerParams(
            collective_id=0, has_side_effects=True, vmem_limit_bytes=39 * 2**20
        ),
        cost_estimate=pl.CostEstimate(
            flops=6 * N * D * D, bytes_accessed=8 * N * D, transcendentals=N * D
        ),
    )(features, cotangent, neighbours, segments, live, weight, bias.reshape(1, rows))
    act, fgrad, wgrad, bgrad = pl.pallas_call(
        functools.partial(finish, dims),
        out_shape=[
            jax.ShapeDtypeStruct(features.shape, BF16),
            jax.ShapeDtypeStruct(features.shape, BF16),
            jax.ShapeDtypeStruct(weight.shape, F32),
            jax.ShapeDtypeStruct((1, rows), F32),
        ],
        in_specs=[vmem_spec] * len(kept),
        out_specs=[any_spec] * 3 + [vmem_spec],
        scratch_shapes=[
            vmem((A * LATE, local, wide), BF16),
            dma((1,)), dma((batches - LATE,)), dma((A * LATE,)), dma((1,)),
        ],
        compiler_params=pltpu.CompilerParams(vmem_limit_bytes=8 * 2**20),
    )(
        *[pltpu.with_memory_space_constraint(x, pltpu.VMEM) for x in kept_arrays],
    )
    return act, fgrad, wgrad, bgrad.reshape(rows)


def solution(mesh):
    both = ("dp", "rep")
    dims = split_axes(mesh.shape["dp"], mesh.shape["rep"])
    return jax.shard_map(
        functools.partial(per_device, dims),
        mesh=mesh,
        in_specs=(
            P(None, both, None), P(None, both, None), P(None, both, None),
            P(None, both), P(None, both), P(both, None), P(both),
        ),
        out_specs=(P(None, both, None), P(None, both, None), P(both, None), P(both)),
        check_vma=False,
    )
```
